128 devices in a mesh: mp: 2 (over z_hi), patch: 16 (over x, y), latent: 4 (over z_lo, core).
Axes of the slice: x: 4, y: 4, z: 4 (z_hi: 2, z_lo: 2; z = z_hi * 2 + z_lo), core: 2. Of those that a mesh axis runs over, the one named last changes fastest.
Arguments:
- dino_acts: bfloat16 [256, 256, 1536], P(('mp', 'patch', 'latent')), may hold values from -600 to 600
- siglip_acts: bfloat16 [256, 729, 1152], P(('mp', 'patch', 'latent')), may hold values from -600 to 600
- dino_encoder: bfloat16 [1536, 4096], P(None, 'latent'), may hold values from -0.15625 to 0.15625
- siglip_encoder: bfloat16 [1152, 4096], P(None, 'latent'), may hold values from -0.1875 to 0.1875
- dino_threshold: bfloat16 [4096], P('latent'), may hold values from 0.049804688 to 0.5
- siglip_threshold: bfloat16 [4096], P('latent'), may hold values from 0.049804688 to 0.5
Outputs:
- correlation: float32 [4096, 4096], P(('mp', 'patch'), 'latent')
The draws below stay inside these ranges and needn't reach their ends.
All inputs are finite; a program needn't handle non-finite values.
Results may differ from the reference program's by a relative error of at most 0.0003.
Values may be sent and summed in bfloat16 or wider, within the bound.
No kernel may reach another device: no remote copies, remote signals or barrier semaphores. Data moves between devices by JAX's collectives and lax.ppermute only.
A program may use at most 128 MiB of HBM per device.

```python
import math
import jax
import jax.numpy as jnp
import numpy as np
from jax import lax

D_DINO = 1536
D_SIG = 1152
GRID = 16
SIG_SIDE = 27
LATENTS = 4096
PATCHES = 256
SIG_PATCHES = 729
IMAGES = 256


def shared_image(key, trend, spread):
    content_key, scale_key = jax.random.split(key)
    content = jnp.clip(jax.random.normal(content_key, (IMAGES, PATCHES, 16), jnp.float32), -4.0, 4.0)
    position = jnp.arange(IMAGES, dtype=jnp.float32)[:, None] / max(IMAGES - 1, 1)
    unit_draw = jax.random.uniform(scale_key, (IMAGES, PATCHES), jnp.float32)
    row_scale = jnp.exp(trend * position + math.log(spread) * unit_draw)
    return (content, row_scale)


def column_factors(column_key, width, low_end, high_end):
    return jnp.exp(jax.random.uniform(column_key, (width,), jnp.float32, math.log(low_end), math.log(high_end)))


def draw_dino_acts(key, part):
    trend, spread, mixing, low_end, high_end = (0.55, 6.0, 0.8, 0.32, 3.2)
    content, row_scale = shared_image(key, trend, spread)
    key = jax.random.fold_in(key, 11)
    noise_key, column_key = jax.random.split(key)
    shape_full = (IMAGES, PATCHES, D_DINO)
    noise_part = jnp.clip(jax.random.normal(noise_key, shape_full, jnp.float32), -4.0, 4.0)
    channel_index = jnp.arange(D_DINO, dtype=jnp.int32) % 16
    shared_part = jnp.take(content, channel_index, axis=2)
    columns = column_factors(column_key, D_DINO, low_end, high_end)
    values = row_scale[:, :, None] * columns * (mixing * shared_part + math.sqrt(1.0 - mixing * mixing) * noise_part)
    return values.astype(jnp.bfloat16)


def draw_siglip_acts(key, part):
    trend, spread, mixing, low_end, high_end = (0.55, 6.0, 0.8, 0.32, 3.2)
    content, row_scale = shared_image(key, trend, spread)
    key = jax.random.fold_in(key, 23)
    noise_key, column_key = jax.random.split(key)
    shape_full = (IMAGES, SIG_PATCHES, D_SIG)
    noise_part = jnp.clip(jax.random.normal(noise_key, shape_full, jnp.float32), -4.0, 4.0)
    cell_index = jnp.arange(SIG_SIDE, dtype=jnp.int32)
    nearest = (2 * cell_index + 1) * GRID // (2 * SIG_SIDE)
    patch_map = (nearest[:, None] * GRID + nearest[None, :]).reshape(-1)
    channel_index = jnp.arange(D_SIG, dtype=jnp.int32) * 5 % 16
    shared_part = jnp.take(jnp.take(content, patch_map, axis=1), channel_index, axis=2)
    patch_scale = jnp.take(row_scale, patch_map, axis=1)
    columns = column_factors(column_key, D_SIG, low_end, high_end)
    values = patch_scale[:, :, None] * columns * (mixing * shared_part + math.sqrt(1.0 - mixing * mixing) * noise_part)
    return values.astype(jnp.bfloat16)


def block_levels(key, extent, cuts, smallest, top_value):
    gain = 1.0
    for axis_at, shards_of in cuts:
        steps = jax.random.uniform(jax.random.fold_in(jax.random.fold_in(key, 6), axis_at), (shards_of,), jnp.float32, smallest / len(cuts), top_value / len(cuts))
        gain = gain * jnp.repeat(jnp.exp(steps), extent[axis_at] // shards_of).reshape((-1,) + (1,) * (len(extent) - 1 - axis_at))
    return gain


def scatter_about(own_key, dims, deviation, reach, shards=(), kind=jnp.bfloat16):
    values = jax.random.normal(own_key, dims, jnp.float32) * deviation
    if len(shards) > 0:
        values = block_levels(own_key, dims, shards, -0.22, 0.18) * values
    return jnp.clip(values, min=-reach, max=reach).astype(kind)


def setup_inputs(seed: int = 0) -> dict:
    key_of = jax.random.split(jax.random.key(seed), 7)
    return {
        "dino_acts": draw_dino_acts(jax.random.fold_in(key_of[6], 71), 0),
        "siglip_acts": draw_siglip_acts(jax.random.fold_in(key_of[6], 71), 0),
        "dino_encoder": scatter_about(key_of[2], (D_DINO, LATENTS), D_DINO ** -0.5, 0.15625, ((1, 4),)),
        "siglip_encoder": scatter_about(key_of[3], (D_SIG, LATENTS), D_SIG ** -0.5, 0.1875, ((1, 4),)),
        "dino_threshold": jnp.clip(jnp.exp(math.log(0.5) - 2.306499 * jax.random.uniform(key_of[4], (LATENTS,), jnp.float32) ** block_levels(key_of[4], (LATENTS,), ((0, 4),), -0.2, 0.2)), 0.049804688, 0.5).astype(jnp.bfloat16),
        "siglip_threshold": jnp.clip(jnp.exp(math.log(0.5) - 2.306499 * jax.random.uniform(key_of[5], (LATENTS,), jnp.float32) ** block_levels(key_of[5], (LATENTS,), ((0, 4),), -0.2, 0.2)), 0.049804688, 0.5).astype(jnp.bfloat16),
    }


EPS = 1e-06

def resample_table(side_cells, grid_cells):
    weights_table = np.zeros((grid_cells, side_cells), np.float32)
    for target in range(grid_cells):
        source = (target + 0.5) * side_cells / grid_cells - 0.5
        low_index = int(np.floor(source))
        upper_part = source - low_index
        weights_table[target, low_index] += 1.0 - upper_part
        weights_table[target, min(low_index + 1, side_cells - 1)] += upper_part
    return weights_table

def resample(raw_block, weights_table):
    image_count = raw_block.shape[0]
    side_cells = weights_table.shape[1]
    grid_cells = weights_table.shape[0]
    raw_grid = raw_block.astype(jnp.float32).reshape(image_count, side_cells, side_cells, raw_block.shape[-1])
    resample_matrix = jnp.asarray(weights_table, jnp.float32)
    columns_done = jnp.einsum('bj,nijk->nibk', resample_matrix, raw_grid, precision=lax.Precision.HIGHEST)
    both_done = jnp.einsum('ai,nibk->nabk', resample_matrix, columns_done, precision=lax.Precision.HIGHEST)
    return both_done.reshape(image_count, grid_cells * grid_cells, raw_block.shape[-1])

def encode(rows_in, encoder, threshold):
    pre_codes = jnp.dot(rows_in, encoder, preferred_element_type=jnp.float32)
    return jnp.maximum(pre_codes - threshold.astype(jnp.float32), 0.0).astype(jnp.bfloat16)

def reference(dino_acts, siglip_acts, dino_encoder, siglip_encoder, dino_threshold, siglip_threshold):
    weights_table = resample_table(SIG_SIDE, GRID)
    block_images = 8

    def one_block(carry, block_index):
        products, dino_power, siglip_power = carry
        first_image = (block_index * block_images).astype(jnp.int32)
        dino_rows = lax.dynamic_slice_in_dim(dino_acts, first_image, block_images, 0).reshape(-1, D_DINO)
        dino_codes = encode(dino_rows, dino_encoder, dino_threshold)
        raw_block = lax.dynamic_slice_in_dim(siglip_acts, first_image, block_images, 0)
        resampled = resample(raw_block, weights_table).astype(jnp.bfloat16).reshape(-1, D_SIG)
        siglip_codes = encode(resampled, siglip_encoder, siglip_threshold)
        products = products + jnp.dot(siglip_codes.T, dino_codes, preferred_element_type=jnp.float32)
        dino_power = dino_power + lax.optimization_barrier(jnp.sum(jnp.square(dino_codes.astype(jnp.float32)), axis=0))
        siglip_power = siglip_power + lax.optimization_barrier(jnp.sum(jnp.square(siglip_codes.astype(jnp.float32)), axis=0))
        return ((products, dino_power, siglip_power), None)
    start_state = (jnp.zeros((LATENTS, LATENTS), jnp.float32), jnp.zeros((LATENTS,), jnp.float32), jnp.zeros((LATENTS,), jnp.float32))
    block_ids = jnp.arange(IMAGES // block_images, dtype=jnp.int32)
    (products, dino_power, siglip_power), _ = lax.scan(one_block, start_state, block_ids)
    row_total = IMAGES * PATCHES
    siglip_mean = siglip_power / row_total + EPS
    dino_mean = dino_power / row_total + EPS
    return products / row_total / jnp.sqrt(siglip_mean[:, None] * dino_mean[None, :])
```

```python
import functools

import jax
import jax.numpy as jnp
import numpy as np
from jax import lax
from jax.experimental import pallas as pl
from jax.experimental.pallas import tpu as pltpu
from jax.sharding import PartitionSpec as P

GRID = 16
SIG_SIDE = 27
EPS = 1e-06
AXES = ("mp", "patch", "latent")
VMEM = 56 * 1024 * 1024
CODE_TOP = 2.0**15


def resample_table(side_cells, grid_cells):
    weights_table = np.zeros((grid_cells, side_cells), np.float32)
    for target in range(grid_cells):
        source = (target + 0.5) * side_cells / grid_cells - 0.5
        low_index = int(np.floor(source))
        upper_part = source - low_index
        weights_table[target, low_index] += 1.0 - upper_part
        weights_table[target, min(low_index + 1, side_cells - 1)] += upper_part
    return weights_table


def resample_local(raw_block):
    weights_table = resample_table(SIG_SIDE, GRID)
    image_count = raw_block.shape[0]
    raw_grid = raw_block.reshape(image_count, SIG_SIDE, SIG_SIDE, raw_block.shape[-1])
    narrow_matrix = jnp.asarray(weights_table, jnp.bfloat16)
    wide_matrix = jnp.asarray(weights_table, jnp.float32)
    columns_done = jnp.einsum(
        "bj,nijk->nibk", narrow_matrix, raw_grid, preferred_element_type=jnp.float32
    )
    both_done = jnp.einsum(
        "ai,nibk->nabk", wide_matrix, columns_done, precision=lax.Precision.HIGHEST
    )
    return both_done.reshape(image_count, GRID * GRID, raw_block.shape[-1]).astype(jnp.bfloat16)


def place(x, y, z, core):
    return (z // 2) * 64 + (x * 4 + y) * 4 + (z % 2) * 2 + core


def moves(dx=0, dy=0, dz=0, swap=0):
    return [
        (place(x, y, z, c), place((x + dx) % 4, (y + dy) % 4, (z + dz) % 4, c ^ swap))
        for x in range(4) for y in range(4) for z in range(4) for c in range(2)
    ]


def send(value, **step):
    return lax.ppermute(value, AXES, moves(**step))


def params():
    return pltpu.CompilerParams(vmem_limit_bytes=VMEM)


def encode_rows_kernel(x_ref, w_ref, t_ref, code_ref, power_ref):
    pre = jnp.dot(x_ref[...], w_ref[...], preferred_element_type=jnp.float32)
    code = jnp.maximum(pre - t_ref[...].astype(jnp.float32), 0.0).astype(jnp.bfloat16)
    code_ref[...] = code
    wide = code.astype(jnp.float32)
    part = jnp.sum((wide * wide).reshape(-1, 8, wide.shape[1]), axis=0)

    @pl.when(pl.program_id(0) == 0)
    def _():
        power_ref[...] = part

    @pl.when(pl.program_id(0) > 0)
    def _():
        power_ref[...] += part


def encode_rows(acts, weights, threshold, block=256):
    rows, depth = acts.shape
    latents = weights.shape[1]
    return pl.pallas_call(
        encode_rows_kernel,
        grid=(rows // block,),
        in_specs=[
            pl.BlockSpec((block, depth), lambda i: (i, 0)),
            pl.BlockSpec((depth, latents), lambda i: (0, 0)),
            pl.BlockSpec((1, latents), lambda i: (0, 0)),
        ],
        out_specs=[
            pl.BlockSpec((block, latents), lambda i: (i, 0)),
            pl.BlockSpec((8, latents), lambda i: (0, 0)),
        ],
        out_shape=[
            jax.ShapeDtypeStruct((rows, latents), jnp.bfloat16),
            jax.ShapeDtypeStruct((8, latents), jnp.float32),
        ],
        compiler_params=params(),
        cost_estimate=pl.CostEstimate(
            flops=2 * rows * depth * latents, bytes_accessed=2 * (rows * depth + depth * latents + rows * latents),
            transcendentals=0),
        name="dino_codes",
    )(acts, weights, threshold.reshape(1, latents))


def encode_columns_kernel(depth, w_ref, x_ref, code_ref, power_ref):
    pre = lax.dot_general(
        w_ref[:, :depth], x_ref[...], (((1,), (1,)), ((), ())), preferred_element_type=jnp.float32
    )
    threshold = w_ref[:, depth:depth + 128].astype(jnp.float32)[:, :1]
    code = jnp.maximum(pre - threshold, 0.0).astype(jnp.bfloat16)
    code_ref[...] = code
    wide = code.astype(jnp.float32)
    square = wide * wide
    part = square[:, :128]
    for at in range(128, square.shape[1], 128):
        part += square[:, at:at + 128]

    @pl.when(pl.program_id(0) == 0)
    def _():
        power_ref[...] = part

    @pl.when(pl.program_id(0) > 0)
    def _():
        power_ref[...] += part


def encode_columns(weights, acts, block=256):
    rows, depth = acts.shape
    latents, wide_depth = weights.shape
    return pl.pallas_call(
        functools.partial(encode_columns_kernel, depth),
        grid=(rows // block,),
        in_specs=[
            pl.BlockSpec((latents, wide_depth), lambda i: (0, 0)),
            pl.BlockSpec((block, depth), lambda i: (i, 0)),
        ],
        out_specs=[
            pl.BlockSpec((latents, block), lambda i: (0, i)),
            pl.BlockSpec((latents, 128), lambda i: (0, 0)),
        ],
        out_shape=[
            jax.ShapeDtypeStruct((latents, rows), jnp.bfloat16),
            jax.ShapeDtypeStruct((latents, 128), jnp.float32),
        ],
        compiler_params=params(),
        cost_estimate=pl.CostEstimate(
            flops=2 * rows * depth * latents, bytes_accessed=2 * (rows * depth + depth * latents + rows * latents),
            transcendentals=0),
        name="siglip_codes",
    )(weights, acts)


def dot_own(left, d_ref, cols):
    return jnp.dot(left, d_ref[:, cols], preferred_element_type=jnp.float32)


def dot_sibling(left, d_ref, cols):
    half = left.shape[1] // 2
    return jnp.dot(left[:, :half], d_ref[half:, cols], preferred_element_type=jnp.float32) + jnp.dot(
        left[:, half:], d_ref[:half, cols], preferred_element_type=jnp.float32)


def is_own(at_ref, m):
    return lax.rem(at_ref[0] + m, 4) // 2 == at_ref[2]


def products_local_kernel(at_ref, ox_ref, sx_ref, oy_ref, sy_ref, d_ref, out_ref):
    m = pl.program_id(0)
    width = d_ref.shape[1]
    tile = 256

    @pl.when((m < 4) & is_own(at_ref, m))
    def _():
        for at in range(0, width, tile):
            out_ref[0, :, at:at + tile] = dot_own(ox_ref[0], d_ref, slice(at, at + tile))

    @pl.when((m < 4) & jnp.logical_not(is_own(at_ref, m)))
    def _():
        for at in range(0, width, tile):
            out_ref[0, :, at:at + tile] = dot_sibling(sx_ref[0], d_ref, slice(at, at + tile))

    @pl.when(m >= 4)
    def _():
        own = oy_ref[...].reshape(256, -1)
        sib = sy_ref[...].reshape(256, -1)
        for at in range(0, width, tile):
            out_ref[0, :256, at:at + tile] = dot_own(own, d_ref, slice(at, at + tile))
            out_ref[0, 256:, at:at + tile] = dot_sibling(sib, d_ref, slice(at, at + tile))


def products_local(at, own_x, sib_x, own_y, sib_y, dino):
    depth, width = dino.shape
    x_spec = pl.BlockSpec((1, 512, depth), lambda m, at: (lax.rem(at[0] + jnp.minimum(m, 3), 4) % 2, 0, 0))
    y_spec = pl.BlockSpec((2, 1, 128, depth), lambda m, at: (0, lax.rem(at[1] + jnp.maximum(m - 4, 0), 4), 0, 0))
    return pl.pallas_call(
        products_local_kernel,
        grid_spec=pltpu.PrefetchScalarGridSpec(
            num_scalar_prefetch=1,
            grid=(8,),
            in_specs=[x_spec, x_spec, y_spec, y_spec, pl.BlockSpec((depth, width), lambda m, at: (0, 0))],
            out_specs=pl.BlockSpec((1, 512, width), lambda m, at: (m, 0, 0)),
        ),
        out_shape=jax.ShapeDtypeStruct((8, 512, width), jnp.float32),
        compiler_params=params(),
        cost_estimate=pl.CostEstimate(flops=2 * 4096 * depth * width, bytes_accessed=30 << 20, transcendentals=0),
        name="products_near",
    )(at, own_x.reshape(2, 512, depth), sib_x.reshape(2, 512, depth),
      own_y.reshape(2, 4, 128, depth), sib_y.reshape(2, 4, 128, depth), dino)


def squeeze(value):
    value = value * value
    value = value * value
    return (value * value).astype(jnp.bfloat16)


def widen(value):
    return jnp.exp2(jnp.log2(value.astype(jnp.float32)) * 0.125)


def products_far_kernel(m, at_ref, ox_ref, sx_ref, oy_ref, sy_ref, d_ref, px_ref, py_ref,
                        gox_ref, gsx_ref, goy_ref, gsy_ref, gd_ref, x_ref, y_ref):
    finish = squeeze if m else (lambda value: value)
    gain_d = gd_ref[...]
    every = slice(None)

    @pl.when(is_own(at_ref, m))
    def _():
        total = px_ref[0] + dot_own(ox_ref[0], d_ref, every)
        x_ref[...] = finish(total * gox_ref[0] * gain_d)

    @pl.when(jnp.logical_not(is_own(at_ref, m)))
    def _():
        total = px_ref[0] + dot_sibling(sx_ref[0], d_ref, every)
        x_ref[...] = finish(total * gsx_ref[0] * gain_d)

    own = py_ref[0, :256, :] + dot_own(oy_ref[...].reshape(256, -1), d_ref, every)
    y_ref[:256, :] = finish(own * goy_ref[...].reshape(256, 1) * gain_d)
    sib = py_ref[0, 256:, :] + dot_sibling(sy_ref[...].reshape(256, -1), d_ref, every)
    y_ref[256:, :] = finish(sib * gsy_ref[...].reshape(256, 1) * gain_d)


def products_far(m, at, own_x, sib_x, own_y, sib_y, dino, near, gains, tile=256):
    depth, width = dino.shape
    x_at = lambda at: lax.rem(at[0] + m, 4) % 2
    y_at = lambda at: lax.rem(at[1] + m, 4)
    x_spec = pl.BlockSpec((1, 512, depth), lambda n, at: (x_at(at), 0, 0))
    y_spec = pl.BlockSpec((2, 1, 128, depth), lambda n, at: (0, y_at(at), 0, 0))
    gx_spec = pl.BlockSpec((1, 512, 1), lambda n, at: (x_at(at), 0, 0))
    gy_spec = pl.BlockSpec((2, 1, 128, 1), lambda n, at: (0, y_at(at), 0, 0))
    gain_own_x, gain_sib_x, gain_own_y, gain_sib_y, gain_d = gains
    kind = jnp.bfloat16 if m else jnp.float32
    return pl.pallas_call(
        functools.partial(products_far_kernel, m),
        grid_spec=pltpu.PrefetchScalarGridSpec(
            num_scalar_prefetch=1,
            grid=(width // tile,),
            in_specs=[
                x_spec, x_spec, y_spec, y_spec,
                pl.BlockSpec((depth, tile), lambda n, at: (0, n)),
                pl.BlockSpec((1, 512, tile), lambda n, at: (m, 0, n)),
                pl.BlockSpec((1, 512, tile), lambda n, at: (4 + m, 0, n)),
                gx_spec, gx_spec, gy_spec, gy_spec,
                pl.BlockSpec((1, tile), lambda n, at: (0, n)),
            ],
            out_specs=[pl.BlockSpec((512, tile), lambda n, at: (0, n))] * 2,
        ),
        out_shape=[jax.ShapeDtypeStruct((512, width), kind)] * 2,
        compiler_params=params(),
        cost_estimate=pl.CostEstimate(flops=2 * 1024 * depth * width, bytes_accessed=12 << 20, transcendentals=0),
        name="products_far",
    )(at, own_x.reshape(2, 512, depth), sib_x.reshape(2, 512, depth),
      own_y.reshape(2, 4, 128, depth), sib_y.reshape(2, 4, 128, depth), dino, near, near,
      gain_own_x.reshape(2, 512, 1), gain_sib_x.reshape(2, 512, 1),
      gain_own_y.reshape(2, 4, 128, 1), gain_sib_y.reshape(2, 4, 128, 1), gain_d.reshape(1, width))


def shards(dino_acts, siglip_acts, dino_encoder, siglip_encoder, dino_threshold, siglip_threshold):
    z_hi = lax.axis_index("mp")
    patch = lax.axis_index("patch")
    latent = lax.axis_index("latent")
    x, y = patch // 4, patch % 4
    z_lo, core = latent // 2, latent % 2
    at = jnp.stack([x, y, core]).astype(jnp.int32)
    row_total = dino_acts.shape[0] * dino_acts.shape[1] * lax.axis_size(AXES)

    d_own = dino_acts.reshape(-1, dino_acts.shape[-1])
    half = d_own.shape[0] // 2
    d_low = send(d_own[:half], dz=1)
    d_high = send(d_own[half:], dz=-1)
    d_sib = send(d_own, swap=1)

    w_own = jnp.concatenate(
        [siglip_encoder.T, jnp.broadcast_to(siglip_threshold[:, None], (siglip_threshold.shape[0], 128))], axis=1)
    share = w_own.shape[0] // 16
    w_piece = send(lax.dynamic_slice_in_dim(w_own, patch * share, share, 0), dz=1)
    w_other = lax.all_gather(w_piece, "patch", axis=0, tiled=True)

    s_own = resample_local(siglip_acts).reshape(-1, siglip_acts.shape[-1])
    s_low = send(s_own[:half], dz=1)
    s_high = send(s_own[half:], dz=-1)
    s_sib = send(s_own, swap=1)

    d_near = jnp.concatenate([d_own, d_sib])
    s_near = jnp.concatenate([s_own, s_sib])
    dino_near, dp_near = encode_rows(d_near, dino_encoder, dino_threshold)
    x_near, xp_near = encode_columns(w_own, s_near)
    y_near, yp_near = encode_columns(w_other, s_near)
    near = products_local(at, x_near, send(x_near, swap=1), y_near, send(y_near, swap=1), dino_near)

    d_ext = jnp.concatenate([d_low, d_high])
    s_ext = jnp.concatenate([s_low, s_high])
    d_far = jnp.concatenate([d_ext, send(d_ext, swap=1)])
    s_far = jnp.concatenate([s_ext, send(s_ext, swap=1)])
    x_far, xp_far = encode_columns(w_own, s_far)
    y_far, yp_far = encode_columns(w_other, s_far)
    x_far_sib = send(x_far, swap=1)
    y_far_sib = send(y_far, swap=1)
    dino_far, dp_far = encode_rows(d_far, dino_encoder, dino_threshold)

    powers = jnp.concatenate([
        jnp.sum(xp_near + xp_far, axis=1), jnp.sum(yp_near + yp_far, axis=1), jnp.sum(dp_near + dp_far, axis=0)])
    powers = jnp.sum(lax.all_gather(powers.reshape(1, -1), ("mp", "patch"), axis=0, tiled=True), axis=0)
    sig_power = powers[:2048]
    sig_power_sib = send(sig_power.reshape(16, 128), swap=1).reshape(-1)
    dino_power = powers[2048:]

    def gain(power):
        return jnp.where(power > 0, lax.rsqrt(power) * np.float32(np.sqrt(CODE_TOP)), 0.0)

    gains = (gain(sig_power[:1024]), gain(sig_power_sib[:1024]), gain(sig_power[1024:]),
             gain(sig_power_sib[1024:]), gain(dino_power))

    def block(m):
        return products_far(m, at, x_far, x_far_sib, y_far, y_far_sib, dino_far, near, gains)

    arrived_x, arrived_y = [], []
    for m in (1, 3, 2):
        part_x, part_y = block(m)
        arrived_x.append(send(part_x, dx=m))
        arrived_y.append(send(part_y, dy=m))
    total_x, total_y = block(0)
    for value in arrived_x:
        total_x += widen(value)
    for value in arrived_y:
        total_y += widen(value)

    def x_place(column):
        return jnp.where(column // 2 == core, 0, 2) + column % 2

    def pick(total, place_of):
        return lax.dynamic_slice_in_dim(total, place_of * 128, 128, 0)

    second_x, second_y = [], []
    for m in (1, 3, 2):
        second_x.append(send(squeeze(pick(total_x, (y + m) % 4)), dy=m))
        second_y.append(send(squeeze(pick(total_y, x_place((x + m) % 4))), dx=m))
    total_x = pick(total_x, y)
    total_y = pick(total_y, x_place(x))
    for value in second_x:
        total_x += widen(value)
    for value in second_y:
        total_y += widen(value)

    straight = z_hi == z_lo
    mine = jnp.where(straight, total_x, total_y)
    other = jnp.where(straight, total_y, total_x)
    total = mine + widen(send(squeeze(other), dz=2))

    own_set = jnp.where(straight, sig_power[:1024], sig_power[1024:])
    sib_set = jnp.where(straight, sig_power_sib[:1024], sig_power_sib[1024:])
    rows_power = lax.dynamic_slice_in_dim(
        jnp.where(x // 2 == core, own_set, sib_set), (x % 2) * 512 + y * 128, 128, 0)

    def back(power):
        return jnp.sqrt(power / (power + np.float32(EPS * row_total))) * np.float32(1 / np.sqrt(CODE_TOP))

    return total * back(rows_power)[:, None] * back(dino_power)[None, :]


def solution(mesh):
    in_specs = (
        P(("mp", "patch", "latent"), None, None),
        P(("mp", "patch", "latent"), None, None),
        P(None, "latent"),
        P(None, "latent"),
        P("latent"),
        P("latent"),
    )
    out_specs = P(("mp", "patch"), "latent")
    return jax.shard_map(shards, mesh=mesh, in_specs=in_specs, out_specs=out_specs, check_vma=False)
```

```python
import functools

import jax
import jax.numpy as jnp
import numpy as np
from jax import lax
from jax.experimental import pallas as pl
from jax.experimental.pallas import tpu as pltpu
from jax.sharding import PartitionSpec as P

GRID = 16
SIG_SIDE = 27
EPS = 1e-06
AXES = ("mp", "patch", "latent")
VMEM = 56 * 1024 * 1024
TOP = np.float32(np.sqrt(2.0**15))
ANY = pl.BlockSpec(memory_space=pl.ANY)
SMEM = pl.BlockSpec(memory_space=pltpu.SMEM)
FULL = pl.BlockSpec(memory_space=pltpu.VMEM)
PIECE = 288


def resample_table(side_cells, grid_cells):
    weights_table = np.zeros((grid_cells, side_cells), np.float32)
    for target in range(grid_cells):
        source = (target + 0.5) * side_cells / grid_cells - 0.5
        low_index = int(np.floor(source))
        upper_part = source - low_index
        weights_table[target, low_index] += 1.0 - upper_part
        weights_table[target, min(low_index + 1, side_cells - 1)] += upper_part
    return weights_table


def resample_local(raw_block):
    table = resample_table(SIG_SIDE, GRID)
    table = np.kron(table, table).astype(np.float32)
    high = table.astype(jnp.bfloat16)
    low = (table - high.astype(np.float32)).astype(jnp.bfloat16)
    images = raw_block.shape[0]

    def part(matrix):
        return lax.dot_general(
            jnp.broadcast_to(jnp.asarray(matrix), (images,) + matrix.shape), raw_block,
            (((2,), (1,)), ((0,), (0,))), preferred_element_type=jnp.float32)

    return (part(high) + part(low)).astype(jnp.bfloat16)


def place(x, y, z, core):
    return (z // 2) * 64 + (x * 4 + y) * 4 + (z % 2) * 2 + core


def moves(dx=0, dy=0, dz=0, swap=0):
    return [
        (place(x, y, z, c), place((x + dx) % 4, (y + dy) % 4, (z + dz) % 4, c ^ swap))
        for x in range(4) for y in range(4) for z in range(4) for c in range(2)
    ]


def send(value, **step):
    return lax.ppermute(value, AXES, moves(**step))


def params():
    return pltpu.CompilerParams(vmem_limit_bytes=VMEM)


def cost(flops, size):
    return pl.CostEstimate(flops=flops, bytes_accessed=size, transcendentals=0)


def assemble_kernel(at_ref, p0, p1, p2, p3, out_ref, sems):
    first = lax.rem(at_ref[0] + 2 * at_ref[1], 4)
    copies = []
    for step, piece in enumerate((p0, p1, p2, p3)):
        row = pl.multiple_of(lax.rem(first + step, 4) * PIECE, 16)
        copies.append(pltpu.make_async_copy(
            piece.at[pl.ds(0, PIECE), :], out_ref.at[pl.ds(row, PIECE), :], sems.at[step]))
    copies.append(pltpu.make_async_copy(
        p0.at[pl.ds(PIECE, 16), :], out_ref.at[pl.ds(4 * PIECE, 16), :], sems.at[4]))
    for copy in copies:
        copy.start()
    for copy in copies:
        copy.wait()


def assemble(at, pieces):
    return pl.pallas_call(
        assemble_kernel,
        in_specs=[SMEM] + [ANY] * 4,
        out_specs=ANY,
        out_shape=jax.ShapeDtypeStruct((4 * PIECE + 16, pieces[0].shape[1]), jnp.bfloat16),
        scratch_shapes=[pltpu.SemaphoreType.DMA((5,))],
        compiler_params=params(),
        cost_estimate=cost(0, 5 << 20),
        name="encoder_pieces",
    )(at, *pieces)


def encode_kernel(chunks, joined, theta_rows, at_ref, *refs):
    xs, refs = refs[:chunks], refs[chunks:]
    ws, ts, refs = refs[:2], refs[2:4], refs[4:]
    outs, refs = refs[:1 if joined else 2], refs[1 if joined else 2:]
    x_buf, w_buf, t_buf, o_buf, x_sem, w_sem, t_sem, o_sem = refs
    depth = x_buf.shape[1]
    width = w_buf.shape[2]
    copies = []
    row = 0
    for k in range(chunks):
        rows = xs[k].shape[0]
        copies.append(pltpu.make_async_copy(xs[k], x_buf.at[pl.ds(row, rows), :], x_sem.at[k]))
        row += rows
    w_copies = [pltpu.make_async_copy(ws[j].at[pl.ds(0, depth), :], w_buf.at[j], w_sem.at[j]) for j in range(2)]
    t_copies = [pltpu.make_async_copy(ts[j].at[pl.ds(theta_rows[j], 16), :], t_buf.at[j], t_sem.at[j])
                for j in range(2)]
    for copy in copies + [w_copies[0]] + t_copies + [w_copies[1]]:
        copy.start()
    for copy in copies + t_copies:
        copy.wait()
    out_copies = []
    for j in range(2):
        w_copies[j].wait()
        pre = jnp.dot(x_buf[...], w_buf[j], preferred_element_type=jnp.float32)
        theta = t_buf[j].astype(jnp.float32)[:1, :]
        o_buf[j] = jnp.maximum(pre - theta, 0.0).astype(jnp.bfloat16)
        if joined:
            block = at_ref[2] if j == 0 else 1 - at_ref[2]
            target = outs[0].at[:, pl.ds(pl.multiple_of(block * width, width), width)]
        else:
            target = outs[j]
        out_copies.append(pltpu.make_async_copy(o_buf.at[j], target, o_sem.at[j]))
        out_copies[j].start()
    for copy in out_copies:
        copy.wait()


def encode(at, xs, ws, ts, theta_rows, joined, name):
    rows = sum(x.shape[0] for x in xs)
    depth = xs[0].shape[1]
    width = ws[0].shape[1]
    if joined:
        shapes = [jax.ShapeDtypeStruct((rows, 2 * width), jnp.bfloat16)]
    else:
        shapes = [jax.ShapeDtypeStruct((rows, width), jnp.bfloat16)] * 2
    return pl.pallas_call(
        functools.partial(encode_kernel, len(xs), joined, theta_rows),
        in_specs=[SMEM] + [ANY] * (len(xs) + 4),
        out_specs=[ANY] * len(shapes),
        out_shape=shapes,
        scratch_shapes=[
            pltpu.VMEM((rows, depth), jnp.bfloat16),
            pltpu.VMEM((2, depth, width), jnp.bfloat16),
            pltpu.VMEM((2, 16, width), jnp.bfloat16),
            pltpu.VMEM((2, rows, width), jnp.bfloat16),
            pltpu.SemaphoreType.DMA((len(xs),)),
            pltpu.SemaphoreType.DMA((2,)),
            pltpu.SemaphoreType.DMA((2,)),
            pltpu.SemaphoreType.DMA((2,)),
        ],
        compiler_params=params(),
        cost_estimate=cost(4 * rows * depth * width, 2 * (rows * depth + 2 * depth * width + 2 * rows * width)),
        name=name,
    )(at, *xs, *ws, *ts)


def squeeze(value):
    value = value * value
    value = value * value
    return (value * value).astype(jnp.bfloat16)


def widen(value):
    return jnp.exp2(jnp.log2(value.astype(jnp.float32)) * 0.125)


def gain(power):
    return jnp.where(power > 0, lax.rsqrt(jnp.maximum(power, 1e-37)) * TOP, 0.0)


def root(power):
    return jnp.sqrt(power) * np.float32(1 / TOP)


def column(row):
    return jnp.broadcast_to(row, (128, row.shape[1])).T


def pack(row_power, column_power):
    width = column_power.shape[1]
    if row_power.shape[1] < width:
        row_power = jnp.concatenate(
            [row_power, jnp.zeros((1, width - row_power.shape[1]), jnp.float32)], axis=1)
    at = lax.broadcasted_iota(jnp.int32, (16, width), 0)
    out = jnp.zeros((16, width), jnp.float32)
    for base, power in ((0, column_power), (3, row_power)):
        rest = power
        for part in range(3):
            piece = rest.astype(jnp.bfloat16).astype(jnp.float32)
            out = jnp.where(at == base + part, piece, out)
            rest = rest - piece
    return out.astype(jnp.bfloat16)


def unpack(tail, rows):
    tail = tail.astype(jnp.float32)
    column_power = tail[0:1, :] + tail[1:2, :] + tail[2:3, :]
    row_power = tail[3:4, :rows] + tail[4:5, :rows] + tail[5:6, :rows]
    return row_power, column_power


def square_sum(ref, cols):
    total = None
    for at in range(0, ref.shape[0], 256):
        wide = ref[at:at + 256, cols].astype(jnp.float32)
        part = jnp.sum((wide * wide).reshape(32, 8, -1), axis=0)
        total = part if total is None else total + part
    return jnp.sum(total, axis=0, keepdims=True)


def products_kernel(m, at_ref, *refs):
    sx, sy, ds, refs = refs[:4], refs[4:8], refs[8:12], refs[12:]
    outs, refs = refs[:2 if m else 5], refs[2 if m else 5:]
    x_buf, y_buf, d_buf, x_sem, y_sem, d_sem = refs
    rows = sx[0].shape[0]
    width = d_buf.shape[1]
    x_col = pl.multiple_of(lax.rem(at_ref[0] + m, 4) * 512, 512)
    y_at = lax.rem(at_ref[1] + m, 4)
    d_copies, x_copies, y_copies = [], [], []
    for k in range(4):
        here = pl.ds(k * rows, rows)
        d_copies.append(pltpu.make_async_copy(ds[k], d_buf.at[here, :], d_sem.at[k]))
        x_copies.append(pltpu.make_async_copy(sx[k].at[:, pl.ds(x_col, 512)], x_buf.at[here, :], x_sem.at[k]))
        for a in range(4):
            col = pl.multiple_of((a * 4 + y_at) * 128, 128)
            y_copies.append(pltpu.make_async_copy(
                sy[k].at[:, pl.ds(col, 128)], y_buf.at[here, pl.ds(a * 128, 128)], y_sem.at[k * 4 + a]))
    for copy in d_copies + x_copies + y_copies:
        copy.start()
    for copy in d_copies:
        copy.wait()
    tile = 512
    d_power = jnp.concatenate(
        [square_sum(d_buf, slice(at, at + tile)) for at in range(0, width, tile)], axis=1)
    for which, (buf, copies) in enumerate(((x_buf, x_copies), (y_buf, y_copies))):
        for copy in copies:
            copy.wait()
        s_power = square_sum(buf, slice(None))
        out = outs[which]
        for at in range(0, width, tile):
            total = lax.dot_general(
                buf[...], d_buf[:, at:at + tile], (((0,), (0,)), ((), ())), preferred_element_type=jnp.float32)
            if m:
                row_gain = jnp.concatenate([column(gain(s_power))] * (tile // 128), axis=1)
                total = squeeze(total * row_gain * gain(d_power[:, at:at + tile]))
            out[0:512, at:at + tile] = total
        if m:
            out[512:528, :] = pack(s_power, d_power)
        else:
            outs[2 + which][...] = jnp.broadcast_to(s_power, (8, 512))
    if not m:
        outs[4][...] = jnp.broadcast_to(d_power, (8, width))


def products(m, at, sx, sy, ds):
    rows = sx[0].shape[0]
    width = ds[0].shape[1]
    if m:
        shapes = [jax.ShapeDtypeStruct((528, width), jnp.bfloat16)] * 2
    else:
        shapes = [jax.ShapeDtypeStruct(s, jnp.float32)
                  for s in ((512, width), (512, width), (8, 512), (8, 512), (8, width))]
    return pl.pallas_call(
        functools.partial(products_kernel, m),
        in_specs=[SMEM] + [ANY] * 12,
        out_specs=[FULL] * len(shapes),
        out_shape=shapes,
        scratch_shapes=[
            pltpu.VMEM((4 * rows, 512), jnp.bfloat16),
            pltpu.VMEM((4 * rows, 512), jnp.bfloat16),
            pltpu.VMEM((4 * rows, width), jnp.bfloat16),
            pltpu.SemaphoreType.DMA((4,)),
            pltpu.SemaphoreType.DMA((16,)),
            pltpu.SemaphoreType.DMA((4,)),
        ],
        compiler_params=params(),
        cost_estimate=cost(2 * 1024 * 4 * rows * width, 10 << 20),
        name="products",
    )(at, *sx, *sy, *ds)


def first_sum_kernel(axis, at_ref, own_ref, rp_ref, cp_ref, m1, m2, m3,
                     o1, o2, o3, keep_ref, keep_rp_ref, keep_cp_ref, scale_ref, power_ref):
    messages = (m1, m2, m3)
    width = own_ref.shape[1]
    row_total, column_total = rp_ref[0:1, :], cp_ref[0:1, :]
    column_roots = []
    for k, message in enumerate(messages):
        row_power, column_power = unpack(message[512:528, :], 512)
        scale_ref[k] = column(root(row_power))
        column_roots.append(root(column_power))
        row_total = row_total + row_power
        column_total = column_total + column_power
    scale_ref[3] = column(gain(row_total))
    power_ref[...] = jnp.broadcast_to(row_total, (8, 512))
    column_gain = gain(column_total)
    for m, out in ((1, o1), (3, o3), (2, o2), (0, keep_ref)):
        start = pl.multiple_of(lax.rem(at_ref[axis] + m, 4) * 128, 128)
        here = pl.ds(start, 128)
        scales = [scale_ref[k, here, :] for k in range(4)]
        for at in range(0, width, 128):
            cols = slice(at, at + 128)
            total = own_ref[here, cols]
            for k, message in enumerate(messages):
                total = total + widen(message[here, cols]) * (scales[k] * column_roots[k][:, cols])
            if m:
                total = squeeze(total * (scales[3] * column_gain[:, cols]))
            out[0:128, cols] = total
        here_power = power_ref[:, here][0:1, :]
        if m:
            out[128:144, :] = pack(here_power, column_total)
        else:
            keep_rp_ref[...] = jnp.broadcast_to(here_power, (8, 128))
    keep_cp_ref[...] = jnp.broadcast_to(column_total, (8, width))


def first_sum(axis, at, own, row_power, column_power, messages):
    width = own.shape[1]
    shapes = [jax.ShapeDtypeStruct((144, width), jnp.bfloat16)] * 3 + [
        jax.ShapeDtypeStruct(s, jnp.float32) for s in ((128, width), (8, 128), (8, width))]
    return pl.pallas_call(
        functools.partial(first_sum_kernel, axis),
        in_specs=[SMEM] + [FULL] * 6,
        out_specs=[FULL] * 6,
        out_shape=shapes,
        scratch_shapes=[pltpu.VMEM((4, 512, 128), jnp.float32), pltpu.VMEM((8, 512), jnp.float32)],
        compiler_params=params(),
        cost_estimate=cost(20 << 20, 6 << 20),
        name="first_sum",
    )(at, own, row_power, column_power, *messages)


def add_messages(own_ref, rp_ref, cp_ref, messages):
    row_total, column_total = rp_ref[0:1, :], cp_ref[0:1, :]
    scales = []
    for message in messages:
        row_power, column_power = unpack(message[128:144, :], 128)
        scales.append((column(root(row_power)), root(column_power)))
        row_total = row_total + row_power
        column_total = column_total + column_power
    tiles = []
    for at in range(0, own_ref.shape[1], 128):
        cols = slice(at, at + 128)
        total = own_ref[:, cols]
        for message, (rows, columns) in zip(messages, scales):
            total = total + widen(message[0:128, cols]) * (rows * columns[:, cols])
        tiles.append(total)
    return tiles, row_total, column_total


def second_sum_kernel(at_ref, *refs):
    x_refs, y_refs, outs = refs[:6], refs[6:12], refs[12:]
    z_ref, keep_ref, keep_rp_ref, keep_cp_ref = outs
    straight = at_ref[3] == 1
    x_tiles, x_rows, x_columns = add_messages(*x_refs[:3], x_refs[3:])
    y_tiles, y_rows, y_columns = add_messages(*y_refs[:3], y_refs[3:])
    other_rows = jnp.where(straight, y_rows, x_rows)
    other_columns = jnp.where(straight, y_columns, x_columns)
    row_gain, column_gain = column(gain(other_rows)), gain(other_columns)
    for t, (x_tile, y_tile) in enumerate(zip(x_tiles, y_tiles)):
        cols = slice(t * 128, t * 128 + 128)
        keep_ref[:, cols] = jnp.where(straight, x_tile, y_tile)
        other = jnp.where(straight, y_tile, x_tile)
        z_ref[0:128, cols] = squeeze(other * (row_gain * column_gain[:, cols]))
    z_ref[128:144, :] = pack(other_rows, other_columns)
    keep_rp_ref[...] = jnp.broadcast_to(jnp.where(straight, x_rows, y_rows), keep_rp_ref.shape)
    keep_cp_ref[...] = jnp.broadcast_to(jnp.where(straight, x_columns, y_columns), keep_cp_ref.shape)


def second_sum(at, x_kept, x_messages, y_kept, y_messages):
    width = x_kept[0].shape[1]
    shapes = [jax.ShapeDtypeStruct((144, width), jnp.bfloat16)] + [
        jax.ShapeDtypeStruct(s, jnp.float32) for s in ((128, width), (8, 128), (8, width))]
    return pl.pallas_call(
        second_sum_kernel,
        in_specs=[SMEM] + [FULL] * 12,
        out_specs=[FULL] * 4,
        out_shape=shapes,
        compiler_params=params(),
        cost_estimate=cost(10 << 20, 4 << 20),
        name="second_sum",
    )(at, *x_kept, *x_messages, *y_kept, *y_messages)


def last_sum_kernel(row_total, own_ref, rp_ref, cp_ref, message, out_ref):
    tiles, rows, columns = add_messages(own_ref, rp_ref, cp_ref, (message,))

    def back(power):
        return jnp.where(power > 0, lax.rsqrt(power + np.float32(EPS * row_total)), 0.0)

    row_back, column_back = column(back(rows)), back(columns)
    for t, tile in enumerate(tiles):
        cols = slice(t * 128, t * 128 + 128)
        out_ref[:, cols] = tile * (row_back * column_back[:, cols])


def last_sum(row_total, kept, message):
    return pl.pallas_call(
        functools.partial(last_sum_kernel, row_total),
        in_specs=[FULL] * 4,
        out_specs=FULL,
        out_shape=jax.ShapeDtypeStruct(kept[0].shape, jnp.float32),
        compiler_params=params(),
        cost_estimate=cost(4 << 20, 2 << 20),
        name="last_sum",
    )(*kept, message)


def shards(dino_acts, siglip_acts, dino_encoder, siglip_encoder, dino_threshold, siglip_threshold):
    z_hi = lax.axis_index("mp")
    patch = lax.axis_index("patch")
    latent = lax.axis_index("latent")
    x, y = patch // 4, patch % 4
    z_lo, core = latent // 2, latent % 2
    at = jnp.stack([x, y, core, (z_hi == z_lo).astype(jnp.int32)]).astype(jnp.int32)
    row_total = dino_acts.shape[0] * dino_acts.shape[1] * lax.axis_size(AXES)
    latents = dino_encoder.shape[1]

    thresholds = jnp.concatenate([
        jnp.broadcast_to(dino_threshold[None, :], (16, latents)),
        jnp.broadcast_to(siglip_threshold[None, :], (16, latents))])

    first = (x + 2 * y) % 4
    piece = jnp.concatenate([
        lax.dynamic_slice_in_dim(siglip_encoder, first * PIECE, PIECE, 0), thresholds[16:]])
    piece = jnp.concatenate([send(piece[:160], dz=1), send(piece[160:], dz=-1)])

    d_low = send(dino_acts[0], dz=1)
    d_high = send(dino_acts[1], dz=-1)
    dino_sibling = send(dino_encoder, swap=1)
    siglip_sibling = send(siglip_encoder, swap=1)
    thresholds_sibling = send(thresholds, swap=1)

    sampled = resample_local(siglip_acts)
    s_low = send(sampled[0], dz=1)
    s_high = send(sampled[1], dz=-1)

    other = assemble(at, [piece, send(piece, dx=-1), send(piece, dy=1), send(piece, dx=1)])
    other_sibling = send(other, swap=1)

    theta = (thresholds, thresholds_sibling)
    def dino_codes(xs):
        own, away = encode(at, xs, (dino_encoder, dino_sibling), theta, (0, 0), False, "dino_codes")
        return own, send(away, swap=1)

    def siglip_codes(xs):
        near, = encode(at, xs, (siglip_encoder, siglip_sibling), theta, (16, 16), True, "siglip_codes")
        far, = encode(at, xs, (other, other_sibling), (other, other_sibling), (4 * PIECE, 4 * PIECE), True,
                      "siglip_codes")
        return near, far, send(near, swap=1), send(far, swap=1)

    d_near = dino_codes([dino_acts.reshape(-1, dino_acts.shape[-1])])
    s_near = siglip_codes([sampled.reshape(-1, sampled.shape[-1])])
    d_far = dino_codes([d_low, d_high])
    s_far = siglip_codes([s_low, s_high])

    sx = (s_near[0], s_far[0], s_near[2], s_far[2])
    sy = (s_near[1], s_far[1], s_near[3], s_far[3])
    ds = (d_near[0], d_far[0], d_near[1], d_far[1])

    arrived_x, arrived_y = [None] * 4, [None] * 4
    for m in (2, 1, 3):
        part_x, part_y = products(m, at, sx, sy, ds)
        arrived_x[m] = send(part_x, dx=m)
        arrived_y[m] = send(part_y, dy=m)
    own_x, own_y, power_x, power_y, power_d = products(0, at, sx, sy, ds)
    first_x = first_sum(1, at, own_x, power_x, power_d, arrived_x[1:])
    first_y = first_sum(0, at, own_y, power_y, power_d, arrived_y[1:])

    second_x = [send(first_x[m - 1], dy=m) for m in (1, 2, 3)]
    second_y = [send(first_y[m - 1], dx=m) for m in (1, 2, 3)]
    message, *kept = second_sum(at, first_x[3:], second_x, first_y[3:], second_y)

    return last_sum(row_total, kept, send(message, dz=2))


def solution(mesh):
    in_specs = (
        P(("mp", "patch", "latent"), None, None),
        P(("mp", "patch", "latent"), None, None),
        P(None, "latent"),
        P(None, "latent"),
        P("latent"),
        P("latent"),
    )
    out_specs = P(("mp", "patch"), "latent")
    return jax.shard_map(shards, mesh=mesh, in_specs=in_specs, out_specs=out_specs, check_vma=False)
```

```python
import functools

import jax
import jax.numpy as jnp
import numpy as np
from jax import lax
from jax.experimental import pallas as pl
from jax.experimental.pallas import tpu as pltpu
from jax.sharding import PartitionSpec as P

GRID = 16
SIG_SIDE = 27
EPS = 1e-06
AXES = ("mp", "patch", "latent")
VMEM = 24 * 1024 * 1024
TOP = np.float32(np.sqrt(2.0**15))
ANY = pl.BlockSpec(memory_space=pltpu.HBM)
SMEM = pl.BlockSpec(memory_space=pltpu.SMEM)
FULL = pl.BlockSpec(memory_space=pltpu.VMEM)
PIECE = 256


def resample_table(side_cells, grid_cells):
    weights_table = np.zeros((grid_cells, side_cells), np.float32)
    for target in range(grid_cells):
        source = (target + 0.5) * side_cells / grid_cells - 0.5
        low_index = int(np.floor(source))
        upper_part = source - low_index
        weights_table[target, low_index] += 1.0 - upper_part
        weights_table[target, min(low_index + 1, side_cells - 1)] += upper_part
    return weights_table


def resample_local(raw_block):
    table = resample_table(SIG_SIDE, GRID)
    table = np.kron(table, table).astype(np.float32)
    high = table.astype(jnp.bfloat16)
    low = (table - high.astype(np.float32)).astype(jnp.bfloat16)
    images = raw_block.shape[0]

    def part(matrix):
        return lax.dot_general(
            jnp.broadcast_to(jnp.asarray(matrix), (images,) + matrix.shape), raw_block,
            (((2,), (1,)), ((0,), (0,))), preferred_element_type=jnp.float32)

    return (part(high) + part(low)).astype(jnp.bfloat16)


def place(x, y, z, core):
    return (z // 2) * 64 + (x * 4 + y) * 4 + (z % 2) * 2 + core


def moves(step):
    out = []
    for x in range(4):
        for y in range(4):
            for z in range(4):
                for c in range(2):
                    dx, dy, dz, swap = step(c)
                    target = place((x + dx) % 4, (y + dy) % 4, (z + dz) % 4, c ^ swap)
                    out.append((place(x, y, z, c), target))
    return out


def send(value, step):
    return lax.ppermute(value, AXES, moves(step))


def to_sibling(value):
    return send(value, lambda c: (0, 0, 0, 1))


def along_z(value):
    return send(value, lambda c: (0, 0, -1 if c else 1, 0))


def first_way(value, m):
    return send(value, lambda c: (0, m, 0, 0) if c else (m, 0, 0, 0))


def second_way(value, m):
    return send(value, lambda c: (m, 0, 0, 0) if c else (0, m, 0, 0))


def params():
    return pltpu.CompilerParams(vmem_limit_bytes=VMEM)


def cost(flops, size):
    return pl.CostEstimate(flops=flops, bytes_accessed=size, transcendentals=0)


def encode_kernel(chunks, theta_row, *refs):
    xs, (w_ref, t_ref, out, o_buf, o_sem) = refs[:chunks], refs[chunks:]
    depth = xs[0].shape[1]
    theta = t_ref[theta_row:theta_row + 16, :].astype(jnp.float32)[:1, :]
    copies = []
    row = 0
    for k in range(chunks):
        rows = xs[k].shape[0]
        here = pl.ds(row, rows)
        pre = jnp.dot(xs[k][...], w_ref[0:depth, :], preferred_element_type=jnp.float32)
        o_buf[here, :] = jnp.maximum(pre - theta, 0.0).astype(jnp.bfloat16)
        copies.append(pltpu.make_async_copy(o_buf.at[here, :], out.at[here, :], o_sem.at[k]))
        copies[k].start()
        row += rows
    for copy in copies:
        copy.wait()


def encode(xs, weights, thresholds, theta_row, name):
    rows = sum(x.shape[0] for x in xs)
    depth = xs[0].shape[1]
    width = weights.shape[1]
    return pl.pallas_call(
        functools.partial(encode_kernel, len(xs), theta_row),
        in_specs=[FULL] * (len(xs) + 2),
        out_specs=ANY,
        out_shape=jax.ShapeDtypeStruct((rows, width), jnp.bfloat16),
        scratch_shapes=[
            pltpu.VMEM((rows, width), jnp.bfloat16),
            pltpu.SemaphoreType.DMA((len(xs),)),
        ],
        compiler_params=params(),
        cost_estimate=cost(2 * rows * depth * width // 32, 0),
        name=name,
    )(*xs, weights, thresholds)


def encode_pieces_kernel(chunks, at_ref, *refs):
    xs, ws, (out, o_buf, o_sem) = refs[:chunks], refs[chunks:chunks + 4], refs[chunks + 4:]
    depth = xs[0].shape[1]
    copies = []
    for step in range(4):
        col = pl.multiple_of(lax.rem(at_ref[0] + step, 4) * PIECE, PIECE)
        theta = ws[step][depth:depth + 16, :].astype(jnp.float32)[:1, :]
        row = 0
        for k in range(chunks):
            rows = xs[k].shape[0]
            pre = jnp.dot(xs[k][...], ws[step][0:depth, :], preferred_element_type=jnp.float32)
            o_buf[step, row:row + rows, :] = jnp.maximum(pre - theta, 0.0).astype(jnp.bfloat16)
            row += rows
        copies.append(pltpu.make_async_copy(o_buf.at[step], out.at[:, pl.ds(col, PIECE)], o_sem.at[step]))
        copies[step].start()
    for copy in copies:
        copy.wait()


def encode_pieces(at, xs, pieces, name):
    rows = sum(x.shape[0] for x in xs)
    depth = xs[0].shape[1]
    return pl.pallas_call(
        functools.partial(encode_pieces_kernel, len(xs)),
        in_specs=[SMEM] + [FULL] * (len(xs) + 4),
        out_specs=ANY,
        out_shape=jax.ShapeDtypeStruct((rows, 4 * PIECE), jnp.bfloat16),
        scratch_shapes=[
            pltpu.VMEM((4, rows, PIECE), jnp.bfloat16),
            pltpu.SemaphoreType.DMA((4,)),
        ],
        compiler_params=params(),
        cost_estimate=cost(8 * rows * depth * PIECE // 32, 0),
        name=name,
    )(at, *xs, *pieces)


def squeeze(value):
    value = value * value
    value = value * value
    return (value * value).astype(jnp.bfloat16)


def widen(value):
    return jnp.exp2(jnp.log2(value.astype(jnp.float32)) * 0.125)


def gain(power):
    return jnp.where(power > 0, lax.rsqrt(jnp.maximum(power, 1e-37)) * TOP, 0.0)


def root(power):
    return jnp.sqrt(power) * np.float32(1 / TOP)


def column(row):
    return jnp.broadcast_to(row, (128, row.shape[1])).T


def pack(row_power, column_power):
    width = column_power.shape[1]
    if row_power.shape[1] < width:
        row_power = jnp.concatenate(
            [row_power, jnp.zeros((1, width - row_power.shape[1]), jnp.float32)], axis=1)
    at = lax.broadcasted_iota(jnp.int32, (16, width), 0)
    out = jnp.zeros((16, width), jnp.float32)
    for base, power in ((0, column_power), (3, row_power)):
        rest = power
        for part in range(3):
            piece = rest.astype(jnp.bfloat16).astype(jnp.float32)
            out = jnp.where(at == base + part, piece, out)
            rest = rest - piece
    return out.astype(jnp.bfloat16)


def unpack(tail, rows):
    tail = tail.astype(jnp.float32)
    column_power = tail[0:1, :] + tail[1:2, :] + tail[2:3, :]
    row_power = tail[3:4, :rows] + tail[4:5, :rows] + tail[5:6, :rows]
    return row_power, column_power


def square_sum(ref, cols):
    total = None
    for at in range(0, ref.shape[0], 256):
        wide = ref[at:at + 256, cols].astype(jnp.float32)
        part = jnp.sum((wide * wide).reshape(32, 8, -1), axis=0)
        total = part if total is None else total + part
    return jnp.sum(total, axis=0, keepdims=True)


def products_kernel(m, at_ref, *refs):
    ss, ds, refs = refs[:8], refs[8:12], refs[12:]
    if m == 2:
        out, out_dp, refs = refs[0], refs[1], refs[2:]
    elif m:
        in_dp, out, refs = refs[0], refs[1], refs[2:]
    else:
        in_dp, message, _, out, out_sp, out_dp, refs = *refs[:6], refs[6:]
    s_buf, o_buf, a_buf, s_sem, o_sem = refs
    rows, width = ds[0].shape
    tile = 512
    core = at_ref[1]
    target = lax.rem(at_ref[2] + m, 4)
    s_copies = []
    for which in range(2):
        for k in range(2):
            for b in range(4):
                block = jnp.where(core == 0, target * 4 + b, b * 4 + target)
                mine = block // 8 == core
                col = pl.ds(pl.multiple_of(lax.rem(block, 8) * 128, 128), 128)
                choices = [pltpu.make_async_copy(
                    ss[which * 4 + k * 2 + choice].at[:, col],
                    s_buf.at[which, pl.ds(k * 2 * rows, 2 * rows), pl.ds(b * 128, 128)],
                    s_sem.at[which * 8 + k * 4 + b]) for choice in range(2)]
                first = choices[k]
                second = choices[1 - k]
                pl.when(mine)(first.start)
                pl.when(jnp.logical_not(mine))(second.start)
                s_copies.append(first)
    out_copies = []
    gains = []
    if not m:
        copies = [pltpu.make_async_copy(message.at[pl.ds(at, rows), :], o_buf.at[i, pl.ds(0, rows), :], o_sem.at[i])
                  for i, (at, rows) in enumerate(((0, 512), (512, 512), (1024, 16)))]
        for copy in copies:
            copy.start()
        for copy in copies:
            copy.wait()
        row_power, column_power = unpack(o_buf[2, 0:16, :], 1024)
        column_root = root(column_power)
        out_dp[...] = jnp.broadcast_to(in_dp[0:1, :] + column_power, out_dp.shape)
    for which in range(2):
        for copy in s_copies[which * 8:which * 8 + 8]:
            copy.wait()
        s_power = square_sum(s_buf.at[which], slice(None))
        if m:
            row_gain = jnp.concatenate([column(gain(s_power))] * (tile // 128), axis=1)
            a_buf[which] = jnp.broadcast_to(s_power, (8, 512))
        else:
            mine = slice(which * 512, which * 512 + 512)
            out_sp[:, mine] = jnp.broadcast_to(s_power + row_power[:, mine], (8, 512))
            row_root = jnp.concatenate([column(root(row_power[:, mine]))] * (tile // 128), axis=1)
        for t in range(width // tile):
            cols = slice(t * tile, t * tile + tile)
            if which == 0:
                if m == 2:
                    out_dp[:, cols] = jnp.broadcast_to(sum(square_sum(d, cols) for d in ds), (8, tile))
                if m:
                    gains.append(gain((out_dp if m == 2 else in_dp)[0:1, cols]))
            total = sum(
                lax.dot_general(s_buf[which, k * rows:k * rows + rows, :], ds[k][:, cols], (((0,), (0,)), ((), ())),
                                preferred_element_type=jnp.float32) for k in range(4))
            if m:
                total = squeeze(total * row_gain * gains[t])
            if m:
                o_buf[which, :, cols] = total
            else:
                out[mine, cols] = total + widen(o_buf[which, :, cols]) * (row_root * column_root[:, cols])
        if m:
            out_copies.append(pltpu.make_async_copy(
                o_buf.at[which], out.at[pl.ds(which * 512, 512), :], o_sem.at[which]))
            out_copies[which].start()
    if m:
        tail = o_buf.at[2, pl.ds(0, 16), :]
        tail[...] = pack(jnp.concatenate([a_buf[0, 0:1, :], a_buf[1, 0:1, :]], axis=1),
                         (out_dp if m == 2 else in_dp)[0:1, :])
        out_copies.append(pltpu.make_async_copy(tail, out.at[pl.ds(1024, 16), :], o_sem.at[2]))
        out_copies[2].start()
    for copy in out_copies:
        copy.wait()


def products(m, at, ss, ds, d_power=None, message=None, after=None):
    rows = ds[0].shape[0]
    width = ds[0].shape[1]
    f32 = jnp.float32
    if m:
        shapes, specs = [jax.ShapeDtypeStruct((1040, width), jnp.bfloat16)], [ANY]
    else:
        shapes = [jax.ShapeDtypeStruct(s, f32) for s in ((1024, width), (8, 1024), (8, width))]
        specs = [FULL] * 3
    operands = [at, *ss, *ds]
    if m == 2:
        shapes, specs = shapes + [jax.ShapeDtypeStruct((8, width), f32)], specs + [FULL]
    else:
        operands.append(d_power)
    in_specs = [SMEM] + [ANY] * 8 + [FULL] * (len(operands) - 9)
    if not m:
        operands += [message, after]
        in_specs += [ANY] * 2
    return pl.pallas_call(
        functools.partial(products_kernel, m),
        in_specs=in_specs,
        out_specs=specs,
        out_shape=shapes,
        scratch_shapes=[
            pltpu.VMEM((2, 4 * rows, 512), jnp.bfloat16),
            pltpu.VMEM((3, 512, width), jnp.bfloat16),
            pltpu.VMEM((2, 8, 512), f32),
            pltpu.SemaphoreType.DMA((16,)),
            pltpu.SemaphoreType.DMA((3,)),
        ],
        compiler_params=params(),
        cost_estimate=cost(2 * 1024 * 4 * rows * width, 10 << 20),
        name="products",
    )(*operands)


ORDER = (2, 1, 3, 0)


def first_sum_kernel(at_ref, own_ref, sp_ref, dp_ref, *refs):
    messages, (o1, o2, o3, keep_ref, keep_rp_ref, keep_cp_ref), scratch = refs[:2], refs[2:8], refs[8:]
    m_buf, o_buf, scale_ref, power_ref, m_sem, o_sem = scratch
    width = own_ref.shape[1]
    tails, blocks = [], []
    for k, message in enumerate(messages):
        rows = pl.ds(1024, 16)
        tails.append(pltpu.make_async_copy(message.at[rows, :], m_buf.at[k, rows, :], m_sem.at[8, k]))
    for i, m in enumerate(ORDER):
        target = lax.rem(at_ref[3] + m, 4)
        for which in range(2):
            rows = pl.ds(pl.multiple_of(which * 512 + target * 128, 128), 128)
            blocks.append((rows, [
                pltpu.make_async_copy(message.at[rows, :], m_buf.at[k, rows, :], m_sem.at[2 * i + which, k])
                for k, message in enumerate(messages)]))
    for copies in [tails] + [copies for _, copies in blocks]:
        for copy in copies:
            copy.start()
    for copy in tails:
        copy.wait()

    row_total, column_total = sp_ref[0:1, :], dp_ref[0:1, :]
    column_roots = []
    for k in range(2):
        row_power, column_power = unpack(m_buf[k, 1024:1040, :], 1024)
        scale_ref[k] = column(root(row_power))
        column_roots.append(root(column_power))
        row_total = row_total + row_power
        column_total = column_total + column_power
    scale_ref[2] = column(gain(row_total))
    column_gain = gain(column_total)
    power_ref[...] = jnp.broadcast_to(row_total, power_ref.shape)
    keep_cp_ref[...] = jnp.broadcast_to(column_total, keep_cp_ref.shape)

    out_copies = []
    for i, m in enumerate(ORDER):
        powers = []
        for which in range(2):
            here, copies = blocks[2 * i + which]
            for copy in copies:
                copy.wait()
            scales = [scale_ref[k, here, :] for k in range(3)]
            for at in range(0, width, 128):
                cols = slice(at, at + 128)
                total = own_ref[here, cols]
                for k in range(2):
                    total = total + widen(m_buf[k, here, cols]) * (scales[k] * column_roots[k][:, cols])
                if m:
                    o_buf[i, which * 128:which * 128 + 128, cols] = squeeze(
                        total * (scales[2] * column_gain[:, cols]))
                else:
                    keep_ref[which * 128:which * 128 + 128, cols] = total
            powers.append(power_ref[:, here])
        powers = jnp.concatenate(powers, axis=1)
        if m:
            o_buf[i, 256:272, :] = pack(powers[0:1, :], column_total)
            out_copies.append(pltpu.make_async_copy(o_buf.at[i], (o1, o2, o3)[m - 1], o_sem.at[i]))
            out_copies[i].start()
        else:
            keep_rp_ref[...] = powers
    for copy in out_copies:
        copy.wait()


def first_sum(at, own, row_power, column_power, messages):
    width = own.shape[1]
    shapes = [jax.ShapeDtypeStruct((272, width), jnp.bfloat16)] * 3 + [
        jax.ShapeDtypeStruct(s, jnp.float32) for s in ((256, width), (8, 256), (8, width))]
    return pl.pallas_call(
        first_sum_kernel,
        in_specs=[SMEM] + [FULL] * 3 + [ANY] * 2,
        out_specs=[ANY] * 3 + [FULL] * 3,
        out_shape=shapes,
        scratch_shapes=[
            pltpu.VMEM((2, 1040, width), jnp.bfloat16),
            pltpu.VMEM((3, 272, width), jnp.bfloat16),
            pltpu.VMEM((3, 1024, 128), jnp.float32),
            pltpu.VMEM((8, 1024), jnp.float32),
            pltpu.SemaphoreType.DMA((9, 2)),
            pltpu.SemaphoreType.DMA((3,)),
        ],
        compiler_params=params(),
        cost_estimate=cost(20 << 20, 6 << 20),
        name="first_sum",
    )(at, own, row_power, column_power, *messages)


def add_messages(own_ref, rp_ref, cp_ref, messages):
    rows, width = own_ref.shape
    row_total, column_total = rp_ref[0:1, :], cp_ref[0:1, :]
    scales = []
    for message in messages:
        row_power, column_power = unpack(message[rows:rows + 16, :], rows)
        scales.append((column(root(row_power)), root(column_power)))
        row_total = row_total + row_power
        column_total = column_total + column_power
    blocks = []
    for row in range(0, rows, 128):
        here = slice(row, row + 128)
        tiles = []
        for at in range(0, width, 128):
            cols = slice(at, at + 128)
            total = own_ref[here, cols]
            for message, (row_scale, column_scale) in zip(messages, scales):
                total = total + widen(message[here, cols]) * (row_scale[here, :] * column_scale[:, cols])
            tiles.append(total)
        blocks.append(tiles)
    return blocks, row_total, column_total


def second_sum_kernel(at_ref, own_ref, rp_ref, cp_ref, m1, m2, m3, z_ref, keep_ref, keep_rp_ref, keep_cp_ref):
    straight = at_ref[4] == 1
    blocks, rows, columns = add_messages(own_ref, rp_ref, cp_ref, (m1, m2, m3))
    other_rows = jnp.where(straight, rows[:, 128:], rows[:, :128])
    row_gain, column_gain = column(gain(other_rows)), gain(columns)
    for t, (first, second) in enumerate(zip(*blocks)):
        cols = slice(t * 128, t * 128 + 128)
        keep_ref[:, cols] = jnp.where(straight, first, second)
        other = jnp.where(straight, second, first)
        z_ref[0:128, cols] = squeeze(other * (row_gain * column_gain[:, cols]))
    z_ref[128:144, :] = pack(other_rows, columns)
    keep_rp_ref[...] = jnp.broadcast_to(jnp.where(straight, rows[:, :128], rows[:, 128:]), keep_rp_ref.shape)
    keep_cp_ref[...] = jnp.broadcast_to(columns, keep_cp_ref.shape)


def second_sum(at, kept, messages):
    width = kept[0].shape[1]
    shapes = [jax.ShapeDtypeStruct((144, width), jnp.bfloat16)] + [
        jax.ShapeDtypeStruct(s, jnp.float32) for s in ((128, width), (8, 128), (8, width))]
    return pl.pallas_call(
        second_sum_kernel,
        in_specs=[SMEM] + [FULL] * 6,
        out_specs=[FULL] * 4,
        out_shape=shapes,
        compiler_params=params(),
        cost_estimate=cost(10 << 20, 4 << 20),
        name="second_sum",
    )(at, *kept, *messages)


def last_sum_kernel(row_total, own_ref, rp_ref, cp_ref, message, out_ref):
    (tiles,), rows, columns = add_messages(own_ref, rp_ref, cp_ref, (message,))

    def back(power):
        return jnp.where(power > 0, lax.rsqrt(power + np.float32(EPS * row_total)), 0.0)

    row_back, column_back = column(back(rows)), back(columns)
    for t, tile in enumerate(tiles):
        cols = slice(t * 128, t * 128 + 128)
        out_ref[:, cols] = tile * (row_back * column_back[:, cols])


def last_sum(row_total, kept, message):
    return pl.pallas_call(
        functools.partial(last_sum_kernel, row_total),
        in_specs=[FULL] * 4,
        out_specs=FULL,
        out_shape=jax.ShapeDtypeStruct(kept[0].shape, jnp.float32),
        compiler_params=params(),
        cost_estimate=cost(4 << 20, 2 << 20),
        name="last_sum",
    )(*kept, message)


def shards(dino_acts, siglip_acts, dino_encoder, siglip_encoder, dino_threshold, siglip_threshold):
    z_hi = lax.axis_index("mp")
    patch = lax.axis_index("patch")
    latent = lax.axis_index("latent")
    x, y = patch // 4, patch % 4
    z_lo, core = latent // 2, latent % 2
    first = (x + 2 * y) % 4
    at = jnp.stack([
        first, core, jnp.where(core == 0, x, y), jnp.where(core == 0, y, x),
        (z_hi == z_lo).astype(jnp.int32)]).astype(jnp.int32)
    row_total = dino_acts.shape[0] * dino_acts.shape[1] * lax.axis_size(AXES)
    latents = dino_encoder.shape[1]

    thresholds = jnp.concatenate([
        jnp.broadcast_to(dino_threshold[None, :], (16, latents)),
        jnp.broadcast_to(siglip_threshold[None, :], (16, latents))])

    theta = (thresholds, to_sibling(thresholds))
    d_own = dino_acts.reshape(-1, dino_acts.shape[-1])
    dino_sibling = to_sibling(dino_encoder)
    siglip_sibling = to_sibling(siglip_encoder)

    piece = along_z(jnp.concatenate([
        lax.dynamic_slice_in_dim(siglip_encoder, first * PIECE, PIECE, 1),
        lax.dynamic_slice_in_dim(thresholds[16:], first * PIECE, PIECE, 1)]))
    s_own = resample_local(siglip_acts).reshape(-1, siglip_acts.shape[-1])
    s_ext = along_z(s_own)
    piece, s_own, d_own, siglip_sibling, dino_sibling = lax.optimization_barrier(
        (piece, s_own, d_own, siglip_sibling, dino_sibling))
    d_ext = along_z(d_own)
    pieces = [
        piece,
        send(piece, lambda c: (-1, 0, 0, 0)),
        send(piece, lambda c: (0, 1, 0, 0)),
        send(piece, lambda c: (1, 0, 0, 0)),
    ]

    def dino_codes(xs):
        away = encode(xs, dino_sibling, theta[1], 0, "dino_codes")
        return encode(xs, dino_encoder, theta[0], 0, "dino_codes"), to_sibling(away)

    def siglip_codes(xs, weights, thresholds, row):
        return encode(xs, weights, thresholds, row, "siglip_codes")

    d_near, d_near_sibling = dino_codes([d_own])
    s_ext, d_near = lax.optimization_barrier((s_ext, d_near))
    xs = [s_own, s_ext]
    one = [siglip_codes(xs, siglip_encoder, theta[0], 16), siglip_codes(xs, siglip_sibling, theta[1], 16)]
    *one, p0, p1, p2, p3 = lax.optimization_barrier((*one, *pieces))
    pieces = [p0, p1, p2, p3]
    pieces_sibling = [to_sibling(p) for p in pieces]
    two = [encode_pieces(at, xs, pieces, "siglip_codes")]
    d_ext, two[0] = lax.optimization_barrier((d_ext, two[0]))
    two.append(encode_pieces(at, xs, pieces_sibling, "siglip_codes"))
    d_far, d_far_sibling = dino_codes([d_ext])

    ss = [*one, to_sibling(one[0]), to_sibling(one[1]), *two, to_sibling(two[0]), to_sibling(two[1])]
    ds = (d_near, d_far, d_near_sibling, d_far_sibling)

    part, d_power = products(2, at, ss, ds)
    from_two = first_way(part, 2)
    arrived = []
    for m in (1, 3):
        part, = products(m, at, ss, ds, d_power)
        arrived.append(first_way(part, m))
    own = products(0, at, ss, ds, d_power, from_two, part)
    sums = first_sum(at, *own, arrived)

    message, *kept = second_sum(at, sums[3:], [second_way(sums[m - 1], m) for m in (1, 2, 3)])

    return last_sum(row_total, kept, send(message, lambda c: (0, 0, 2, 0)))


def solution(mesh):
    in_specs = (
        P(("mp", "patch", "latent"), None, None),
        P(("mp", "patch", "latent"), None, None),
        P(None, "latent"),
        P(None, "latent"),
        P("latent"),
        P("latent"),
    )
    out_specs = P(("mp", "patch"), "latent")
    return jax.shard_map(shards, mesh=mesh, in_specs=in_specs, out_specs=out_specs, check_vma=False)
```

```python
import functools

import jax
import jax.numpy as jnp
import numpy as np
from jax import lax
from jax.experimental import pallas as pl
from jax.experimental.pallas import tpu as pltpu
from jax.sharding import PartitionSpec as P

GRID = 16
SIG_SIDE = 27
EPS = 1e-06
AXES = ("mp", "patch", "latent")
VMEM = 16 * 1024 * 1024
TOP = np.float32(np.sqrt(2.0**15))
ANY = pl.BlockSpec(memory_space=pl.ANY)
HBM = pl.BlockSpec(memory_space=pltpu.HBM)
SMEM = pl.BlockSpec(memory_space=pltpu.SMEM)
FULL = pl.BlockSpec(memory_space=pltpu.VMEM)
PIECE = 256


def resample_table(side_cells, grid_cells):
    weights_table = np.zeros((grid_cells, side_cells), np.float32)
    for target in range(grid_cells):
        source = (target + 0.5) * side_cells / grid_cells - 0.5
        low_index = int(np.floor(source))
        upper_part = source - low_index
        weights_table[target, low_index] += 1.0 - upper_part
        weights_table[target, min(low_index + 1, side_cells - 1)] += upper_part
    return weights_table


def resample_local(raw_block):
    table = resample_table(SIG_SIDE, GRID)
    table = np.kron(table, table).astype(np.float32)
    high = table.astype(jnp.bfloat16)
    low = (table - high.astype(np.float32)).astype(jnp.bfloat16)
    images = raw_block.shape[0]

    def part(matrix):
        return lax.dot_general(
            jnp.broadcast_to(jnp.asarray(matrix), (images,) + matrix.shape), raw_block,
            (((2,), (1,)), ((0,), (0,))), preferred_element_type=jnp.float32)

    return (part(high) + part(low)).astype(jnp.bfloat16)


def place(x, y, z, core):
    return (z // 2) * 64 + (x * 4 + y) * 4 + (z % 2) * 2 + core


def moves(step):
    out = []
    for x in range(4):
        for y in range(4):
            for z in range(4):
                for c in range(2):
                    dx, dy, dz, swap = step(c)
                    target = place((x + dx) % 4, (y + dy) % 4, (z + dz) % 4, c ^ swap)
                    out.append((place(x, y, z, c), target))
    return out


def send(value, step):
    return lax.ppermute(value, AXES, moves(step))


def to_sibling(value):
    return send(value, lambda c: (0, 0, 0, 1))


def along_z(value):
    return send(value, lambda c: (0, 0, -1 if c else 1, 0))


def first_way(value, m):
    return send(value, lambda c: (0, m, 0, 0) if c else (m, 0, 0, 0))


def second_way(value, m):
    return send(value, lambda c: (m, 0, 0, 0) if c else (0, m, 0, 0))


def params():
    return pltpu.CompilerParams(vmem_limit_bytes=VMEM)


def cost(flops, size):
    return pl.CostEstimate(flops=flops, bytes_accessed=size, transcendentals=0)


def encode_kernel(chunks, theta_row, *refs):
    xs, (w_ref, t_ref, out, o_buf, o_sem) = refs[:chunks], refs[chunks:]
    depth = xs[0].shape[1]
    theta = t_ref[theta_row:theta_row + 16, :].astype(jnp.float32)[:1, :]
    copies = []
    row = 0
    for k in range(chunks):
        rows = xs[k].shape[0]
        here = pl.ds(row, rows)
        pre = jnp.dot(xs[k][...], w_ref[0:depth, :], preferred_element_type=jnp.float32)
        o_buf[here, :] = jnp.maximum(pre - theta, 0.0).astype(jnp.bfloat16)
        copies.append(pltpu.make_async_copy(o_buf.at[here, :], out.at[here, :], o_sem.at[k]))
        copies[k].start()
        row += rows
    for copy in copies:
        copy.wait()


def encode(xs, weights, thresholds, theta_row, name):
    rows = sum(x.shape[0] for x in xs)
    depth = xs[0].shape[1]
    width = weights.shape[1]
    return pl.pallas_call(
        functools.partial(encode_kernel, len(xs), theta_row),
        in_specs=[FULL] * (len(xs) + 2),
        out_specs=HBM,
        out_shape=jax.ShapeDtypeStruct((rows, width), jnp.bfloat16),
        scratch_shapes=[
            pltpu.VMEM((rows, width), jnp.bfloat16),
            pltpu.SemaphoreType.DMA((len(xs),)),
        ],
        compiler_params=params(),
        cost_estimate=cost(2 * rows * depth * width // 32, 0),
        name=name,
    )(*xs, weights, thresholds)


def encode_pieces_kernel(chunks, at_ref, *refs):
    xs, ws, (out, w_buf, o_buf, w_sem, o_sem) = refs[:chunks], refs[chunks:chunks + 4], refs[chunks + 4:]
    depth = xs[0].shape[1]
    w_copies = [pltpu.make_async_copy(ws[k], w_buf.at[k], w_sem.at[k]) for k in range(4)]
    for copy in w_copies:
        copy.start()
    copies = []
    for step in range(4):
        col = pl.multiple_of(lax.rem(at_ref[0] + step, 4) * PIECE, PIECE)
        w_copies[step].wait()
        theta = w_buf[step, depth:depth + 16, :].astype(jnp.float32)[:1, :]
        row = 0
        for k in range(chunks):
            rows = xs[k].shape[0]
            pre = jnp.dot(xs[k][...], w_buf[step, 0:depth, :], preferred_element_type=jnp.float32)
            o_buf[step, row:row + rows, :] = jnp.maximum(pre - theta, 0.0).astype(jnp.bfloat16)
            row += rows
        copies.append(pltpu.make_async_copy(o_buf.at[step], out.at[:, pl.ds(col, PIECE)], o_sem.at[step]))
        copies[step].start()
    for copy in copies:
        copy.wait()


def encode_pieces(at, xs, pieces, name):
    rows = sum(x.shape[0] for x in xs)
    depth = xs[0].shape[1]
    return pl.pallas_call(
        functools.partial(encode_pieces_kernel, len(xs)),
        in_specs=[SMEM] + [FULL] * len(xs) + [ANY] * 4,
        out_specs=HBM,
        out_shape=jax.ShapeDtypeStruct((rows, 4 * PIECE), jnp.bfloat16),
        scratch_shapes=[
            pltpu.VMEM((4,) + pieces[0].shape, jnp.bfloat16),
            pltpu.VMEM((4, rows, PIECE), jnp.bfloat16),
            pltpu.SemaphoreType.DMA((4,)),
            pltpu.SemaphoreType.DMA((4,)),
        ],
        compiler_params=params(),
        cost_estimate=cost(8 * rows * depth * PIECE // 32, 0),
        name=name,
    )(at, *xs, *pieces)


def squeeze(value):
    value = value * value
    value = value * value
    return (value * value).astype(jnp.bfloat16)


def widen(value):
    return jnp.exp2(jnp.log2(value.astype(jnp.float32)) * 0.125)


def gain(power):
    return jnp.where(power > 0, lax.rsqrt(jnp.maximum(power, 1e-37)) * TOP, 0.0)


def root(power):
    return jnp.sqrt(power) * np.float32(1 / TOP)


def column(row):
    return jnp.broadcast_to(row, (128, row.shape[1])).T


def pack(row_power, column_power):
    width = column_power.shape[1]
    if row_power.shape[1] < width:
        row_power = jnp.concatenate(
            [row_power, jnp.zeros((1, width - row_power.shape[1]), jnp.float32)], axis=1)
    at = lax.broadcasted_iota(jnp.int32, (16, width), 0)
    out = jnp.zeros((16, width), jnp.float32)
    for base, power in ((0, column_power), (3, row_power)):
        rest = power
        for part in range(3):
            piece = rest.astype(jnp.bfloat16).astype(jnp.float32)
            out = jnp.where(at == base + part, piece, out)
            rest = rest - piece
    return out.astype(jnp.bfloat16)


def unpack(tail, rows):
    tail = tail.astype(jnp.float32)
    column_power = tail[0:1, :] + tail[1:2, :] + tail[2:3, :]
    row_power = tail[3:4, :rows] + tail[4:5, :rows] + tail[5:6, :rows]
    return row_power, column_power


def square_sum(ref, cols):
    total = None
    for at in range(0, ref.shape[0], 256):
        wide = ref[at:at + 256, cols].astype(jnp.float32)
        part = jnp.sum((wide * wide).reshape(32, 8, -1), axis=0)
        total = part if total is None else total + part
    return jnp.sum(total, axis=0, keepdims=True)


def products_kernel(jobs, leads, at_ref, *refs):
    ss, ds, refs = refs[:8], refs[8:12], list(refs[12:])
    dp_ref = None if leads else refs.pop(0)
    relays = [refs.pop(0) if m in (1, 3) else None for m, _ in jobs]
    if jobs[0][0] == 0:
        refs.pop(0)
    outs = [[refs.pop(0) for _ in range(1 if m in (1, 3) else 2)] for m, _ in jobs]
    if leads:
        dp_ref = refs.pop(0)
    s_bufs, r_bufs, o_bufs, s_sem, r_sem, o_sem = refs
    rows, width = ds[0].shape
    tile = width // 2
    core = at_ref[1]
    s_copies, r_copies, copies = [], [], []
    for j, (m, turn) in enumerate(jobs):
        target = lax.rem(at_ref[2] + m, 4)
        s_copies.append([])
        for k in range(2):
            for b in range(4):
                block = jnp.where(core == 0, target * 4 + b, b * 4 + target)
                mine = block // 8 == core
                col = pl.ds(pl.multiple_of(lax.rem(block, 8) * 128, 128), 128)
                for which in range(2):
                    chosen = at_ref[4] == (which if turn == 0 else 1 - which)
                    choices = [pltpu.make_async_copy(
                        ss[which * 4 + k * 2 + choice].at[:, col],
                        s_bufs.at[j, pl.ds(k * 2 * rows, 2 * rows), pl.ds(b * 128, 128)],
                        s_sem.at[j, k * 4 + b]) for choice in range(2)]
                    pl.when(chosen & mine)(choices[k].start)
                    pl.when(chosen & jnp.logical_not(mine))(choices[1 - k].start)
                s_copies[j].append(choices[k])
        r_copies.append(None)
        if m in (1, 3):
            r_copies[j] = pltpu.make_async_copy(relays[j], r_bufs.at[j], r_sem.at[j])
            r_copies[j].start()
    if leads:
        for t in range(2):
            cols = slice(t * tile, t * tile + tile)
            dp_ref[:, cols] = jnp.broadcast_to(sum(square_sum(d, cols) for d in ds), (8, tile))

    def job(j, m):
        s_buf, r_buf, o_buf, out = s_bufs.at[j], r_bufs.at[j], o_bufs.at[j], outs[j]
        relayed = {1: 0, 3: 1}.get(m)
        column_powers = [dp_ref[0:1, 0:tile], dp_ref[0:1, tile:width]]

        def dots(t, ks):
            return sum(
                lax.dot_general(s_buf[k * rows:k * rows + rows, :], ds[k][:, t * tile:t * tile + tile],
                                (((0,), (0,)), ((), ())), preferred_element_type=jnp.float32) for k in ks)

        for copy in s_copies[j][:4]:
            copy.wait()
        near = dots(0, (0, 1))
        for copy in s_copies[j][4:]:
            copy.wait()
        s_power = square_sum(s_buf, slice(None))
        row_powers = [s_power, s_power]
        if relayed is not None:
            r_copies[j].wait()
            r_rows, r_columns = unpack(r_buf[512:528, :], 512)
            row_powers[relayed] = s_power + r_rows
            column_powers[relayed] = column_powers[relayed] + r_columns
            r_scale = jnp.concatenate([column(root(r_rows))] * (tile // 128), axis=1) * root(r_columns)
        for t in range(2):
            cols = slice(t * tile, t * tile + tile)
            total = near + dots(0, (2, 3)) if t == 0 else dots(1, (0, 1, 2, 3))
            if t == relayed:
                total = total + widen(r_buf[0:512, :]) * r_scale
            if not m:
                out[0][:, cols] = total
                continue
            if t == 0 or relayed is not None:
                row_gain = jnp.concatenate([column(gain(row_powers[t]))] * (tile // 128), axis=1)
            o_buf[0:512, cols] = squeeze(total * row_gain * gain(column_powers[t]))
            o_buf[512:528, cols] = pack(row_powers[t], column_powers[t])
            target_ref = out[t] if m == 2 else out[0].at[:, pl.ds(t * tile, tile)]
            copy = pltpu.make_async_copy(o_buf.at[:, pl.ds(t * tile, tile)], target_ref, o_sem.at[j, t])
            copy.start()
            copies.append(copy)
        if not m:
            out[1][...] = jnp.broadcast_to(s_power, out[1].shape)

    for j, (m, _) in enumerate(jobs):
        job(j, m)
    for copy in copies:
        copy.wait()


def products(jobs, at, ss, ds, d_power=None, relays=(), after=None):
    rows, width = ds[0].shape
    f32 = jnp.float32
    leads = d_power is None
    count = len(jobs)
    shapes, specs = [], []
    for m, _ in jobs:
        if m == 2:
            shapes += [jax.ShapeDtypeStruct((528, width // 2), jnp.bfloat16)] * 2
            specs += [HBM] * 2
        elif m:
            shapes += [jax.ShapeDtypeStruct((528, width), jnp.bfloat16)]
            specs += [HBM]
        else:
            shapes += [jax.ShapeDtypeStruct(s, f32) for s in ((512, width), (8, 512))]
            specs += [FULL] * 2
    operands = [at, *ss, *ds]
    if leads:
        shapes, specs = shapes + [jax.ShapeDtypeStruct((8, width), f32)], specs + [FULL]
    else:
        operands.append(d_power)
    in_specs = [SMEM] + [HBM] * 8 + [FULL] * (len(operands) - 9)
    extra = [*relays] if after is None else [after]
    return pl.pallas_call(
        functools.partial(products_kernel, jobs, leads),
        in_specs=in_specs + [HBM] * len(extra),
        out_specs=specs,
        out_shape=shapes,
        scratch_shapes=[
            pltpu.VMEM((count, 4 * rows, 512), jnp.bfloat16),
            pltpu.VMEM((count, 528, width // 2), jnp.bfloat16),
            pltpu.VMEM((count, 528, width), jnp.bfloat16),
            pltpu.SemaphoreType.DMA((count, 8)),
            pltpu.SemaphoreType.DMA((count,)),
            pltpu.SemaphoreType.DMA((count, 2)),
        ],
        compiler_params=params(),
        cost_estimate=cost(2 * 512 * 4 * rows * width * count, 5 << 20),
        name="products",
    )(*operands, *extra)


ORDER = (2, 1, 3, 0)


def first_sum_kernel(at_ref, own_ref, sp_ref, dp_ref, *refs):
    messages, (o1, o2, o3, keep_ref, keep_rp_ref, keep_cp_ref), scratch = refs[:2], refs[2:8], refs[8:]
    m_buf, o_buf, scale_ref, power_ref, m_sem, o_sem = scratch
    width = own_ref.shape[1]
    tails, blocks = [], []
    for k, message in enumerate(messages):
        rows = pl.ds(512, 16)
        tails.append(pltpu.make_async_copy(message.at[rows, :], m_buf.at[k, rows, :], m_sem.at[4, k]))
    for i, m in enumerate(ORDER):
        rows = pl.ds(pl.multiple_of(lax.rem(at_ref[3] + m, 4) * 128, 128), 128)
        blocks.append((rows, [
            pltpu.make_async_copy(message.at[rows, :], m_buf.at[k, rows, :], m_sem.at[i, k])
            for k, message in enumerate(messages)]))
    for copies in [tails] + [copies for _, copies in blocks]:
        for copy in copies:
            copy.start()
    for copy in tails:
        copy.wait()

    row_total, column_total = sp_ref[0:1, :], dp_ref[0:1, :]
    column_roots = []
    half = width // 2
    for k in range(2):
        parts = [unpack(m_buf[k, 512:528, h * half:h * half + half], 512) for h in range(2)]
        for h in range(2):
            scale_ref[2 * k + h] = column(root(parts[h][0]))
        column_power = jnp.concatenate([part[1] for part in parts], axis=1)
        column_roots.append(root(column_power))
        row_total = row_total + parts[0][0]
        column_total = column_total + column_power
    scale_ref[4] = column(gain(row_total))
    column_gain = gain(column_total)
    power_ref[...] = jnp.broadcast_to(row_total, power_ref.shape)
    keep_cp_ref[...] = jnp.broadcast_to(column_total, keep_cp_ref.shape)

    out_copies = []
    for i, m in enumerate(ORDER):
        here, copies = blocks[i]
        for copy in copies:
            copy.wait()
        scales = [scale_ref[k, here, :] for k in range(5)]
        for at in range(0, width, 128):
            cols = slice(at, at + 128)
            total = own_ref[here, cols]
            for k in range(2):
                total = total + widen(m_buf[k, here, cols]) * (
                    scales[2 * k + at // half] * column_roots[k][:, cols])
            if m:
                o_buf[i, 0:128, cols] = squeeze(total * (scales[4] * column_gain[:, cols]))
            else:
                keep_ref[:, cols] = total
        powers = power_ref[:, here]
        if m:
            o_buf[i, 128:144, :] = pack(powers[0:1, :], column_total)
            out_copies.append(pltpu.make_async_copy(o_buf.at[i], (o1, o2, o3)[m - 1], o_sem.at[i]))
            out_copies[i].start()
        else:
            keep_rp_ref[...] = powers
    for copy in out_copies:
        copy.wait()


def first_sum(at, own, row_power, column_power, messages):
    width = own.shape[1]
    shapes = [jax.ShapeDtypeStruct((144, width), jnp.bfloat16)] * 3 + [
        jax.ShapeDtypeStruct(s, jnp.float32) for s in ((128, width), (8, 128), (8, width))]
    return pl.pallas_call(
        first_sum_kernel,
        in_specs=[SMEM] + [FULL] * 3 + [HBM] * 2,
        out_specs=[HBM] * 3 + [FULL] * 3,
        out_shape=shapes,
        scratch_shapes=[
            pltpu.VMEM((2, 528, width), jnp.bfloat16),
            pltpu.VMEM((3, 144, width), jnp.bfloat16),
            pltpu.VMEM((5, 512, 128), jnp.float32),
            pltpu.VMEM((8, 512), jnp.float32),
            pltpu.SemaphoreType.DMA((5, 2)),
            pltpu.SemaphoreType.DMA((3,)),
        ],
        compiler_params=params(),
        cost_estimate=cost(10 << 20, 3 << 20),
        name="first_sum",
    )(at, own, row_power, column_power, *messages)


def add_messages(own_ref, rp_ref, cp_ref, messages):
    rows, width = own_ref.shape
    row_total, column_total = rp_ref[0:1, :], cp_ref[0:1, :]
    scales = []
    for message in messages:
        row_power, column_power = unpack(message[rows:rows + 16, :], rows)
        scales.append((column(root(row_power)), root(column_power)))
        row_total = row_total + row_power
        column_total = column_total + column_power
    tiles = []
    for at in range(0, width, 128):
        cols = slice(at, at + 128)
        total = own_ref[:, cols]
        for message, (row_scale, column_scale) in zip(messages, scales):
            total = total + widen(message[0:rows, cols]) * (row_scale * column_scale[:, cols])
        tiles.append(total)
    return tiles, row_total, column_total


def second_sum_kernel(own_ref, rp_ref, cp_ref, m1, m2, m3, z_ref):
    tiles, rows, columns = add_messages(own_ref, rp_ref, cp_ref, (m1, m2, m3))
    row_gain, column_gain = column(gain(rows)), gain(columns)
    for t, tile in enumerate(tiles):
        cols = slice(t * 128, t * 128 + 128)
        z_ref[0:128, cols] = squeeze(tile * (row_gain * column_gain[:, cols]))
    z_ref[128:144, :] = pack(rows, columns)


def second_sum(kept, messages):
    return pl.pallas_call(
        second_sum_kernel,
        in_specs=[FULL] * 6,
        out_specs=FULL,
        out_shape=jax.ShapeDtypeStruct((144, kept[0].shape[1]), jnp.bfloat16),
        compiler_params=params(),
        cost_estimate=cost(5 << 20, 2 << 20),
        name="second_sum",
    )(*kept, *messages)


def last_sum_kernel(row_total, own_ref, rp_ref, cp_ref, m1, m2, m3, z, out_ref):
    tiles, rows, columns = add_messages(own_ref, rp_ref, cp_ref, (m1, m2, m3, z))

    def back(power):
        return jnp.where(power > 0, lax.rsqrt(power + np.float32(EPS * row_total)), 0.0)

    row_back, column_back = column(back(rows)), back(columns)
    for t, tile in enumerate(tiles):
        cols = slice(t * 128, t * 128 + 128)
        out_ref[:, cols] = tile * (row_back * column_back[:, cols])


def last_sum(row_total, kept, messages):
    return pl.pallas_call(
        functools.partial(last_sum_kernel, row_total),
        in_specs=[FULL] * 7,
        out_specs=FULL,
        out_shape=jax.ShapeDtypeStruct(kept[0].shape, jnp.float32),
        compiler_params=params(),
        cost_estimate=cost(5 << 20, 2 << 20),
        name="last_sum",
    )(*kept, *messages)


def shards(dino_acts, siglip_acts, dino_encoder, siglip_encoder, dino_threshold, siglip_threshold):
    z_hi = lax.axis_index("mp")
    patch = lax.axis_index("patch")
    latent = lax.axis_index("latent")
    x, y = patch // 4, patch % 4
    z_lo, core = latent // 2, latent % 2
    first = (x + 2 * y) % 4
    at = jnp.stack([
        first, core, jnp.where(core == 0, x, y), jnp.where(core == 0, y, x),
        (z_hi == z_lo).astype(jnp.int32)]).astype(jnp.int32)
    row_total = dino_acts.shape[0] * dino_acts.shape[1] * lax.axis_size(AXES)
    latents = dino_encoder.shape[1]

    thresholds = jnp.concatenate([
        jnp.broadcast_to(dino_threshold[None, :], (16, latents)),
        jnp.broadcast_to(siglip_threshold[None, :], (16, latents))])

    theta = (thresholds, to_sibling(thresholds))
    d_own = dino_acts.reshape(-1, dino_acts.shape[-1])
    dino_sibling = to_sibling(dino_encoder)
    siglip_sibling = to_sibling(siglip_encoder)

    piece = along_z(jnp.concatenate([
        lax.dynamic_slice_in_dim(siglip_encoder, first * PIECE, PIECE, 1),
        lax.dynamic_slice_in_dim(thresholds[16:], first * PIECE, PIECE, 1)]))
    s_own = resample_local(siglip_acts).reshape(-1, siglip_acts.shape[-1])
    s_ext = along_z(s_own)

    def dino_codes(xs):
        away = encode(xs, dino_sibling, theta[1], 0, "dino_codes")
        return encode(xs, dino_encoder, theta[0], 0, "dino_codes"), away

    d_near, d_near_away = dino_codes([d_own])
    piece, s_own, d_own, siglip_sibling, d_near, d_near_away = lax.optimization_barrier(
        (piece, s_own, d_own, siglip_sibling, d_near, d_near_away))
    d_ext = along_z(d_own)
    pieces = [
        piece,
        send(piece, lambda c: (-1, 0, 0, 0)),
        send(piece, lambda c: (0, 1, 0, 0)),
        send(piece, lambda c: (1, 0, 0, 0)),
    ]

    def siglip_codes(xs, weights, thresholds, row):
        return encode(xs, weights, thresholds, row, "siglip_codes")

    xs = [s_own, s_ext]
    one = [siglip_codes(xs, siglip_encoder, theta[0], 16), siglip_codes(xs, siglip_sibling, theta[1], 16)]
    *one, p0, p1, p2, p3 = lax.optimization_barrier((*one, *pieces))
    pieces = [p0, p1, p2, p3]
    pieces_sibling = [to_sibling(p) for p in pieces]
    two = [encode_pieces(at, xs, pieces, "siglip_codes")]
    d_ext, two[0] = lax.optimization_barrier((d_ext, two[0]))
    two.append(encode_pieces(at, xs, pieces_sibling, "siglip_codes"))
    d_far, d_far_away = dino_codes([d_ext])

    sets = [[*pair, to_sibling(pair[0]), to_sibling(pair[1])] for pair in (one, two)]
    ds = (d_near, d_far, to_sibling(d_near_away), to_sibling(d_far_away))

    ss = sets[0] + sets[1]
    d_power = None
    relays, arrived = [], []
    for turn in range(2):
        low, high, *powers = products([(2, turn)], at, ss, ds, d_power)
        d_power = powers[0] if powers else d_power
        relays.append((first_way(low, 1), first_way(high, 3)))
    for turn, pair in enumerate(relays):
        part_one, part_three = products([(1, turn), (3, turn)], at, ss, ds, d_power, relays=pair)
        arrived.append((first_way(part_one, 1), first_way(part_three, 3)))
    own = products([(0, 0), (0, 1)], at, ss, ds, d_power, after=part_three)

    results = []
    for turn, pair in enumerate(arrived):
        sums = first_sum(at, *own[2 * turn:2 * turn + 2], d_power, pair)
        results.append((sums[3:], [second_way(sums[m - 1], m) for m in (1, 2, 3)]))
    message = send(second_sum(*results[0]), lambda c: (0, 0, 2, 0))
    kept, messages = results[1]
    return last_sum(row_total, kept, [*messages, message])


def solution(mesh):
    in_specs = (
        P(("mp", "patch", "latent"), None, None),
        P(("mp", "patch", "latent"), None, None),
        P(None, "latent"),
        P(None, "latent"),
        P("latent"),
        P("latent"),
    )
    out_specs = P(("mp", "patch"), "latent")
    return jax.shard_map(shards, mesh=mesh, in_specs=in_specs, out_specs=out_specs, check_vma=False)
```

```python
import functools

import jax
import jax.numpy as jnp
import numpy as np
from jax import lax
from jax.experimental import pallas as pl
from jax.experimental.pallas import tpu as pltpu
from jax.sharding import PartitionSpec as P

GRID = 16
SIG_SIDE = 27
EPS = 1e-06
AXES = ("mp", "patch", "latent")
VMEM = 16 * 1024 * 1024
TOP = np.float32(np.sqrt(2.0**15))
ANY = pl.BlockSpec(memory_space=pl.ANY)
HBM = pl.BlockSpec(memory_space=pltpu.HBM)
SMEM = pl.BlockSpec(memory_space=pltpu.SMEM)
FULL = pl.BlockSpec(memory_space=pltpu.VMEM)
PIECE = 256


def resample_table(side_cells, grid_cells):
    weights_table = np.zeros((grid_cells, side_cells), np.float32)
    for target in range(grid_cells):
        source = (target + 0.5) * side_cells / grid_cells - 0.5
        low_index = int(np.floor(source))
        upper_part = source - low_index
        weights_table[target, low_index] += 1.0 - upper_part
        weights_table[target, min(low_index + 1, side_cells - 1)] += upper_part
    return weights_table


def resample_local(raw_block):
    table = resample_table(SIG_SIDE, GRID)
    table = np.kron(table, table).astype(np.float32)
    high = table.astype(jnp.bfloat16)
    low = (table - high.astype(np.float32)).astype(jnp.bfloat16)
    images = raw_block.shape[0]

    def part(matrix):
        return lax.dot_general(
            jnp.broadcast_to(jnp.asarray(matrix), (images,) + matrix.shape), raw_block,
            (((2,), (1,)), ((0,), (0,))), preferred_element_type=jnp.float32)

    return (part(high) + part(low)).astype(jnp.bfloat16)


def place(x, y, z, core):
    return (z // 2) * 64 + (x * 4 + y) * 4 + (z % 2) * 2 + core


def moves(step):
    out = []
    for x in range(4):
        for y in range(4):
            for z in range(4):
                for c in range(2):
                    dx, dy, dz, swap = step(c)
                    target = place((x + dx) % 4, (y + dy) % 4, (z + dz) % 4, c ^ swap)
                    out.append((place(x, y, z, c), target))
    return out


def send(value, step):
    return lax.ppermute(value, AXES, moves(step))


def to_sibling(value):
    return send(value, lambda c: (0, 0, 0, 1))


def along_z(value):
    return send(value, lambda c: (0, 0, -1 if c else 1, 0))


def first_way(value, m):
    return send(value, lambda c: (0, m, 0, 0) if c else (m, 0, 0, 0))


def second_way(value, m):
    return send(value, lambda c: (m, 0, 0, 0) if c else (0, m, 0, 0))


def params():
    return pltpu.CompilerParams(vmem_limit_bytes=VMEM)


def cost(flops, size):
    return pl.CostEstimate(flops=flops, bytes_accessed=size, transcendentals=0)


def encode_kernel(chunks, theta_row, *refs):
    xs, (w_ref, t_ref, out, o_buf, o_sem) = refs[:chunks], refs[chunks:]
    depth = xs[0].shape[1]
    theta = t_ref[theta_row:theta_row + 16, :].astype(jnp.float32)[:1, :]
    copies = []
    row = 0
    for k in range(chunks):
        rows = xs[k].shape[0]
        here = pl.ds(row, rows)
        pre = jnp.dot(xs[k][...], w_ref[0:depth, :], preferred_element_type=jnp.float32)
        o_buf[here, :] = jnp.maximum(pre - theta, 0.0).astype(jnp.bfloat16)
        copies.append(pltpu.make_async_copy(o_buf.at[here, :], out.at[here, :], o_sem.at[k]))
        copies[k].start()
        row += rows
    for copy in copies:
        copy.wait()


def encode(xs, weights, thresholds, theta_row, name):
    rows = sum(x.shape[0] for x in xs)
    depth = xs[0].shape[1]
    width = weights.shape[1]
    return pl.pallas_call(
        functools.partial(encode_kernel, len(xs), theta_row),
        in_specs=[FULL] * (len(xs) + 2),
        out_specs=HBM,
        out_shape=jax.ShapeDtypeStruct((rows, width), jnp.bfloat16),
        scratch_shapes=[
            pltpu.VMEM((rows, width), jnp.bfloat16),
            pltpu.SemaphoreType.DMA((len(xs),)),
        ],
        compiler_params=params(),
        cost_estimate=cost(2 * rows * depth * width // 32, 0),
        name=name,
    )(*xs, weights, thresholds)


def encode_both_kernel(chunks, theta_row, *refs):
    xs, refs = refs[:chunks], refs[chunks:]
    w_ref, v_ref, t_ref, u_ref, out_a, out_b, v_buf, o_buf, v_sem, o_sem = refs
    v_copy = pltpu.make_async_copy(v_ref, v_buf, v_sem)
    v_copy.start()
    copies = []
    for j, (weights, thresholds, out) in enumerate(((w_ref, t_ref, out_a), (v_buf, u_ref, out_b))):
        if j:
            v_copy.wait()
        theta = thresholds[theta_row:theta_row + 16, :].astype(jnp.float32)[:1, :]
        row = 0
        for k in range(chunks):
            rows = xs[k].shape[0]
            here = pl.ds(row, rows)
            pre = jnp.dot(xs[k][...], weights[...], preferred_element_type=jnp.float32)
            o_buf[j, here, :] = jnp.maximum(pre - theta, 0.0).astype(jnp.bfloat16)
            copy = pltpu.make_async_copy(o_buf.at[j, here, :], out.at[here, :], o_sem.at[j, k])
            copy.start()
            copies.append(copy)
            row += rows
    for copy in copies:
        copy.wait()


def encode_both(xs, weights, thresholds, theta_row, name):
    rows = sum(x.shape[0] for x in xs)
    depth, width = weights[0].shape
    return pl.pallas_call(
        functools.partial(encode_both_kernel, len(xs), theta_row),
        in_specs=[FULL] * (len(xs) + 1) + [HBM] + [FULL] * 2,
        out_specs=[HBM] * 2,
        out_shape=[jax.ShapeDtypeStruct((rows, width), jnp.bfloat16)] * 2,
        scratch_shapes=[
            pltpu.VMEM((depth, width), jnp.bfloat16),
            pltpu.VMEM((2, rows, width), jnp.bfloat16),
            pltpu.SemaphoreType.DMA,
            pltpu.SemaphoreType.DMA((2, len(xs))),
        ],
        compiler_params=params(),
        cost_estimate=cost(4 * rows * depth * width // 32, 0),
        name=name,
    )(*xs, *weights, *thresholds)


def encode_pieces_kernel(chunks, at_ref, *refs):
    xs, ws, (out, w_buf, o_buf, w_sem, o_sem) = refs[:chunks], refs[chunks:chunks + 4], refs[chunks + 4:]
    depth = xs[0].shape[1]
    w_copies = [pltpu.make_async_copy(ws[k], w_buf.at[:, pl.ds(k * PIECE, PIECE)], w_sem.at[k]) for k in range(4)]
    for copy in w_copies:
        copy.start()
    copies = []
    for pair in range(2):
        for copy in w_copies[2 * pair:2 * pair + 2]:
            copy.wait()
        here = slice(2 * pair * PIECE, 2 * (pair + 1) * PIECE)
        theta = w_buf[depth:depth + 16, here].astype(jnp.float32)[:1, :]
        row = 0
        for k in range(chunks):
            rows = xs[k].shape[0]
            pre = jnp.dot(xs[k][...], w_buf[0:depth, here], preferred_element_type=jnp.float32)
            o_buf[row:row + rows, here] = jnp.maximum(pre - theta, 0.0).astype(jnp.bfloat16)
            row += rows
        for step in (2 * pair, 2 * pair + 1):
            col = pl.multiple_of(lax.rem(at_ref[0] + step, 4) * PIECE, PIECE)
            copies.append(pltpu.make_async_copy(
                o_buf.at[:, pl.ds(step * PIECE, PIECE)], out.at[:, pl.ds(col, PIECE)], o_sem.at[step]))
            copies[step].start()
    for copy in copies:
        copy.wait()


def encode_pieces(at, xs, pieces, name):
    rows = sum(x.shape[0] for x in xs)
    depth = xs[0].shape[1]
    return pl.pallas_call(
        functools.partial(encode_pieces_kernel, len(xs)),
        in_specs=[SMEM] + [FULL] * len(xs) + [ANY] * 4,
        out_specs=HBM,
        out_shape=jax.ShapeDtypeStruct((rows, 4 * PIECE), jnp.bfloat16),
        scratch_shapes=[
            pltpu.VMEM((pieces[0].shape[0], 4 * PIECE), jnp.bfloat16),
            pltpu.VMEM((rows, 4 * PIECE), jnp.bfloat16),
            pltpu.SemaphoreType.DMA((4,)),
            pltpu.SemaphoreType.DMA((4,)),
        ],
        compiler_params=params(),
        cost_estimate=cost(8 * rows * depth * PIECE // 32, 0),
        name=name,
    )(at, *xs, *pieces)


def squeeze(value):
    value = value * value
    value = value * value
    return (value * value).astype(jnp.bfloat16)


def widen(value):
    return jnp.exp2(jnp.log2(value.astype(jnp.float32)) * 0.125)


def gain(power):
    return jnp.where(power > 0, lax.rsqrt(jnp.maximum(power, 1e-37)) * TOP, 0.0)


def root(power):
    return jnp.sqrt(power) * np.float32(1 / TOP)


def column(row):
    return jnp.broadcast_to(row, (128, row.shape[1])).T


def pack(row_power, column_power):
    width = column_power.shape[1]
    if row_power.shape[1] < width:
        row_power = jnp.concatenate(
            [row_power, jnp.zeros((1, width - row_power.shape[1]), jnp.float32)], axis=1)
    at = lax.broadcasted_iota(jnp.int32, (16, width), 0)
    out = jnp.zeros((16, width), jnp.float32)
    for base, power in ((0, column_power), (3, row_power)):
        rest = power
        for part in range(3):
            piece = rest.astype(jnp.bfloat16).astype(jnp.float32)
            out = jnp.where(at == base + part, piece, out)
            rest = rest - piece
    return out.astype(jnp.bfloat16)


def unpack(tail, rows):
    tail = tail.astype(jnp.float32)
    column_power = tail[0:1, :] + tail[1:2, :] + tail[2:3, :]
    row_power = tail[3:4, :rows] + tail[4:5, :rows] + tail[5:6, :rows]
    return row_power, column_power


def square_sum(ref, cols):
    total = None
    for at in range(0, ref.shape[0], 256):
        wide = ref[at:at + 256, cols].astype(jnp.float32)
        part = jnp.sum((wide * wide).reshape(32, 8, -1), axis=0)
        total = part if total is None else total + part
    return jnp.sum(total, axis=0, keepdims=True)


def products_kernel(jobs, leads, at_ref, *refs):
    ss, ds, refs = refs[:8], refs[8:12], list(refs[12:])
    dp_ref = None if leads else refs.pop(0)
    relays = [refs.pop(0) if m in (1, 3) else None for m, _ in jobs]
    if jobs[0][0] == 0:
        refs.pop(0)
    outs = [[refs.pop(0) for _ in range(1 if m in (1, 3) else 2)] for m, _ in jobs]
    if leads:
        dp_ref = refs.pop(0)
    s_bufs, r_bufs, o_bufs, s_sem, r_sem, o_sem = refs
    rows, width = ds[0].shape
    tile = width // 2
    core = at_ref[1]
    s_copies, r_copies, copies = [], [], []
    for j, (m, turn) in enumerate(jobs):
        target = lax.rem(at_ref[2] + m, 4)
        s_copies.append([])
        for k in range(2):
            for b in range(4):
                block = jnp.where(core == 0, target * 4 + b, b * 4 + target)
                mine = block // 8 == core
                col = pl.ds(pl.multiple_of(lax.rem(block, 8) * 128, 128), 128)
                for which in range(2):
                    chosen = at_ref[4] == (which if turn == 0 else 1 - which)
                    choices = [pltpu.make_async_copy(
                        ss[which * 4 + k * 2 + choice].at[:, col],
                        s_bufs.at[j, pl.ds(k * 2 * rows, 2 * rows), pl.ds(b * 128, 128)],
                        s_sem.at[j, k * 4 + b]) for choice in range(2)]
                    pl.when(chosen & mine)(choices[k].start)
                    pl.when(chosen & jnp.logical_not(mine))(choices[1 - k].start)
                s_copies[j].append(choices[k])
        r_copies.append(None)
        if m in (1, 3):
            r_copies[j] = pltpu.make_async_copy(relays[j], r_bufs.at[j], r_sem.at[j])
            r_copies[j].start()
    if leads:
        for t in range(2):
            cols = slice(t * tile, t * tile + tile)
            dp_ref[:, cols] = jnp.broadcast_to(sum(square_sum(d, cols) for d in ds), (8, tile))

    def job(j, m):
        s_buf, r_buf, o_buf, out = s_bufs.at[j], r_bufs.at[j], o_bufs.at[j], outs[j]
        relayed = {1: 0, 3: 1}.get(m)
        column_powers = [dp_ref[0:1, 0:tile], dp_ref[0:1, tile:width]]

        def dots(t, ks):
            return sum(
                lax.dot_general(s_buf[k * rows:k * rows + rows, :], ds[k][:, t * tile:t * tile + tile],
                                (((0,), (0,)), ((), ())), preferred_element_type=jnp.float32) for k in ks)

        for copy in s_copies[j][:4]:
            copy.wait()
        near = dots(0, (0, 1))
        for copy in s_copies[j][4:]:
            copy.wait()
        s_power = square_sum(s_buf, slice(None))
        row_powers = [s_power, s_power]
        if relayed is not None:
            r_copies[j].wait()
            r_rows, r_columns = unpack(r_buf[512:528, :], 512)
            row_powers[relayed] = s_power + r_rows
            column_powers[relayed] = column_powers[relayed] + r_columns
            r_scale = jnp.concatenate([column(root(r_rows))] * (tile // 128), axis=1) * root(r_columns)
        for t in range(2):
            cols = slice(t * tile, t * tile + tile)
            total = near + dots(0, (2, 3)) if t == 0 else dots(1, (0, 1, 2, 3))
            if t == relayed:
                total = total + widen(r_buf[0:512, :]) * r_scale
            if not m:
                out[0][:, cols] = total
                continue
            if t == 0 or relayed is not None:
                row_gain = jnp.concatenate([column(gain(row_powers[t]))] * (tile // 128), axis=1)
            o_buf[0:512, cols] = squeeze(total * row_gain * gain(column_powers[t]))
            o_buf[512:528, cols] = pack(row_powers[t], column_powers[t])
            target_ref = out[t] if m == 2 else out[0].at[:, pl.ds(t * tile, tile)]
            copy = pltpu.make_async_copy(o_buf.at[:, pl.ds(t * tile, tile)], target_ref, o_sem.at[j, t])
            copy.start()
            copies.append(copy)
        if not m:
            out[1][...] = jnp.broadcast_to(s_power, out[1].shape)

    for j, (m, _) in enumerate(jobs):
        job(j, m)
    for copy in copies:
        copy.wait()


def products(jobs, at, ss, ds, d_power=None, relays=(), after=None):
    rows, width = ds[0].shape
    f32 = jnp.float32
    leads = d_power is None
    count = len(jobs)
    shapes, specs = [], []
    for m, _ in jobs:
        if m == 2:
            shapes += [jax.ShapeDtypeStruct((528, width // 2), jnp.bfloat16)] * 2
            specs += [HBM] * 2
        elif m:
            shapes += [jax.ShapeDtypeStruct((528, width), jnp.bfloat16)]
            specs += [HBM]
        else:
            shapes += [jax.ShapeDtypeStruct(s, f32) for s in ((512, width), (8, 512))]
            specs += [FULL] * 2
    operands = [at, *ss, *ds]
    if leads:
        shapes, specs = shapes + [jax.ShapeDtypeStruct((8, width), f32)], specs + [FULL]
    else:
        operands.append(d_power)
    in_specs = [SMEM] + [HBM] * 8 + [FULL] * (len(operands) - 9)
    extra = [*relays] if after is None else [after]
    return pl.pallas_call(
        functools.partial(products_kernel, jobs, leads),
        in_specs=in_specs + [HBM] * len(extra),
        out_specs=specs,
        out_shape=shapes,
        scratch_shapes=[
            pltpu.VMEM((count, 4 * rows, 512), jnp.bfloat16),
            pltpu.VMEM((count, 528, width // 2), jnp.bfloat16),
            pltpu.VMEM((count, 528, width), jnp.bfloat16),
            pltpu.SemaphoreType.DMA((count, 8)),
            pltpu.SemaphoreType.DMA((count,)),
            pltpu.SemaphoreType.DMA((count, 2)),
        ],
        compiler_params=params(),
        cost_estimate=cost(2 * 512 * 4 * rows * width * count, 5 << 20),
        name="products",
    )(*operands, *extra)


ORDER = (2, 1, 3, 0)


def first_sum_kernel(at_ref, own_ref, sp_ref, dp_ref, *refs):
    messages, (o1, o2, o3, keep_ref, keep_rp_ref, keep_cp_ref), scratch = refs[:2], refs[2:8], refs[8:]
    m_buf, o_buf, scale_ref, power_ref, m_sem, o_sem = scratch
    width = own_ref.shape[1]
    tails, blocks = [], []
    for k, message in enumerate(messages):
        rows = pl.ds(512, 16)
        tails.append(pltpu.make_async_copy(message.at[rows, :], m_buf.at[k, rows, :], m_sem.at[4, k]))
    for i, m in enumerate(ORDER):
        rows = pl.ds(pl.multiple_of(lax.rem(at_ref[3] + m, 4) * 128, 128), 128)
        blocks.append((rows, [
            pltpu.make_async_copy(message.at[rows, :], m_buf.at[k, rows, :], m_sem.at[i, k])
            for k, message in enumerate(messages)]))
    for copies in [tails] + [copies for _, copies in blocks]:
        for copy in copies:
            copy.start()
    for copy in tails:
        copy.wait()

    row_total, column_total = sp_ref[0:1, :], dp_ref[0:1, :]
    column_roots = []
    half = width // 2
    for k in range(2):
        parts = [unpack(m_buf[k, 512:528, h * half:h * half + half], 512) for h in range(2)]
        for h in range(2):
            scale_ref[2 * k + h] = column(root(parts[h][0]))
        column_power = jnp.concatenate([part[1] for part in parts], axis=1)
        column_roots.append(root(column_power))
        row_total = row_total + parts[0][0]
        column_total = column_total + column_power
    scale_ref[4] = column(gain(row_total))
    column_gain = gain(column_total)
    power_ref[...] = jnp.broadcast_to(row_total, power_ref.shape)
    keep_cp_ref[...] = jnp.broadcast_to(column_total, keep_cp_ref.shape)

    out_copies = []
    for i, m in enumerate(ORDER):
        here, copies = blocks[i]
        for copy in copies:
            copy.wait()
        scales = [scale_ref[k, here, :] for k in range(5)]
        for at in range(0, width, 128):
            cols = slice(at, at + 128)
            total = own_ref[here, cols]
            for k in range(2):
                total = total + widen(m_buf[k, here, cols]) * (
                    scales[2 * k + at // half] * column_roots[k][:, cols])
            if m:
                o_buf[i, 0:128, cols] = squeeze(total * (scales[4] * column_gain[:, cols]))
            else:
                keep_ref[:, cols] = total
        powers = power_ref[:, here]
        if m:
            o_buf[i, 128:144, :] = pack(powers[0:1, :], column_total)
            out_copies.append(pltpu.make_async_copy(o_buf.at[i], (o1, o2, o3)[m - 1], o_sem.at[i]))
            out_copies[i].start()
        else:
            keep_rp_ref[...] = powers
    for copy in out_copies:
        copy.wait()


def first_sum(at, own, row_power, column_power, messages):
    width = own.shape[1]
    shapes = [jax.ShapeDtypeStruct((144, width), jnp.bfloat16)] * 3 + [
        jax.ShapeDtypeStruct(s, jnp.float32) for s in ((128, width), (8, 128), (8, width))]
    return pl.pallas_call(
        first_sum_kernel,
        in_specs=[SMEM] + [FULL] * 3 + [HBM] * 2,
        out_specs=[HBM] * 3 + [FULL] * 3,
        out_shape=shapes,
        scratch_shapes=[
            pltpu.VMEM((2, 528, width), jnp.bfloat16),
            pltpu.VMEM((3, 144, width), jnp.bfloat16),
            pltpu.VMEM((5, 512, 128), jnp.float32),
            pltpu.VMEM((8, 512), jnp.float32),
            pltpu.SemaphoreType.DMA((5, 2)),
            pltpu.SemaphoreType.DMA((3,)),
        ],
        compiler_params=params(),
        cost_estimate=cost(10 << 20, 3 << 20),
        name="first_sum",
    )(at, own, row_power, column_power, *messages)


def add_messages(own_ref, rp_ref, cp_ref, messages):
    rows, width = own_ref.shape
    row_total, column_total = rp_ref[0:1, :], cp_ref[0:1, :]
    scales = []
    for message in messages:
        row_power, column_power = unpack(message[rows:rows + 16, :], rows)
        scales.append((column(root(row_power)), root(column_power)))
        row_total = row_total + row_power
        column_total = column_total + column_power
    tiles = []
    for at in range(0, width, 128):
        cols = slice(at, at + 128)
        total = own_ref[:, cols]
        for message, (row_scale, column_scale) in zip(messages, scales):
            total = total + widen(message[0:rows, cols]) * (row_scale * column_scale[:, cols])
        tiles.append(total)
    return tiles, row_total, column_total


def second_sum_kernel(own_ref, rp_ref, cp_ref, m1, m2, m3, z_ref):
    tiles, rows, columns = add_messages(own_ref, rp_ref, cp_ref, (m1, m2, m3))
    row_gain, column_gain = column(gain(rows)), gain(columns)
    for t, tile in enumerate(tiles):
        cols = slice(t * 128, t * 128 + 128)
        z_ref[0:128, cols] = squeeze(tile * (row_gain * column_gain[:, cols]))
    z_ref[128:144, :] = pack(rows, columns)


def second_sum(kept, messages):
    return pl.pallas_call(
        second_sum_kernel,
        in_specs=[FULL] * 6,
        out_specs=FULL,
        out_shape=jax.ShapeDtypeStruct((144, kept[0].shape[1]), jnp.bfloat16),
        compiler_params=params(),
        cost_estimate=cost(5 << 20, 2 << 20),
        name="second_sum",
    )(*kept, *messages)


def last_sum_kernel(row_total, own_ref, rp_ref, cp_ref, m1, m2, m3, z, out_ref):
    tiles, rows, columns = add_messages(own_ref, rp_ref, cp_ref, (m1, m2, m3, z))

    def back(power):
        return jnp.where(power > 0, lax.rsqrt(power + np.float32(EPS * row_total)), 0.0)

    row_back, column_back = column(back(rows)), back(columns)
    for t, tile in enumerate(tiles):
        cols = slice(t * 128, t * 128 + 128)
        out_ref[:, cols] = tile * (row_back * column_back[:, cols])


def last_sum(row_total, kept, messages):
    return pl.pallas_call(
        functools.partial(last_sum_kernel, row_total),
        in_specs=[FULL] * 7,
        out_specs=FULL,
        out_shape=jax.ShapeDtypeStruct(kept[0].shape, jnp.float32),
        compiler_params=params(),
        cost_estimate=cost(5 << 20, 2 << 20),
        name="last_sum",
    )(*kept, *messages)


def shards(dino_acts, siglip_acts, dino_encoder, siglip_encoder, dino_threshold, siglip_threshold):
    z_hi = lax.axis_index("mp")
    patch = lax.axis_index("patch")
    latent = lax.axis_index("latent")
    x, y = patch // 4, patch % 4
    z_lo, core = latent // 2, latent % 2
    first = (x + 2 * y) % 4
    at = jnp.stack([
        first, core, jnp.where(core == 0, x, y), jnp.where(core == 0, y, x),
        (z_hi == z_lo).astype(jnp.int32)]).astype(jnp.int32)
    row_total = dino_acts.shape[0] * dino_acts.shape[1] * lax.axis_size(AXES)
    latents = dino_encoder.shape[1]

    thresholds = jnp.concatenate([
        jnp.broadcast_to(dino_threshold[None, :], (16, latents)),
        jnp.broadcast_to(siglip_threshold[None, :], (16, latents))])

    theta = (thresholds, to_sibling(thresholds))
    d_own = dino_acts.reshape(-1, dino_acts.shape[-1])
    dino_sibling = to_sibling(dino_encoder)
    siglip_sibling = to_sibling(siglip_encoder)

    piece = along_z(jnp.concatenate([
        lax.dynamic_slice_in_dim(siglip_encoder, first * PIECE, PIECE, 1),
        lax.dynamic_slice_in_dim(thresholds[16:], first * PIECE, PIECE, 1)]))
    s_own = resample_local(siglip_acts).reshape(-1, siglip_acts.shape[-1])
    s_ext = along_z(s_own)

    def dino_codes(xs):
        away = encode(xs, dino_sibling, theta[1], 0, "dino_codes")
        return encode(xs, dino_encoder, theta[0], 0, "dino_codes"), away

    piece, s_own, d_own, siglip_sibling, dino_sibling, theta_sibling = lax.optimization_barrier(
        (piece, s_own, d_own, siglip_sibling, dino_sibling, theta[1]))
    theta = (thresholds, theta_sibling)
    d_ext = along_z(d_own)
    pieces = [
        piece,
        send(piece, lambda c: (-1, 0, 0, 0)),
        send(piece, lambda c: (0, 1, 0, 0)),
        send(piece, lambda c: (1, 0, 0, 0)),
    ]

    d_near, d_near_away = encode_both([d_own], (dino_encoder, dino_sibling), theta, 0, "dino_codes")
    s_own, s_ext, d_near, d_near_away = lax.optimization_barrier((s_own, s_ext, d_near, d_near_away))
    xs = [s_own, s_ext]
    one = encode_both(xs, (siglip_encoder, siglip_sibling), theta, 16, "siglip_codes")
    *one, p0, p1, p2, p3 = lax.optimization_barrier((*one, *pieces))
    pieces = [p0, p1, p2, p3]
    pieces_sibling = [to_sibling(p) for p in pieces]
    two = [encode_pieces(at, xs, pieces, "siglip_codes")]
    d_ext, two[0] = lax.optimization_barrier((d_ext, two[0]))
    two.append(encode_pieces(at, xs, pieces_sibling, "siglip_codes"))
    d_far, d_far_away = dino_codes([d_ext])

    sets = [[*pair, to_sibling(pair[0]), to_sibling(pair[1])] for pair in (one, two)]
    ds = (d_near, d_far, to_sibling(d_near_away), to_sibling(d_far_away))

    ss = sets[0] + sets[1]
    d_power = None
    relays, arrived = [], []
    for turn in range(2):
        low, high, *powers = products([(2, turn)], at, ss, ds, d_power)
        d_power = powers[0] if powers else d_power
        relays.append((first_way(low, 1), first_way(high, 3)))
    for turn, pair in enumerate(relays):
        part_one, part_three = products([(1, turn), (3, turn)], at, ss, ds, d_power, relays=pair)
        arrived.append((first_way(part_one, 1), first_way(part_three, 3)))
    own = products([(0, 0), (0, 1)], at, ss, ds, d_power, after=part_three)

    results = []
    for turn, pair in enumerate(arrived):
        sums = first_sum(at, *own[2 * turn:2 * turn + 2], d_power, pair)
        results.append((sums[3:], [second_way(sums[m - 1], m) for m in (1, 2, 3)]))
    message = send(second_sum(*results[0]), lambda c: (0, 0, 2, 0))
    kept, messages = results[1]
    return last_sum(row_total, kept, [*messages, message])


def solution(mesh):
    in_specs = (
        P(("mp", "patch", "latent"), None, None),
        P(("mp", "patch", "latent"), None, None),
        P(None, "latent"),
        P(None, "latent"),
        P("latent"),
        P("latent"),
    )
    out_specs = P(("mp", "patch"), "latent")
    return jax.shard_map(shards, mesh=mesh, in_specs=in_specs, out_specs=out_specs, check_vma=False)
```

```python
import functools

import jax
import jax.numpy as jnp
import numpy as np
from jax import lax
from jax.experimental import pallas as pl
from jax.experimental.pallas import tpu as pltpu
from jax.sharding import PartitionSpec as P

GRID = 16
SIG_SIDE = 27
EPS = 1e-06
AXES = ("mp", "patch", "latent")
VMEM = 16 * 1024 * 1024
TOP = np.float32(np.sqrt(2.0**15))
ANY = pl.BlockSpec(memory_space=pl.ANY)
HBM = pl.BlockSpec(memory_space=pltpu.HBM)
SMEM = pl.BlockSpec(memory_space=pltpu.SMEM)
FULL = pl.BlockSpec(memory_space=pltpu.VMEM)
PIECE = 256


def resample_table(side_cells, grid_cells):
    weights_table = np.zeros((grid_cells, side_cells), np.float32)
    for target in range(grid_cells):
        source = (target + 0.5) * side_cells / grid_cells - 0.5
        low_index = int(np.floor(source))
        upper_part = source - low_index
        weights_table[target, low_index] += 1.0 - upper_part
        weights_table[target, min(low_index + 1, side_cells - 1)] += upper_part
    return weights_table


def resample_local(raw_block):
    table = resample_table(SIG_SIDE, GRID)
    table = np.kron(table, table).astype(np.float32)
    high = table.astype(jnp.bfloat16)
    low = (table - high.astype(np.float32)).astype(jnp.bfloat16)
    images = raw_block.shape[0]

    def part(matrix):
        return lax.dot_general(
            jnp.broadcast_to(jnp.asarray(matrix), (images,) + matrix.shape), raw_block,
            (((2,), (1,)), ((0,), (0,))), preferred_element_type=jnp.float32)

    return (part(high) + part(low)).astype(jnp.bfloat16)


def place(x, y, z, core):
    return (z // 2) * 64 + (x * 4 + y) * 4 + (z % 2) * 2 + core


def moves(step):
    out = []
    for x in range(4):
        for y in range(4):
            for z in range(4):
                for c in range(2):
                    dx, dy, dz, swap = step(c)
                    target = place((x + dx) % 4, (y + dy) % 4, (z + dz) % 4, c ^ swap)
                    out.append((place(x, y, z, c), target))
    return out


def send(value, step):
    return lax.ppermute(value, AXES, moves(step))


def to_sibling(value):
    return send(value, lambda c: (0, 0, 0, 1))


def along_z(value):
    return send(value, lambda c: (0, 0, -1 if c else 1, 0))


def first_way(value, m):
    return send(value, lambda c: (0, m, 0, 0) if c else (m, 0, 0, 0))


def second_way(value, m):
    return send(value, lambda c: (m, 0, 0, 0) if c else (0, m, 0, 0))


def params():
    return pltpu.CompilerParams(vmem_limit_bytes=VMEM)


def cost(flops, size):
    return pl.CostEstimate(flops=flops, bytes_accessed=size, transcendentals=0)


def encode_kernel(chunks, theta_row, *refs):
    xs, (w_ref, t_ref, out, o_buf, o_sem) = refs[:chunks], refs[chunks:]
    depth = xs[0].shape[1]
    theta = t_ref[theta_row:theta_row + 16, :].astype(jnp.float32)[:1, :]
    copies = []
    row = 0
    for k in range(chunks):
        rows = xs[k].shape[0]
        here = pl.ds(row, rows)
        pre = jnp.dot(xs[k][...], w_ref[0:depth, :], preferred_element_type=jnp.float32)
        o_buf[here, :] = jnp.maximum(pre - theta, 0.0).astype(jnp.bfloat16)
        copies.append(pltpu.make_async_copy(o_buf.at[here, :], out.at[here, :], o_sem.at[k]))
        copies[k].start()
        row += rows
    for copy in copies:
        copy.wait()


def encode(xs, weights, thresholds, theta_row, name):
    rows = sum(x.shape[0] for x in xs)
    depth = xs[0].shape[1]
    width = weights.shape[1]
    return pl.pallas_call(
        functools.partial(encode_kernel, len(xs), theta_row),
        in_specs=[FULL] * (len(xs) + 2),
        out_specs=HBM,
        out_shape=jax.ShapeDtypeStruct((rows, width), jnp.bfloat16),
        scratch_shapes=[
            pltpu.VMEM((rows, width), jnp.bfloat16),
            pltpu.SemaphoreType.DMA((len(xs),)),
        ],
        compiler_params=params(),
        cost_estimate=cost(2 * rows * depth * width // 32, 0),
        name=name,
    )(*xs, weights, thresholds)


def encode_both_kernel(chunks, theta_row, *refs):
    xs, refs = refs[:chunks], refs[chunks:]
    w_ref, v_ref, t_ref, u_ref, out_a, out_b, v_buf, o_buf, v_sem, o_sem = refs
    v_copy = pltpu.make_async_copy(v_ref, v_buf, v_sem)
    v_copy.start()
    copies = []
    for j, (weights, thresholds, out) in enumerate(((w_ref, t_ref, out_a), (v_buf, u_ref, out_b))):
        if j:
            v_copy.wait()
        theta = thresholds[theta_row:theta_row + 16, :].astype(jnp.float32)[:1, :]
        row = 0
        for k in range(chunks):
            rows = xs[k].shape[0]
            here = pl.ds(row, rows)
            pre = jnp.dot(xs[k][...], weights[...], preferred_element_type=jnp.float32)
            o_buf[j, here, :] = jnp.maximum(pre - theta, 0.0).astype(jnp.bfloat16)
            copy = pltpu.make_async_copy(o_buf.at[j, here, :], out.at[here, :], o_sem.at[j, k])
            copy.start()
            copies.append(copy)
            row += rows
    for copy in copies:
        copy.wait()


def encode_both(xs, weights, thresholds, theta_row, name):
    rows = sum(x.shape[0] for x in xs)
    depth, width = weights[0].shape
    return pl.pallas_call(
        functools.partial(encode_both_kernel, len(xs), theta_row),
        in_specs=[FULL] * (len(xs) + 1) + [HBM] + [FULL] * 2,
        out_specs=[HBM] * 2,
        out_shape=[jax.ShapeDtypeStruct((rows, width), jnp.bfloat16)] * 2,
        scratch_shapes=[
            pltpu.VMEM((depth, width), jnp.bfloat16),
            pltpu.VMEM((2, rows, width), jnp.bfloat16),
            pltpu.SemaphoreType.DMA,
            pltpu.SemaphoreType.DMA((2, len(xs))),
        ],
        compiler_params=params(),
        cost_estimate=cost(4 * rows * depth * width // 32, 0),
        name=name,
    )(*xs, *weights, *thresholds)


def encode_pieces_kernel(chunks, at_ref, *refs):
    xs, ws, (out, w_buf, o_buf, w_sem, o_sem) = refs[:chunks], refs[chunks:chunks + 4], refs[chunks + 4:]
    depth = xs[0].shape[1]
    w_copies = [pltpu.make_async_copy(ws[k], w_buf.at[:, pl.ds(k * PIECE, PIECE)], w_sem.at[k]) for k in range(4)]
    for copy in w_copies:
        copy.start()
    copies = []
    for pair in range(2):
        for copy in w_copies[2 * pair:2 * pair + 2]:
            copy.wait()
        here = slice(2 * pair * PIECE, 2 * (pair + 1) * PIECE)
        theta = w_buf[depth:depth + 16, here].astype(jnp.float32)[:1, :]
        row = 0
        for k in range(chunks):
            rows = xs[k].shape[0]
            pre = jnp.dot(xs[k][...], w_buf[0:depth, here], preferred_element_type=jnp.float32)
            o_buf[row:row + rows, here] = jnp.maximum(pre - theta, 0.0).astype(jnp.bfloat16)
            row += rows
        for step in (2 * pair, 2 * pair + 1):
            col = pl.multiple_of(lax.rem(at_ref[0] + step, 4) * PIECE, PIECE)
            copies.append(pltpu.make_async_copy(
                o_buf.at[:, pl.ds(step * PIECE, PIECE)], out.at[:, pl.ds(col, PIECE)], o_sem.at[step]))
            copies[step].start()
    for copy in copies:
        copy.wait()


def encode_pieces(at, xs, pieces, name):
    rows = sum(x.shape[0] for x in xs)
    depth = xs[0].shape[1]
    return pl.pallas_call(
        functools.partial(encode_pieces_kernel, len(xs)),
        in_specs=[SMEM] + [FULL] * len(xs) + [ANY] * 4,
        out_specs=HBM,
        out_shape=jax.ShapeDtypeStruct((rows, 4 * PIECE), jnp.bfloat16),
        scratch_shapes=[
            pltpu.VMEM((pieces[0].shape[0], 4 * PIECE), jnp.bfloat16),
            pltpu.VMEM((rows, 4 * PIECE), jnp.bfloat16),
            pltpu.SemaphoreType.DMA((4,)),
            pltpu.SemaphoreType.DMA((4,)),
        ],
        compiler_params=params(),
        cost_estimate=cost(8 * rows * depth * PIECE // 32, 0),
        name=name,
    )(at, *xs, *pieces)


def squeeze(value):
    value = value * value
    value = value * value
    return (value * value).astype(jnp.bfloat16)


def widen(value):
    return jnp.exp2(jnp.log2(value.astype(jnp.float32)) * 0.125)


def gain(power):
    return jnp.where(power > 0, lax.rsqrt(jnp.maximum(power, 1e-37)) * TOP, 0.0)


def root(power):
    return jnp.sqrt(power) * np.float32(1 / TOP)


def column(row):
    return jnp.broadcast_to(row, (128, row.shape[1])).T


def pack(row_power, column_power):
    width = column_power.shape[1]
    if row_power.shape[1] < width:
        row_power = jnp.concatenate(
            [row_power, jnp.zeros((1, width - row_power.shape[1]), jnp.float32)], axis=1)
    at = lax.broadcasted_iota(jnp.int32, (16, width), 0)
    out = jnp.zeros((16, width), jnp.float32)
    for base, power in ((0, column_power), (3, row_power)):
        rest = power
        for part in range(3):
            piece = rest.astype(jnp.bfloat16).astype(jnp.float32)
            out = jnp.where(at == base + part, piece, out)
            rest = rest - piece
    return out.astype(jnp.bfloat16)


def unpack(tail, rows):
    tail = tail.astype(jnp.float32)
    column_power = tail[0:1, :] + tail[1:2, :] + tail[2:3, :]
    row_power = tail[3:4, :rows] + tail[4:5, :rows] + tail[5:6, :rows]
    return row_power, column_power


def square_sum(ref, cols):
    total = None
    for at in range(0, ref.shape[0], 256):
        wide = ref[at:at + 256, cols].astype(jnp.float32)
        part = jnp.sum((wide * wide).reshape(32, 8, -1), axis=0)
        total = part if total is None else total + part
    return jnp.sum(total, axis=0, keepdims=True)


def products_kernel(jobs, leads, at_ref, *refs):
    ss, ds, refs = refs[:8], refs[8:12], list(refs[12:])
    dp_ref = None if leads else refs.pop(0)
    relays = [refs.pop(0) if m in (1, 3) else None for m, _ in jobs]
    if jobs[0][0] == 0:
        refs.pop(0)
    outs = [[refs.pop(0) for _ in range(1 if m in (1, 3) else 2)] for m, _ in jobs]
    if leads:
        dp_ref = refs.pop(0)
    s_bufs, r_bufs, o_bufs, s_sem, r_sem, o_sem = refs
    rows, width = ds[0].shape
    tile = width // 2
    core = at_ref[1]
    s_copies, r_copies, copies = [], [], []
    for j, (m, turn) in enumerate(jobs):
        target = lax.rem(at_ref[2] + m, 4)
        s_copies.append([])
        for k in range(2):
            here = pl.ds(k * 2 * rows, 2 * rows)
            for which in range(2):
                chosen = at_ref[4] == (which if turn == 0 else 1 - which)
                blocks = [ss[which * 4 + k * 2 + choice] for choice in (k, 1 - k)]
                for quarter in range(2):
                    col = pl.ds(pl.multiple_of(lax.rem(target, 2) * 512, 512), 512)
                    copy = pltpu.make_async_copy(blocks[quarter].at[:, col], s_bufs.at[j, here, :], s_sem.at[j, k])
                    pl.when((core == 0) & chosen & (target // 2 == quarter))(copy.start)
                for b in range(4):
                    col = pl.ds(pl.multiple_of((b % 2 * 4 + target) * 128, 128), 128)
                    part = pltpu.make_async_copy(
                        blocks[1 - b // 2].at[:, col], s_bufs.at[j, here, pl.ds(b * 128, 128)], s_sem.at[j, k])
                    pl.when((core == 1) & chosen)(part.start)
            s_copies[j].append(copy)
        r_copies.append(None)
        if m in (1, 3):
            r_copies[j] = pltpu.make_async_copy(relays[j], r_bufs.at[j], r_sem.at[j])
            r_copies[j].start()
    if leads:
        for t in range(2):
            cols = slice(t * tile, t * tile + tile)
            dp_ref[:, cols] = jnp.broadcast_to(sum(square_sum(d, cols) for d in ds), (8, tile))

    def job(j, m):
        s_buf, r_buf, o_buf, out = s_bufs.at[j], r_bufs.at[j], o_bufs.at[j], outs[j]
        relayed = {1: 0, 3: 1}.get(m)
        column_powers = [dp_ref[0:1, 0:tile], dp_ref[0:1, tile:width]]

        def dots(t, ks):
            return sum(
                lax.dot_general(s_buf[k * rows:k * rows + rows, :], ds[k][:, t * tile:t * tile + tile],
                                (((0,), (0,)), ((), ())), preferred_element_type=jnp.float32) for k in ks)

        s_copies[j][0].wait()
        near = dots(0, (0, 1))
        s_copies[j][1].wait()
        s_power = square_sum(s_buf, slice(None))
        row_powers = [s_power, s_power]
        if relayed is not None:
            r_copies[j].wait()
            r_rows, r_columns = unpack(r_buf[512:528, :], 512)
            row_powers[relayed] = s_power + r_rows
            column_powers[relayed] = column_powers[relayed] + r_columns
            r_scale = jnp.concatenate([column(root(r_rows))] * (tile // 128), axis=1) * root(r_columns)
        for t in range(2):
            cols = slice(t * tile, t * tile + tile)
            total = near + dots(0, (2, 3)) if t == 0 else dots(1, (0, 1, 2, 3))
            if t == relayed:
                total = total + widen(r_buf[0:512, :]) * r_scale
            if not m:
                out[0][:, cols] = total
                continue
            if t == 0 or relayed is not None:
                row_gain = jnp.concatenate([column(gain(row_powers[t]))] * (tile // 128), axis=1)
            o_buf[0:512, cols] = squeeze(total * row_gain * gain(column_powers[t]))
            o_buf[512:528, cols] = pack(row_powers[t], column_powers[t])
            target_ref = out[t] if m == 2 else out[0].at[:, pl.ds(t * tile, tile)]
            copy = pltpu.make_async_copy(o_buf.at[:, pl.ds(t * tile, tile)], target_ref, o_sem.at[j, t])
            copy.start()
            copies.append(copy)
        if not m:
            out[1][...] = jnp.broadcast_to(s_power, out[1].shape)

    for j, (m, _) in enumerate(jobs):
        job(j, m)
    for copy in copies:
        copy.wait()


def products(jobs, at, ss, ds, d_power=None, relays=(), after=None):
    rows, width = ds[0].shape
    f32 = jnp.float32
    leads = d_power is None
    count = len(jobs)
    shapes, specs = [], []
    for m, _ in jobs:
        if m == 2:
            shapes += [jax.ShapeDtypeStruct((528, width // 2), jnp.bfloat16)] * 2
            specs += [HBM] * 2
        elif m:
            shapes += [jax.ShapeDtypeStruct((528, width), jnp.bfloat16)]
            specs += [HBM]
        else:
            shapes += [jax.ShapeDtypeStruct(s, f32) for s in ((512, width), (8, 512))]
            specs += [FULL] * 2
    operands = [at, *ss, *ds]
    if leads:
        shapes, specs = shapes + [jax.ShapeDtypeStruct((8, width), f32)], specs + [FULL]
    else:
        operands.append(d_power)
    in_specs = [SMEM] + [HBM] * 8 + [FULL] * (len(operands) - 9)
    extra = [*relays] if after is None else [after]
    return pl.pallas_call(
        functools.partial(products_kernel, jobs, leads),
        in_specs=in_specs + [HBM] * len(extra),
        out_specs=specs,
        out_shape=shapes,
        scratch_shapes=[
            pltpu.VMEM((count, 4 * rows, 512), jnp.bfloat16),
            pltpu.VMEM((count, 528, width // 2), jnp.bfloat16),
            pltpu.VMEM((count, 528, width), jnp.bfloat16),
            pltpu.SemaphoreType.DMA((count, 2)),
            pltpu.SemaphoreType.DMA((count,)),
            pltpu.SemaphoreType.DMA((count, 2)),
        ],
        compiler_params=params(),
        cost_estimate=cost(2 * 512 * 4 * rows * width * count, 5 << 20),
        name="products",
    )(*operands, *extra)


ORDER = (2, 1, 3, 0)


def first_sum_kernel(at_ref, own_ref, sp_ref, dp_ref, *refs):
    messages, (o1, o2, o3, keep_ref, keep_rp_ref, keep_cp_ref), scratch = refs[:2], refs[2:8], refs[8:]
    m_buf, o_buf, scale_ref, power_ref, m_sem, o_sem = scratch
    width = own_ref.shape[1]
    tails, blocks = [], []
    for k, message in enumerate(messages):
        rows = pl.ds(512, 16)
        tails.append(pltpu.make_async_copy(message.at[rows, :], m_buf.at[k, rows, :], m_sem.at[4, k]))
    for i, m in enumerate(ORDER):
        rows = pl.ds(pl.multiple_of(lax.rem(at_ref[3] + m, 4) * 128, 128), 128)
        blocks.append((rows, [
            pltpu.make_async_copy(message.at[rows, :], m_buf.at[k, rows, :], m_sem.at[i, k])
            for k, message in enumerate(messages)]))
    for copies in [tails] + [copies for _, copies in blocks]:
        for copy in copies:
            copy.start()
    for copy in tails:
        copy.wait()

    row_total, column_total = sp_ref[0:1, :], dp_ref[0:1, :]
    column_roots = []
    half = width // 2
    for k in range(2):
        parts = [unpack(m_buf[k, 512:528, h * half:h * half + half], 512) for h in range(2)]
        for h in range(2):
            scale_ref[2 * k + h] = column(root(parts[h][0]))
        column_power = jnp.concatenate([part[1] for part in parts], axis=1)
        column_roots.append(root(column_power))
        row_total = row_total + parts[0][0]
        column_total = column_total + column_power
    scale_ref[4] = column(gain(row_total))
    column_gain = gain(column_total)
    power_ref[...] = jnp.broadcast_to(row_total, power_ref.shape)
    keep_cp_ref[...] = jnp.broadcast_to(column_total, keep_cp_ref.shape)

    out_copies = []
    for i, m in enumerate(ORDER):
        here, copies = blocks[i]
        for copy in copies:
            copy.wait()
        scales = [scale_ref[k, here, :] for k in range(5)]
        for at in range(0, width, 128):
            cols = slice(at, at + 128)
            total = own_ref[here, cols]
            for k in range(2):
                total = total + widen(m_buf[k, here, cols]) * (
                    scales[2 * k + at // half] * column_roots[k][:, cols])
            if m:
                o_buf[i, 0:128, cols] = squeeze(total * (scales[4] * column_gain[:, cols]))
            else:
                keep_ref[:, cols] = total
        powers = power_ref[:, here]
        if m:
            o_buf[i, 128:144, :] = pack(powers[0:1, :], column_total)
            out_copies.append(pltpu.make_async_copy(o_buf.at[i], (o1, o2, o3)[m - 1], o_sem.at[i]))
            out_copies[i].start()
        else:
            keep_rp_ref[...] = powers
    for copy in out_copies:
        copy.wait()


def first_sum(at, own, row_power, column_power, messages):
    width = own.shape[1]
    shapes = [jax.ShapeDtypeStruct((144, width), jnp.bfloat16)] * 3 + [
        jax.ShapeDtypeStruct(s, jnp.float32) for s in ((128, width), (8, 128), (8, width))]
    return pl.pallas_call(
        first_sum_kernel,
        in_specs=[SMEM] + [FULL] * 3 + [HBM] * 2,
        out_specs=[HBM] * 3 + [FULL] * 3,
        out_shape=shapes,
        scratch_shapes=[
            pltpu.VMEM((2, 528, width), jnp.bfloat16),
            pltpu.VMEM((3, 144, width), jnp.bfloat16),
            pltpu.VMEM((5, 512, 128), jnp.float32),
            pltpu.VMEM((8, 512), jnp.float32),
            pltpu.SemaphoreType.DMA((5, 2)),
            pltpu.SemaphoreType.DMA((3,)),
        ],
        compiler_params=params(),
        cost_estimate=cost(10 << 20, 3 << 20),
        name="first_sum",
    )(at, own, row_power, column_power, *messages)


def add_messages(own_ref, rp_ref, cp_ref, messages):
    rows, width = own_ref.shape
    row_total, column_total = rp_ref[0:1, :], cp_ref[0:1, :]
    scales = []
    for message in messages:
        row_power, column_power = unpack(message[rows:rows + 16, :], rows)
        scales.append((column(root(row_power)), root(column_power)))
        row_total = row_total + row_power
        column_total = column_total + column_power
    tiles = []
    for at in range(0, width, 128):
        cols = slice(at, at + 128)
        total = own_ref[:, cols]
        for message, (row_scale, column_scale) in zip(messages, scales):
            total = total + widen(message[0:rows, cols]) * (row_scale * column_scale[:, cols])
        tiles.append(total)
    return tiles, row_total, column_total


def second_sum_kernel(own_ref, rp_ref, cp_ref, m1, m2, m3, z_ref):
    tiles, rows, columns = add_messages(own_ref, rp_ref, cp_ref, (m1, m2, m3))
    row_gain, column_gain = column(gain(rows)), gain(columns)
    for t, tile in enumerate(tiles):
        cols = slice(t * 128, t * 128 + 128)
        z_ref[0:128, cols] = squeeze(tile * (row_gain * column_gain[:, cols]))
    z_ref[128:144, :] = pack(rows, columns)


def second_sum(kept, messages):
    return pl.pallas_call(
        second_sum_kernel,
        in_specs=[FULL] * 6,
        out_specs=FULL,
        out_shape=jax.ShapeDtypeStruct((144, kept[0].shape[1]), jnp.bfloat16),
        compiler_params=params(),
        cost_estimate=cost(5 << 20, 2 << 20),
        name="second_sum",
    )(*kept, *messages)


def last_sum_kernel(row_total, own_ref, rp_ref, cp_ref, m1, m2, m3, z, out_ref):
    tiles, rows, columns = add_messages(own_ref, rp_ref, cp_ref, (m1, m2, m3, z))

    def back(power):
        return jnp.where(power > 0, lax.rsqrt(power + np.float32(EPS * row_total)), 0.0)

    row_back, column_back = column(back(rows)), back(columns)
    for t, tile in enumerate(tiles):
        cols = slice(t * 128, t * 128 + 128)
        out_ref[:, cols] = tile * (row_back * column_back[:, cols])


def last_sum(row_total, kept, messages):
    return pl.pallas_call(
        functools.partial(last_sum_kernel, row_total),
        in_specs=[FULL] * 7,
        out_specs=FULL,
        out_shape=jax.ShapeDtypeStruct(kept[0].shape, jnp.float32),
        compiler_params=params(),
        cost_estimate=cost(5 << 20, 2 << 20),
        name="last_sum",
    )(*kept, *messages)


def shards(dino_acts, siglip_acts, dino_encoder, siglip_encoder, dino_threshold, siglip_threshold):
    z_hi = lax.axis_index("mp")
    patch = lax.axis_index("patch")
    latent = lax.axis_index("latent")
    x, y = patch // 4, patch % 4
    z_lo, core = latent // 2, latent % 2
    first = (x + 2 * y) % 4
    at = jnp.stack([
        first, core, jnp.where(core == 0, x, y), jnp.where(core == 0, y, x),
        (z_hi == z_lo).astype(jnp.int32)]).astype(jnp.int32)
    row_total = dino_acts.shape[0] * dino_acts.shape[1] * lax.axis_size(AXES)
    latents = dino_encoder.shape[1]

    thresholds = jnp.concatenate([
        jnp.broadcast_to(dino_threshold[None, :], (16, latents)),
        jnp.broadcast_to(siglip_threshold[None, :], (16, latents))])

    theta = (thresholds, to_sibling(thresholds))
    d_own = dino_acts.reshape(-1, dino_acts.shape[-1])
    dino_sibling = to_sibling(dino_encoder)
    siglip_sibling = to_sibling(siglip_encoder)

    piece = along_z(jnp.concatenate([
        lax.dynamic_slice_in_dim(siglip_encoder, first * PIECE, PIECE, 1),
        lax.dynamic_slice_in_dim(thresholds[16:], first * PIECE, PIECE, 1)]))
    s_own = resample_local(siglip_acts).reshape(-1, siglip_acts.shape[-1])
    s_ext = along_z(s_own)

    def dino_codes(xs):
        away = encode(xs, dino_sibling, theta[1], 0, "dino_codes")
        return encode(xs, dino_encoder, theta[0], 0, "dino_codes"), away

    piece, s_own, d_own, siglip_sibling, dino_sibling, theta_sibling = lax.optimization_barrier(
        (piece, s_own, d_own, siglip_sibling, dino_sibling, theta[1]))
    theta = (thresholds, theta_sibling)
    d_ext = along_z(d_own)
    pieces = [
        piece,
        send(piece, lambda c: (-1, 0, 0, 0)),
        send(piece, lambda c: (0, 1, 0, 0)),
        send(piece, lambda c: (1, 0, 0, 0)),
    ]

    d_near, d_near_away = encode_both([d_own], (dino_encoder, dino_sibling), theta, 0, "dino_codes")
    s_own, s_ext, d_near, d_near_away = lax.optimization_barrier((s_own, s_ext, d_near, d_near_away))
    xs = [s_own, s_ext]
    one = encode_both(xs, (siglip_encoder, siglip_sibling), theta, 16, "siglip_codes")
    *one, p0, p1, p2, p3 = lax.optimization_barrier((*one, *pieces))
    pieces = [p0, p1, p2, p3]
    pieces_sibling = [to_sibling(p) for p in pieces]
    two = [encode_pieces(at, xs, pieces, "siglip_codes")]
    d_ext, two[0] = lax.optimization_barrier((d_ext, two[0]))
    two.append(encode_pieces(at, xs, pieces_sibling, "siglip_codes"))
    d_far, d_far_away = dino_codes([d_ext])

    sets = [[*pair, to_sibling(pair[0]), to_sibling(pair[1])] for pair in (one, two)]
    ds = (d_near, d_far, to_sibling(d_near_away), to_sibling(d_far_away))

    ss = sets[0] + sets[1]
    d_power = None
    relays, arrived = [], []
    for turn in range(2):
        low, high, *powers = products([(2, turn)], at, ss, ds, d_power)
        d_power = powers[0] if powers else d_power
        relays.append((first_way(low, 1), first_way(high, 3)))
    for turn, pair in enumerate(relays):
        part_one, part_three = products([(1, turn), (3, turn)], at, ss, ds, d_power, relays=pair)
        arrived.append((first_way(part_one, 1), first_way(part_three, 3)))
    own = products([(0, 0), (0, 1)], at, ss, ds, d_power, after=part_three)

    results = []
    for turn, pair in enumerate(arrived):
        sums = first_sum(at, *own[2 * turn:2 * turn + 2], d_power, pair)
        results.append((sums[3:], [second_way(sums[m - 1], m) for m in (1, 2, 3)]))
    message = send(second_sum(*results[0]), lambda c: (0, 0, 2, 0))
    kept, messages = results[1]
    return last_sum(row_total, kept, [*messages, message])


def solution(mesh):
    in_specs = (
        P(("mp", "patch", "latent"), None, None),
        P(("mp", "patch", "latent"), None, None),
        P(None, "latent"),
        P(None, "latent"),
        P("latent"),
        P("latent"),
    )
    out_specs = P(("mp", "patch"), "latent")
    return jax.shard_map(shards, mesh=mesh, in_specs=in_specs, out_specs=out_specs, check_vma=False)
```

```python
import functools

import jax
import jax.numpy as jnp
import numpy as np
from jax import lax
from jax.experimental import pallas as pl
from jax.experimental.pallas import tpu as pltpu
from jax.sharding import PartitionSpec as P

GRID = 16
SIG_SIDE = 27
EPS = 1e-06
AXES = ("mp", "patch", "latent")
VMEM = 16 * 1024 * 1024
TOP = np.float32(np.sqrt(2.0**15))
ANY = pl.BlockSpec(memory_space=pl.ANY)
HBM = pl.BlockSpec(memory_space=pltpu.HBM)
SMEM = pl.BlockSpec(memory_space=pltpu.SMEM)
FULL = pl.BlockSpec(memory_space=pltpu.VMEM)
PIECE = 256


def resample_table(side_cells, grid_cells):
    weights_table = np.zeros((grid_cells, side_cells), np.float32)
    for target in range(grid_cells):
        source = (target + 0.5) * side_cells / grid_cells - 0.5
        low_index = int(np.floor(source))
        upper_part = source - low_index
        weights_table[target, low_index] += 1.0 - upper_part
        weights_table[target, min(low_index + 1, side_cells - 1)] += upper_part
    return weights_table


def resample_local(raw_block):
    table = resample_table(SIG_SIDE, GRID)
    table = np.kron(table, table).astype(np.float32)
    high = table.astype(jnp.bfloat16)
    low = (table - high.astype(np.float32)).astype(jnp.bfloat16)
    images = raw_block.shape[0]

    def part(matrix):
        return lax.dot_general(
            jnp.broadcast_to(jnp.asarray(matrix), (images,) + matrix.shape), raw_block,
            (((2,), (1,)), ((0,), (0,))), preferred_element_type=jnp.float32)

    return (part(high) + part(low)).astype(jnp.bfloat16)


def place(x, y, z, core):
    return (z // 2) * 64 + (x * 4 + y) * 4 + (z % 2) * 2 + core


def moves(step):
    out = []
    for x in range(4):
        for y in range(4):
            for z in range(4):
                for c in range(2):
                    dx, dy, dz, swap = step(c)
                    target = place((x + dx) % 4, (y + dy) % 4, (z + dz) % 4, c ^ swap)
                    out.append((place(x, y, z, c), target))
    return out


def send(value, step):
    return lax.ppermute(value, AXES, moves(step))


def to_sibling(value):
    return send(value, lambda c: (0, 0, 0, 1))


def along_z(value):
    return send(value, lambda c: (0, 0, -1 if c else 1, 0))


def first_way(value, m):
    return send(value, lambda c: (0, m, 0, 0) if c else (m, 0, 0, 0))


def second_way(value, m):
    return send(value, lambda c: (m, 0, 0, 0) if c else (0, m, 0, 0))


def params():
    return pltpu.CompilerParams(vmem_limit_bytes=VMEM)


def cost(flops, size):
    return pl.CostEstimate(flops=flops, bytes_accessed=size, transcendentals=0)


def encode_kernel(chunks, theta_row, *refs):
    xs, (w_ref, t_ref, out, o_buf, o_sem) = refs[:chunks], refs[chunks:]
    depth = xs[0].shape[1]
    theta = t_ref[theta_row:theta_row + 16, :].astype(jnp.float32)[:1, :]
    copies = []
    row = 0
    for k in range(chunks):
        rows = xs[k].shape[0]
        here = pl.ds(row, rows)
        pre = jnp.dot(xs[k][...], w_ref[0:depth, :], preferred_element_type=jnp.float32)
        o_buf[here, :] = jnp.maximum(pre - theta, 0.0).astype(jnp.bfloat16)
        copies.append(pltpu.make_async_copy(o_buf.at[here, :], out.at[here, :], o_sem.at[k]))
        copies[k].start()
        row += rows
    for copy in copies:
        copy.wait()


def encode(xs, weights, thresholds, theta_row, name):
    rows = sum(x.shape[0] for x in xs)
    depth = xs[0].shape[1]
    width = weights.shape[1]
    return pl.pallas_call(
        functools.partial(encode_kernel, len(xs), theta_row),
        in_specs=[FULL] * (len(xs) + 2),
        out_specs=HBM,
        out_shape=jax.ShapeDtypeStruct((rows, width), jnp.bfloat16),
        scratch_shapes=[
            pltpu.VMEM((rows, width), jnp.bfloat16),
            pltpu.SemaphoreType.DMA((len(xs),)),
        ],
        compiler_params=params(),
        cost_estimate=cost(2 * rows * depth * width // 32, 0),
        name=name,
    )(*xs, weights, thresholds)


def encode_both_kernel(chunks, theta_row, *refs):
    xs, refs = refs[:chunks], refs[chunks:]
    w_ref, v_ref, t_ref, u_ref, out_a, out_b, v_buf, o_buf, v_sem, o_sem = refs
    v_copy = pltpu.make_async_copy(v_ref, v_buf, v_sem)
    v_copy.start()
    copies = []
    for j, (weights, thresholds, out) in enumerate(((w_ref, t_ref, out_a), (v_buf, u_ref, out_b))):
        if j:
            v_copy.wait()
        theta = thresholds[theta_row:theta_row + 16, :].astype(jnp.float32)[:1, :]
        row = 0
        for k in range(chunks):
            rows = xs[k].shape[0]
            here = pl.ds(row, rows)
            pre = jnp.dot(xs[k][...], weights[...], preferred_element_type=jnp.float32)
            o_buf[j, here, :] = jnp.maximum(pre - theta, 0.0).astype(jnp.bfloat16)
            copy = pltpu.make_async_copy(o_buf.at[j, here, :], out.at[here, :], o_sem.at[j, k])
            copy.start()
            copies.append(copy)
            row += rows
    for copy in copies:
        copy.wait()


def encode_both(xs, weights, thresholds, theta_row, name):
    rows = sum(x.shape[0] for x in xs)
    depth, width = weights[0].shape
    return pl.pallas_call(
        functools.partial(encode_both_kernel, len(xs), theta_row),
        in_specs=[FULL] * (len(xs) + 1) + [HBM] + [FULL] * 2,
        out_specs=[HBM] * 2,
        out_shape=[jax.ShapeDtypeStruct((rows, width), jnp.bfloat16)] * 2,
        scratch_shapes=[
            pltpu.VMEM((depth, width), jnp.bfloat16),
            pltpu.VMEM((2, rows, width), jnp.bfloat16),
            pltpu.SemaphoreType.DMA,
            pltpu.SemaphoreType.DMA((2, len(xs))),
        ],
        compiler_params=params(),
        cost_estimate=cost(4 * rows * depth * width // 32, 0),
        name=name,
    )(*xs, *weights, *thresholds)


def encode_pieces_kernel(chunks, at_ref, *refs):
    xs, ws, (out, w_buf, o_buf, w_sem, o_sem) = refs[:chunks], refs[chunks:chunks + 4], refs[chunks + 4:]
    depth = xs[0].shape[1]
    w_copies = [pltpu.make_async_copy(ws[k], w_buf.at[:, pl.ds(k * PIECE, PIECE)], w_sem.at[k]) for k in range(4)]
    for copy in w_copies:
        copy.start()
    copies = []
    for pair in range(2):
        for copy in w_copies[2 * pair:2 * pair + 2]:
            copy.wait()
        here = slice(2 * pair * PIECE, 2 * (pair + 1) * PIECE)
        theta = w_buf[depth:depth + 16, here].astype(jnp.float32)[:1, :]
        row = 0
        for k in range(chunks):
            rows = xs[k].shape[0]
            pre = jnp.dot(xs[k][...], w_buf[0:depth, here], preferred_element_type=jnp.float32)
            o_buf[row:row + rows, here] = jnp.maximum(pre - theta, 0.0).astype(jnp.bfloat16)
            row += rows
        for step in (2 * pair, 2 * pair + 1):
            col = pl.multiple_of(lax.rem(at_ref[0] + step, 4) * PIECE, PIECE)
            copies.append(pltpu.make_async_copy(
                o_buf.at[:, pl.ds(step * PIECE, PIECE)], out.at[:, pl.ds(col, PIECE)], o_sem.at[step]))
            copies[step].start()
    for copy in copies:
        copy.wait()


def encode_pieces(at, xs, pieces, name):
    rows = sum(x.shape[0] for x in xs)
    depth = xs[0].shape[1]
    return pl.pallas_call(
        functools.partial(encode_pieces_kernel, len(xs)),
        in_specs=[SMEM] + [FULL] * len(xs) + [ANY] * 4,
        out_specs=HBM,
        out_shape=jax.ShapeDtypeStruct((rows, 4 * PIECE), jnp.bfloat16),
        scratch_shapes=[
            pltpu.VMEM((pieces[0].shape[0], 4 * PIECE), jnp.bfloat16),
            pltpu.VMEM((rows, 4 * PIECE), jnp.bfloat16),
            pltpu.SemaphoreType.DMA((4,)),
            pltpu.SemaphoreType.DMA((4,)),
        ],
        compiler_params=params(),
        cost_estimate=cost(8 * rows * depth * PIECE // 32, 0),
        name=name,
    )(at, *xs, *pieces)


def squeeze(value):
    value = value * value
    value = value * value
    return (value * value).astype(jnp.bfloat16)


def widen(value):
    return jnp.exp2(jnp.log2(value.astype(jnp.float32)) * 0.125)


def gain(power):
    return jnp.where(power > 0, lax.rsqrt(jnp.maximum(power, 1e-37)) * TOP, 0.0)


def root(power):
    return jnp.sqrt(power) * np.float32(1 / TOP)


def column(row):
    return jnp.broadcast_to(row, (128, row.shape[1])).T


def pack(row_power, column_power):
    width = column_power.shape[1]
    if row_power.shape[1] < width:
        row_power = jnp.concatenate(
            [row_power, jnp.zeros((1, width - row_power.shape[1]), jnp.float32)], axis=1)
    at = lax.broadcasted_iota(jnp.int32, (16, width), 0)
    out = jnp.zeros((16, width), jnp.float32)
    for base, power in ((0, column_power), (3, row_power)):
        rest = power
        for part in range(3):
            piece = rest.astype(jnp.bfloat16).astype(jnp.float32)
            out = jnp.where(at == base + part, piece, out)
            rest = rest - piece
    return out.astype(jnp.bfloat16)


def unpack(tail, rows):
    tail = tail.astype(jnp.float32)
    column_power = tail[0:1, :] + tail[1:2, :] + tail[2:3, :]
    row_power = tail[3:4, :rows] + tail[4:5, :rows] + tail[5:6, :rows]
    return row_power, column_power


def square_sum(ref, cols):
    total = None
    for at in range(0, ref.shape[0], 256):
        wide = ref[at:at + 256, cols].astype(jnp.float32)
        part = jnp.sum((wide * wide).reshape(32, 8, -1), axis=0)
        total = part if total is None else total + part
    return jnp.sum(total, axis=0, keepdims=True)


def products_kernel(jobs, leads, at_ref, *refs):
    ss, ds, refs = refs[:8], refs[8:12], list(refs[12:])
    dp_ref = None if leads else refs.pop(0)
    relays = [refs.pop(0) if m in (1, 3) else None for m, _ in jobs]
    if jobs[0][0] == 0:
        refs.pop(0)
    outs = [[refs.pop(0) for _ in range(1 if m in (1, 3) else 2)] for m, _ in jobs]
    if leads:
        dp_ref = refs.pop(0)
    s_bufs, r_bufs, o_bufs, s_sem, r_sem, o_sem = refs
    rows, width = ds[0].shape
    tile = width // 2
    core = at_ref[1]
    s_copies, r_copies, copies = [], [], []
    for j, (m, turn) in enumerate(jobs):
        target = lax.rem(at_ref[2] + m, 4)
        s_copies.append([])
        for k in range(2):
            here = pl.ds(k * 2 * rows, 2 * rows)
            for which in range(2):
                chosen = at_ref[4] == (which if turn == 0 else 1 - which)
                blocks = [ss[which * 4 + k * 2 + choice] for choice in (k, 1 - k)]
                for quarter in range(2):
                    col = pl.ds(pl.multiple_of(lax.rem(target, 2) * 512, 512), 512)
                    copy = pltpu.make_async_copy(blocks[quarter].at[:, col], s_bufs.at[j, here, :], s_sem.at[j, k])
                    pl.when((core == 0) & chosen & (target // 2 == quarter))(copy.start)
                for b in range(4):
                    col = pl.ds(pl.multiple_of((b % 2 * 4 + target) * 128, 128), 128)
                    part = pltpu.make_async_copy(
                        blocks[1 - b // 2].at[:, col], s_bufs.at[j, here, pl.ds(b * 128, 128)], s_sem.at[j, k])
                    pl.when((core == 1) & chosen)(part.start)
            s_copies[j].append(copy)
        r_copies.append(None)
        if m in (1, 3):
            r_copies[j] = pltpu.make_async_copy(relays[j], r_bufs.at[j], r_sem.at[j])
            r_copies[j].start()
    if leads:
        for t in range(2):
            cols = slice(t * tile, t * tile + tile)
            dp_ref[:, cols] = jnp.broadcast_to(sum(square_sum(d, cols) for d in ds), (8, tile))

    def job(j, m):
        s_buf, r_buf, o_buf, out = s_bufs.at[j], r_bufs.at[j], o_bufs.at[j], outs[j]
        relayed = {1: 0, 3: 1}.get(m)
        column_powers = [dp_ref[0:1, 0:tile], dp_ref[0:1, tile:width]]

        def dots(t, ks):
            return sum(
                lax.dot_general(s_buf[k * rows:k * rows + rows, :], ds[k][:, t * tile:t * tile + tile],
                                (((0,), (0,)), ((), ())), preferred_element_type=jnp.float32) for k in ks)

        s_copies[j][0].wait()
        near = dots(0, (0, 1))
        s_copies[j][1].wait()
        s_power = square_sum(s_buf, slice(None))
        row_powers = [s_power, s_power]
        if relayed is not None:
            r_copies[j].wait()
            r_rows, r_columns = unpack(r_buf[512:528, :], 512)
            row_powers[relayed] = s_power + r_rows
            column_powers[relayed] = column_powers[relayed] + r_columns
            r_scale = jnp.concatenate([column(root(r_rows))] * (tile // 128), axis=1) * root(r_columns)
        for t in range(2):
            cols = slice(t * tile, t * tile + tile)
            total = near + dots(0, (2, 3)) if t == 0 else dots(1, (0, 1, 2, 3))
            if t == relayed:
                total = total + widen(r_buf[0:512, :]) * r_scale
            if not m:
                out[0][:, cols] = total
                continue
            if t == 0 or relayed is not None:
                row_gain = jnp.concatenate([column(gain(row_powers[t]))] * (tile // 128), axis=1)
            o_buf[0:512, cols] = squeeze(total * row_gain * gain(column_powers[t]))
            o_buf[512:528, cols] = pack(row_powers[t], column_powers[t])
            target_ref = out[t] if m == 2 else out[0].at[:, pl.ds(t * tile, tile)]
            copy = pltpu.make_async_copy(o_buf.at[:, pl.ds(t * tile, tile)], target_ref, o_sem.at[j, t])
            copy.start()
            copies.append(copy)
        if not m:
            out[1][...] = jnp.broadcast_to(s_power, out[1].shape)

    for j, (m, _) in enumerate(jobs):
        job(j, m)
    for copy in copies:
        copy.wait()


def products(jobs, at, ss, ds, d_power=None, relays=(), after=None):
    rows, width = ds[0].shape
    f32 = jnp.float32
    leads = d_power is None
    count = len(jobs)
    shapes, specs = [], []
    for m, _ in jobs:
        if m == 2:
            shapes += [jax.ShapeDtypeStruct((528, width // 2), jnp.bfloat16)] * 2
            specs += [HBM] * 2
        elif m:
            shapes += [jax.ShapeDtypeStruct((528, width), jnp.bfloat16)]
            specs += [HBM]
        else:
            shapes += [jax.ShapeDtypeStruct(s, f32) for s in ((512, width), (8, 512))]
            specs += [FULL] * 2
    operands = [at, *ss, *ds]
    if leads:
        shapes, specs = shapes + [jax.ShapeDtypeStruct((8, width), f32)], specs + [FULL]
    else:
        operands.append(d_power)
    in_specs = [SMEM] + [HBM] * 8 + [FULL] * (len(operands) - 9)
    extra = [*relays] if after is None else [after]
    return pl.pallas_call(
        functools.partial(products_kernel, jobs, leads),
        in_specs=in_specs + [HBM] * len(extra),
        out_specs=specs,
        out_shape=shapes,
        scratch_shapes=[
            pltpu.VMEM((count, 4 * rows, 512), jnp.bfloat16),
            pltpu.VMEM((count, 528, width // 2), jnp.bfloat16),
            pltpu.VMEM((count, 528, width), jnp.bfloat16),
            pltpu.SemaphoreType.DMA((count, 2)),
            pltpu.SemaphoreType.DMA((count,)),
            pltpu.SemaphoreType.DMA((count, 2)),
        ],
        compiler_params=params(),
        cost_estimate=cost(2 * 512 * 4 * rows * width * count, 5 << 20),
        name="products",
    )(*operands, *extra)


ORDER = (2, 1, 3, 0)


def first_sum_kernel(at_ref, own_ref, sp_ref, dp_ref, *refs):
    messages, (o1, o2, o3, keep_ref, keep_rp_ref, keep_cp_ref), scratch = refs[:2], refs[2:8], refs[8:]
    m_buf, o_buf, scale_ref, power_ref, m_sem, o_sem = scratch
    width = own_ref.shape[1]
    tails, blocks = [], []
    for k, message in enumerate(messages):
        rows = pl.ds(512, 16)
        tails.append(pltpu.make_async_copy(message.at[rows, :], m_buf.at[k, rows, :], m_sem.at[4, k]))
    for i, m in enumerate(ORDER):
        rows = pl.ds(pl.multiple_of(lax.rem(at_ref[3] + m, 4) * 128, 128), 128)
        blocks.append((rows, [
            pltpu.make_async_copy(message.at[rows, :], m_buf.at[k, rows, :], m_sem.at[i, k])
            for k, message in enumerate(messages)]))
    for copies in [tails] + [copies for _, copies in blocks]:
        for copy in copies:
            copy.start()
    for copy in tails:
        copy.wait()

    row_total, column_total = sp_ref[0:1, :], dp_ref[0:1, :]
    column_roots = []
    half = width // 2
    for k in range(2):
        parts = [unpack(m_buf[k, 512:528, h * half:h * half + half], 512) for h in range(2)]
        for h in range(2):
            scale_ref[2 * k + h] = column(root(parts[h][0]))
        column_power = jnp.concatenate([part[1] for part in parts], axis=1)
        column_roots.append(root(column_power))
        row_total = row_total + parts[0][0]
        column_total = column_total + column_power
    scale_ref[4] = column(gain(row_total))
    column_gain = gain(column_total)
    power_ref[...] = jnp.broadcast_to(row_total, power_ref.shape)
    keep_cp_ref[...] = jnp.broadcast_to(column_total, keep_cp_ref.shape)

    out_copies = []
    for i, m in enumerate(ORDER):
        here, copies = blocks[i]
        for copy in copies:
            copy.wait()
        scales = [scale_ref[k, here, :] for k in range(5)]
        for at in range(0, width, 128):
            cols = slice(at, at + 128)
            total = own_ref[here, cols]
            for k in range(2):
                total = total + widen(m_buf[k, here, cols]) * (
                    scales[2 * k + at // half] * column_roots[k][:, cols])
            if m:
                o_buf[i, 0:128, cols] = squeeze(total * (scales[4] * column_gain[:, cols]))
            else:
                keep_ref[:, cols] = total
        powers = power_ref[:, here]
        if m:
            o_buf[i, 128:144, :] = pack(powers[0:1, :], column_total)
            out_copies.append(pltpu.make_async_copy(o_buf.at[i], (o1, o2, o3)[m - 1], o_sem.at[i]))
            out_copies[i].start()
        else:
            keep_rp_ref[...] = powers
    for copy in out_copies:
        copy.wait()


def first_sum(at, own, row_power, column_power, messages):
    width = own.shape[1]
    shapes = [jax.ShapeDtypeStruct((144, width), jnp.bfloat16)] * 3 + [
        jax.ShapeDtypeStruct(s, jnp.float32) for s in ((128, width), (8, 128), (8, width))]
    return pl.pallas_call(
        first_sum_kernel,
        in_specs=[SMEM] + [FULL] * 3 + [HBM] * 2,
        out_specs=[HBM] * 3 + [FULL] * 3,
        out_shape=shapes,
        scratch_shapes=[
            pltpu.VMEM((2, 528, width), jnp.bfloat16),
            pltpu.VMEM((3, 144, width), jnp.bfloat16),
            pltpu.VMEM((5, 512, 128), jnp.float32),
            pltpu.VMEM((8, 512), jnp.float32),
            pltpu.SemaphoreType.DMA((5, 2)),
            pltpu.SemaphoreType.DMA((3,)),
        ],
        compiler_params=params(),
        cost_estimate=cost(10 << 20, 3 << 20),
        name="first_sum",
    )(at, own, row_power, column_power, *messages)


def add_messages(own_ref, rp_ref, cp_ref, messages):
    rows, width = own_ref.shape
    row_total, column_total = rp_ref[0:1, :], cp_ref[0:1, :]
    scales = []
    for message in messages:
        row_power, column_power = unpack(message[rows:rows + 16, :], rows)
        scales.append((column(root(row_power)), root(column_power)))
        row_total = row_total + row_power
        column_total = column_total + column_power
    tiles = []
    for at in range(0, width, 128):
        cols = slice(at, at + 128)
        total = own_ref[:, cols]
        for message, (row_scale, column_scale) in zip(messages, scales):
            total = total + widen(message[0:rows, cols]) * (row_scale * column_scale[:, cols])
        tiles.append(total)
    return tiles, row_total, column_total


def second_sum_kernel(own_ref, rp_ref, cp_ref, m1, m2, m3, z_ref):
    tiles, rows, columns = add_messages(own_ref, rp_ref, cp_ref, (m1, m2, m3))
    row_gain, column_gain = column(gain(rows)), gain(columns)
    for t, tile in enumerate(tiles):
        cols = slice(t * 128, t * 128 + 128)
        z_ref[0:128, cols] = squeeze(tile * (row_gain * column_gain[:, cols]))
    z_ref[128:144, :] = pack(rows, columns)


def second_sum(kept, messages):
    return pl.pallas_call(
        second_sum_kernel,
        in_specs=[FULL] * 6,
        out_specs=FULL,
        out_shape=jax.ShapeDtypeStruct((144, kept[0].shape[1]), jnp.bfloat16),
        compiler_params=params(),
        cost_estimate=cost(5 << 20, 2 << 20),
        name="second_sum",
    )(*kept, *messages)


def last_sum_kernel(row_total, own_ref, rp_ref, cp_ref, m1, m2, m3, z, out_ref):
    tiles, rows, columns = add_messages(own_ref, rp_ref, cp_ref, (m1, m2, m3, z))

    def back(power):
        return jnp.where(power > 0, lax.rsqrt(power + np.float32(EPS * row_total)), 0.0)

    row_back, column_back = column(back(rows)), back(columns)
    for t, tile in enumerate(tiles):
        cols = slice(t * 128, t * 128 + 128)
        out_ref[:, cols] = tile * (row_back * column_back[:, cols])


def last_sum(row_total, kept, messages):
    return pl.pallas_call(
        functools.partial(last_sum_kernel, row_total),
        in_specs=[FULL] * 7,
        out_specs=FULL,
        out_shape=jax.ShapeDtypeStruct(kept[0].shape, jnp.float32),
        compiler_params=params(),
        cost_estimate=cost(5 << 20, 2 << 20),
        name="last_sum",
    )(*kept, *messages)


def shards(dino_acts, siglip_acts, dino_encoder, siglip_encoder, dino_threshold, siglip_threshold):
    z_hi = lax.axis_index("mp")
    patch = lax.axis_index("patch")
    latent = lax.axis_index("latent")
    x, y = patch // 4, patch % 4
    z_lo, core = latent // 2, latent % 2
    first = (x + 2 * y) % 4
    at = jnp.stack([
        first, core, jnp.where(core == 0, x, y), jnp.where(core == 0, y, x),
        (z_hi == z_lo).astype(jnp.int32)]).astype(jnp.int32)
    row_total = dino_acts.shape[0] * dino_acts.shape[1] * lax.axis_size(AXES)
    latents = dino_encoder.shape[1]

    thresholds = jnp.concatenate([
        jnp.broadcast_to(dino_threshold[None, :], (16, latents)),
        jnp.broadcast_to(siglip_threshold[None, :], (16, latents))])

    theta = (thresholds, to_sibling(thresholds))
    d_own = dino_acts.reshape(-1, dino_acts.shape[-1])
    dino_sibling = to_sibling(dino_encoder)
    siglip_sibling = to_sibling(siglip_encoder)

    piece = along_z(jnp.concatenate([
        lax.dynamic_slice_in_dim(siglip_encoder, first * PIECE, PIECE, 1),
        lax.dynamic_slice_in_dim(thresholds[16:], first * PIECE, PIECE, 1)]))
    s_own = resample_local(siglip_acts).reshape(-1, siglip_acts.shape[-1])
    s_ext = along_z(s_own)

    def dino_codes(xs):
        away = encode(xs, dino_sibling, theta[1], 0, "dino_codes")
        return encode(xs, dino_encoder, theta[0], 0, "dino_codes"), away

    piece, s_own, d_own, siglip_sibling, dino_sibling, theta_sibling = lax.optimization_barrier(
        (piece, s_own, d_own, siglip_sibling, dino_sibling, theta[1]))
    theta = (thresholds, theta_sibling)
    d_ext = along_z(d_own)
    pieces = [
        piece,
        send(piece, lambda c: (-1, 0, 0, 0)),
        send(piece, lambda c: (0, 1, 0, 0)),
        send(piece, lambda c: (1, 0, 0, 0)),
    ]

    d_near, d_near_away = encode_both([d_own], (dino_encoder, dino_sibling), theta, 0, "dino_codes")
    s_own, s_ext, d_near, d_near_away = lax.optimization_barrier((s_own, s_ext, d_near, d_near_away))
    xs = [s_own, s_ext]
    one = encode_both(xs, (siglip_encoder, siglip_sibling), theta, 16, "siglip_codes")
    *one, p0, p1, p2, p3 = lax.optimization_barrier((*one, *pieces))
    pieces = [p0, p1, p2, p3]
    pieces_sibling = [to_sibling(p) for p in pieces]
    two = [encode_pieces(at, xs, pieces, "siglip_codes")]
    d_ext, two[0] = lax.optimization_barrier((d_ext, two[0]))
    two.append(encode_pieces(at, xs, pieces_sibling, "siglip_codes"))
    d_far, d_far_away = dino_codes([d_ext])

    sets = [[*pair, to_sibling(pair[0]), to_sibling(pair[1])] for pair in (one, two)]
    ds = (d_near, d_far, to_sibling(d_near_away), to_sibling(d_far_away))

    ss = sets[0] + sets[1]
    d_power = None
    relays, arrived = [], []
    for turn in range(2):
        low, high, *powers = products([(2, turn)], at, ss, ds, d_power)
        d_power = powers[0] if powers else d_power
        relays.append((first_way(low, 1), first_way(high, 3)))
    for turn, pair in enumerate(relays):
        if turn == 0:
            part_one, part_three = products([(1, 0), (3, 0)], at, ss, ds, d_power, relays=pair)
        else:
            part_one, = products([(1, 1)], at, ss, ds, d_power, relays=pair[:1])
            part_three, = products([(3, 1)], at, ss, ds, d_power, relays=pair[1:])
        arrived.append((first_way(part_one, 1), first_way(part_three, 3)))
    own = products([(0, 0), (0, 1)], at, ss, ds, d_power, after=part_three)

    results = []
    for turn, pair in enumerate(arrived):
        sums = first_sum(at, *own[2 * turn:2 * turn + 2], d_power, pair)
        results.append((sums[3:], [second_way(sums[m - 1], m) for m in (1, 2, 3)]))
    message = send(second_sum(*results[0]), lambda c: (0, 0, 2, 0))
    kept, messages = results[1]
    return last_sum(row_total, kept, [*messages, message])


def solution(mesh):
    in_specs = (
        P(("mp", "patch", "latent"), None, None),
        P(("mp", "patch", "latent"), None, None),
        P(None, "latent"),
        P(None, "latent"),
        P("latent"),
        P("latent"),
    )
    out_specs = P(("mp", "patch"), "latent")
    return jax.shard_map(shards, mesh=mesh, in_specs=in_specs, out_specs=out_specs, check_vma=False)
```

```python
import functools

import jax
import jax.numpy as jnp
import numpy as np
from jax import lax
from jax.experimental import pallas as pl
from jax.experimental.pallas import tpu as pltpu
from jax.sharding import PartitionSpec as P

GRID = 16
SIG_SIDE = 27
EPS = 1e-06
AXES = ("mp", "patch", "latent")
VMEM = 16 * 1024 * 1024
TOP = np.float32(np.sqrt(2.0**15))
ANY = pl.BlockSpec(memory_space=pl.ANY)
HBM = pl.BlockSpec(memory_space=pltpu.HBM)
SMEM = pl.BlockSpec(memory_space=pltpu.SMEM)
FULL = pl.BlockSpec(memory_space=pltpu.VMEM)
PIECE = 256


def resample_table(side_cells, grid_cells):
    weights_table = np.zeros((grid_cells, side_cells), np.float32)
    for target in range(grid_cells):
        source = (target + 0.5) * side_cells / grid_cells - 0.5
        low_index = int(np.floor(source))
        upper_part = source - low_index
        weights_table[target, low_index] += 1.0 - upper_part
        weights_table[target, min(low_index + 1, side_cells - 1)] += upper_part
    return weights_table


def resample_local(raw_block):
    table = resample_table(SIG_SIDE, GRID)
    table = np.kron(table, table).astype(np.float32)
    high = table.astype(jnp.bfloat16)
    low = (table - high.astype(np.float32)).astype(jnp.bfloat16)
    images = raw_block.shape[0]

    def part(matrix):
        return lax.dot_general(
            jnp.broadcast_to(jnp.asarray(matrix), (images,) + matrix.shape), raw_block,
            (((2,), (1,)), ((0,), (0,))), preferred_element_type=jnp.float32)

    return (part(high) + part(low)).astype(jnp.bfloat16)


def place(x, y, z, core):
    return (z // 2) * 64 + (x * 4 + y) * 4 + (z % 2) * 2 + core


def moves(step):
    out = []
    for x in range(4):
        for y in range(4):
            for z in range(4):
                for c in range(2):
                    dx, dy, dz, swap = step(c)
                    target = place((x + dx) % 4, (y + dy) % 4, (z + dz) % 4, c ^ swap)
                    out.append((place(x, y, z, c), target))
    return out


def send(value, step):
    return lax.ppermute(value, AXES, moves(step))


def to_sibling(value):
    return send(value, lambda c: (0, 0, 0, 1))


def along_z(value):
    return send(value, lambda c: (0, 0, -1 if c else 1, 0))


def first_way(value, m):
    return send(value, lambda c: (0, m, 0, 0) if c else (m, 0, 0, 0))


def second_way(value, m):
    return send(value, lambda c: (m, 0, 0, 0) if c else (0, m, 0, 0))


def params():
    return pltpu.CompilerParams(vmem_limit_bytes=VMEM)


def cost(flops, size):
    return pl.CostEstimate(flops=flops, bytes_accessed=size, transcendentals=0)


def encode_kernel(chunks, theta_row, *refs):
    xs, (w_ref, t_ref, out, o_buf, o_sem) = refs[:chunks], refs[chunks:]
    depth = xs[0].shape[1]
    theta = t_ref[theta_row:theta_row + 16, :].astype(jnp.float32)[:1, :]
    copies = []
    row = 0
    for k in range(chunks):
        rows = xs[k].shape[0]
        here = pl.ds(row, rows)
        pre = jnp.dot(xs[k][...], w_ref[0:depth, :], preferred_element_type=jnp.float32)
        o_buf[here, :] = jnp.maximum(pre - theta, 0.0).astype(jnp.bfloat16)
        copies.append(pltpu.make_async_copy(o_buf.at[here, :], out.at[here, :], o_sem.at[k]))
        copies[k].start()
        row += rows
    for copy in copies:
        copy.wait()


def encode(xs, weights, thresholds, theta_row, name):
    rows = sum(x.shape[0] for x in xs)
    depth = xs[0].shape[1]
    width = weights.shape[1]
    return pl.pallas_call(
        functools.partial(encode_kernel, len(xs), theta_row),
        in_specs=[FULL] * (len(xs) + 2),
        out_specs=HBM,
        out_shape=jax.ShapeDtypeStruct((rows, width), jnp.bfloat16),
        scratch_shapes=[
            pltpu.VMEM((rows, width), jnp.bfloat16),
            pltpu.SemaphoreType.DMA((len(xs),)),
        ],
        compiler_params=params(),
        cost_estimate=cost(2 * rows * depth * width // 32, 0),
        name=name,
    )(*xs, weights, thresholds)


def encode_both_kernel(chunks, theta_row, *refs):
    xs, refs = refs[:chunks], refs[chunks:]
    w_ref, v_ref, t_ref, u_ref, out_a, out_b, v_buf, o_buf, v_sem, o_sem = refs
    v_copy = pltpu.make_async_copy(v_ref, v_buf, v_sem)
    v_copy.start()
    copies = []
    for j, (weights, thresholds, out) in enumerate(((w_ref, t_ref, out_a), (v_buf, u_ref, out_b))):
        if j:
            v_copy.wait()
        theta = thresholds[theta_row:theta_row + 16, :].astype(jnp.float32)[:1, :]
        row = 0
        for k in range(chunks):
            rows = xs[k].shape[0]
            here = pl.ds(row, rows)
            pre = jnp.dot(xs[k][...], weights[...], preferred_element_type=jnp.float32)
            o_buf[j, here, :] = jnp.maximum(pre - theta, 0.0).astype(jnp.bfloat16)
            copy = pltpu.make_async_copy(o_buf.at[j, here, :], out.at[here, :], o_sem.at[j, k])
            copy.start()
            copies.append(copy)
            row += rows
    for copy in copies:
        copy.wait()


def encode_both(xs, weights, thresholds, theta_row, name):
    rows = sum(x.shape[0] for x in xs)
    depth, width = weights[0].shape
    return pl.pallas_call(
        functools.partial(encode_both_kernel, len(xs), theta_row),
        in_specs=[FULL] * (len(xs) + 1) + [HBM] + [FULL] * 2,
        out_specs=[HBM] * 2,
        out_shape=[jax.ShapeDtypeStruct((rows, width), jnp.bfloat16)] * 2,
        scratch_shapes=[
            pltpu.VMEM((depth, width), jnp.bfloat16),
            pltpu.VMEM((2, rows, width), jnp.bfloat16),
            pltpu.SemaphoreType.DMA,
            pltpu.SemaphoreType.DMA((2, len(xs))),
        ],
        compiler_params=params(),
        cost_estimate=cost(4 * rows * depth * width // 32, 0),
        name=name,
    )(*xs, *weights, *thresholds)


def encode_pieces_kernel(chunks, at_ref, *refs):
    xs, ws, (out, w_buf, o_buf, w_sem, o_sem) = refs[:chunks], refs[chunks:chunks + 4], refs[chunks + 4:]
    depth = xs[0].shape[1]
    w_copies = [pltpu.make_async_copy(ws[k], w_buf.at[:, pl.ds(k * PIECE, PIECE)], w_sem.at[k]) for k in range(4)]
    for copy in w_copies:
        copy.start()
    copies = []
    for pair in range(2):
        for copy in w_copies[2 * pair:2 * pair + 2]:
            copy.wait()
        here = slice(2 * pair * PIECE, 2 * (pair + 1) * PIECE)
        theta = w_buf[depth:depth + 16, here].astype(jnp.float32)[:1, :]
        row = 0
        for k in range(chunks):
            rows = xs[k].shape[0]
            pre = jnp.dot(xs[k][...], w_buf[0:depth, here], preferred_element_type=jnp.float32)
            o_buf[row:row + rows, here] = jnp.maximum(pre - theta, 0.0).astype(jnp.bfloat16)
            row += rows
        for step in (2 * pair, 2 * pair + 1):
            col = pl.multiple_of(lax.rem(at_ref[0] + step, 4) * PIECE, PIECE)
            copies.append(pltpu.make_async_copy(
                o_buf.at[:, pl.ds(step * PIECE, PIECE)], out.at[:, pl.ds(col, PIECE)], o_sem.at[step]))
            copies[step].start()
    for copy in copies:
        copy.wait()


def encode_pieces(at, xs, pieces, name):
    rows = sum(x.shape[0] for x in xs)
    depth = xs[0].shape[1]
    return pl.pallas_call(
        functools.partial(encode_pieces_kernel, len(xs)),
        in_specs=[SMEM] + [FULL] * len(xs) + [ANY] * 4,
        out_specs=HBM,
        out_shape=jax.ShapeDtypeStruct((rows, 4 * PIECE), jnp.bfloat16),
        scratch_shapes=[
            pltpu.VMEM((pieces[0].shape[0], 4 * PIECE), jnp.bfloat16),
            pltpu.VMEM((rows, 4 * PIECE), jnp.bfloat16),
            pltpu.SemaphoreType.DMA((4,)),
            pltpu.SemaphoreType.DMA((4,)),
        ],
        compiler_params=params(),
        cost_estimate=cost(8 * rows * depth * PIECE // 32, 0),
        name=name,
    )(at, *xs, *pieces)


def squeeze(value):
    value = value * value
    value = value * value
    return (value * value).astype(jnp.bfloat16)


def widen(value):
    return jnp.exp2(jnp.log2(value.astype(jnp.float32)) * 0.125)


def gain(power):
    return jnp.where(power > 0, lax.rsqrt(jnp.maximum(power, 1e-37)) * TOP, 0.0)


def root(power):
    return jnp.sqrt(power) * np.float32(1 / TOP)


def column(row):
    return jnp.broadcast_to(row, (128, row.shape[1])).T


def pack(row_power, column_power):
    width = column_power.shape[1]
    if row_power.shape[1] < width:
        row_power = jnp.concatenate(
            [row_power, jnp.zeros((1, width - row_power.shape[1]), jnp.float32)], axis=1)
    at = lax.broadcasted_iota(jnp.int32, (16, width), 0)
    out = jnp.zeros((16, width), jnp.float32)
    for base, power in ((0, column_power), (3, row_power)):
        rest = power
        for part in range(3):
            piece = rest.astype(jnp.bfloat16).astype(jnp.float32)
            out = jnp.where(at == base + part, piece, out)
            rest = rest - piece
    return out.astype(jnp.bfloat16)


def unpack(tail, rows):
    tail = tail.astype(jnp.float32)
    column_power = tail[0:1, :] + tail[1:2, :] + tail[2:3, :]
    row_power = tail[3:4, :rows] + tail[4:5, :rows] + tail[5:6, :rows]
    return row_power, column_power


def square_sum(ref, cols):
    total = None
    for at in range(0, ref.shape[0], 256):
        wide = ref[at:at + 256, cols].astype(jnp.float32)
        part = jnp.sum((wide * wide).reshape(32, 8, -1), axis=0)
        total = part if total is None else total + part
    return jnp.sum(total, axis=0, keepdims=True)


def products_kernel(jobs, leads, at_ref, *refs):
    ss, ds, refs = refs[:8], refs[8:12], list(refs[12:])
    dp_ref = None if leads else refs.pop(0)
    relays = [refs.pop(0) if m in (1, 3) else None for m, _ in jobs]
    if jobs[0][0] == 0:
        refs.pop(0)
    outs = [[refs.pop(0) for _ in range(1 if m in (1, 3) else 2)] for m, _ in jobs]
    if leads:
        dp_ref = refs.pop(0)
    s_bufs, r_bufs, o_bufs, s_sem, r_sem, o_sem = refs
    rows, width = ds[0].shape
    tile = width // 2
    core = at_ref[1]
    s_copies, r_copies, copies = [], [], []
    for j, (m, turn) in enumerate(jobs):
        target = lax.rem(at_ref[2] + m, 4)
        s_copies.append([])
        for k in range(2):
            here = pl.ds(k * 2 * rows, 2 * rows)
            for which in range(2):
                chosen = at_ref[4] == (which if turn == 0 else 1 - which)
                blocks = [ss[which * 4 + k * 2 + choice] for choice in (k, 1 - k)]
                for quarter in range(2):
                    col = pl.ds(pl.multiple_of(lax.rem(target, 2) * 512, 512), 512)
                    copy = pltpu.make_async_copy(blocks[quarter].at[:, col], s_bufs.at[j, here, :], s_sem.at[j, k])
                    pl.when((core == 0) & chosen & (target // 2 == quarter))(copy.start)
                for b in range(4):
                    col = pl.ds(pl.multiple_of((b % 2 * 4 + target) * 128, 128), 128)
                    part = pltpu.make_async_copy(
                        blocks[1 - b // 2].at[:, col], s_bufs.at[j, here, pl.ds(b * 128, 128)], s_sem.at[j, k])
                    pl.when((core == 1) & chosen)(part.start)
            s_copies[j].append(copy)
        r_copies.append(None)
        if m in (1, 3):
            r_copies[j] = pltpu.make_async_copy(relays[j], r_bufs.at[j], r_sem.at[j])
            r_copies[j].start()
    if leads:
        for t in range(2):
            cols = slice(t * tile, t * tile + tile)
            dp_ref[:, cols] = jnp.broadcast_to(sum(square_sum(d, cols) for d in ds), (8, tile))

    def job(j, m):
        s_buf, r_buf, o_buf, out = s_bufs.at[j], r_bufs.at[j], o_bufs.at[j], outs[j]
        relayed = {1: 0, 3: 1}.get(m)
        column_powers = [dp_ref[0:1, 0:tile], dp_ref[0:1, tile:width]]

        def dots(t, ks):
            return sum(
                lax.dot_general(s_buf[k * rows:k * rows + rows, :], ds[k][:, t * tile:t * tile + tile],
                                (((0,), (0,)), ((), ())), preferred_element_type=jnp.float32) for k in ks)

        s_copies[j][0].wait()
        near = dots(0, (0, 1))
        s_copies[j][1].wait()
        s_power = square_sum(s_buf, slice(None))
        row_powers = [s_power, s_power]
        if relayed is not None:
            r_copies[j].wait()
            r_rows, r_columns = unpack(r_buf[512:528, :], 512)
            row_powers[relayed] = s_power + r_rows
            column_powers[relayed] = column_powers[relayed] + r_columns
            r_scale = jnp.concatenate([column(root(r_rows))] * (tile // 128), axis=1) * root(r_columns)
        for t in range(2):
            cols = slice(t * tile, t * tile + tile)
            total = near + dots(0, (2, 3)) if t == 0 else dots(1, (0, 1, 2, 3))
            if t == relayed:
                total = total + widen(r_buf[0:512, :]) * r_scale
            if not m:
                out[0][:, cols] = total
                continue
            if t == 0 or relayed is not None:
                row_gain = jnp.concatenate([column(gain(row_powers[t]))] * (tile // 128), axis=1)
            o_buf[0:512, cols] = squeeze(total * row_gain * gain(column_powers[t]))
            o_buf[512:528, cols] = pack(row_powers[t], column_powers[t])
            target_ref = out[t] if m == 2 else out[0].at[:, pl.ds(t * tile, tile)]
            copy = pltpu.make_async_copy(o_buf.at[:, pl.ds(t * tile, tile)], target_ref, o_sem.at[j, t])
            copy.start()
            copies.append(copy)
        if not m:
            out[1][...] = jnp.broadcast_to(s_power, out[1].shape)

    for j, (m, _) in enumerate(jobs):
        job(j, m)
    for copy in copies:
        copy.wait()


def products(jobs, at, ss, ds, d_power=None, relays=(), after=None):
    rows, width = ds[0].shape
    f32 = jnp.float32
    leads = d_power is None
    count = len(jobs)
    shapes, specs = [], []
    for m, _ in jobs:
        if m == 2:
            shapes += [jax.ShapeDtypeStruct((528, width // 2), jnp.bfloat16)] * 2
            specs += [HBM] * 2
        elif m:
            shapes += [jax.ShapeDtypeStruct((528, width), jnp.bfloat16)]
            specs += [HBM]
        else:
            shapes += [jax.ShapeDtypeStruct(s, f32) for s in ((512, width), (8, 512))]
            specs += [FULL] * 2
    operands = [at, *ss, *ds]
    if leads:
        shapes, specs = shapes + [jax.ShapeDtypeStruct((8, width), f32)], specs + [FULL]
    else:
        operands.append(d_power)
    in_specs = [SMEM] + [HBM] * 8 + [FULL] * (len(operands) - 9)
    extra = [*relays] if after is None else [after]
    return pl.pallas_call(
        functools.partial(products_kernel, jobs, leads),
        in_specs=in_specs + [HBM] * len(extra),
        out_specs=specs,
        out_shape=shapes,
        scratch_shapes=[
            pltpu.VMEM((count, 4 * rows, 512), jnp.bfloat16),
            pltpu.VMEM((count, 528, width // 2), jnp.bfloat16),
            pltpu.VMEM((count, 528, width), jnp.bfloat16),
            pltpu.SemaphoreType.DMA((count, 2)),
            pltpu.SemaphoreType.DMA((count,)),
            pltpu.SemaphoreType.DMA((count, 2)),
        ],
        compiler_params=params(),
        cost_estimate=cost(2 * 512 * 4 * rows * width * count, 5 << 20),
        name="products",
    )(*operands, *extra)


ORDER = (2, 1, 3, 0)


def first_sum_kernel(at_ref, own_ref, sp_ref, dp_ref, *refs):
    messages, (o1, o2, o3, keep_ref, keep_rp_ref, keep_cp_ref), scratch = refs[:2], refs[2:8], refs[8:]
    m_buf, o_buf, scale_ref, power_ref, m_sem, o_sem = scratch
    width = own_ref.shape[1]
    tails, blocks = [], []
    for k, message in enumerate(messages):
        rows = pl.ds(512, 16)
        tails.append(pltpu.make_async_copy(message.at[rows, :], m_buf.at[k, rows, :], m_sem.at[4, k]))
    for i, m in enumerate(ORDER):
        rows = pl.ds(pl.multiple_of(lax.rem(at_ref[3] + m, 4) * 128, 128), 128)
        blocks.append((rows, [
            pltpu.make_async_copy(message.at[rows, :], m_buf.at[k, rows, :], m_sem.at[i, k])
            for k, message in enumerate(messages)]))
    for copies in [tails] + [copies for _, copies in blocks]:
        for copy in copies:
            copy.start()
    for copy in tails:
        copy.wait()

    row_total, column_total = sp_ref[0:1, :], dp_ref[0:1, :]
    column_roots = []
    half = width // 2
    for k in range(2):
        parts = [unpack(m_buf[k, 512:528, h * half:h * half + half], 512) for h in range(2)]
        for h in range(2):
            scale_ref[2 * k + h] = column(root(parts[h][0]))
        column_power = jnp.concatenate([part[1] for part in parts], axis=1)
        column_roots.append(root(column_power))
        row_total = row_total + parts[0][0]
        column_total = column_total + column_power
    scale_ref[4] = column(gain(row_total))
    column_gain = gain(column_total)
    power_ref[...] = jnp.broadcast_to(row_total, power_ref.shape)
    keep_cp_ref[...] = jnp.broadcast_to(column_total, keep_cp_ref.shape)

    out_copies = []
    for i, m in enumerate(ORDER):
        here, copies = blocks[i]
        for copy in copies:
            copy.wait()
        scales = [scale_ref[k, here, :] for k in range(5)]
        for at in range(0, width, 128):
            cols = slice(at, at + 128)
            total = own_ref[here, cols]
            for k in range(2):
                total = total + widen(m_buf[k, here, cols]) * (
                    scales[2 * k + at // half] * column_roots[k][:, cols])
            if m:
                o_buf[i, 0:128, cols] = squeeze(total * (scales[4] * column_gain[:, cols]))
            else:
                keep_ref[:, cols] = total
        powers = power_ref[:, here]
        if m:
            o_buf[i, 128:144, :] = pack(powers[0:1, :], column_total)
            out_copies.append(pltpu.make_async_copy(o_buf.at[i], (o1, o2, o3)[m - 1], o_sem.at[i]))
            out_copies[i].start()
        else:
            keep_rp_ref[...] = powers
    for copy in out_copies:
        copy.wait()


def first_sum(at, own, row_power, column_power, messages):
    width = own.shape[1]
    shapes = [jax.ShapeDtypeStruct((144, width), jnp.bfloat16)] * 3 + [
        jax.ShapeDtypeStruct(s, jnp.float32) for s in ((128, width), (8, 128), (8, width))]
    return pl.pallas_call(
        first_sum_kernel,
        in_specs=[SMEM] + [FULL] * 3 + [HBM] * 2,
        out_specs=[HBM] * 3 + [FULL] * 3,
        out_shape=shapes,
        scratch_shapes=[
            pltpu.VMEM((2, 528, width), jnp.bfloat16),
            pltpu.VMEM((3, 144, width), jnp.bfloat16),
            pltpu.VMEM((5, 512, 128), jnp.float32),
            pltpu.VMEM((8, 512), jnp.float32),
            pltpu.SemaphoreType.DMA((5, 2)),
            pltpu.SemaphoreType.DMA((3,)),
        ],
        compiler_params=params(),
        cost_estimate=cost(10 << 20, 3 << 20),
        name="first_sum",
    )(at, own, row_power, column_power, *messages)


def add_messages(own_ref, rp_ref, cp_ref, messages):
    rows, width = own_ref.shape
    row_total, column_total = rp_ref[0:1, :], cp_ref[0:1, :]
    scales = []
    for message in messages:
        row_power, column_power = unpack(message[rows:rows + 16, :], rows)
        scales.append((column(root(row_power)), root(column_power)))
        row_total = row_total + row_power
        column_total = column_total + column_power
    tiles = []
    for at in range(0, width, 128):
        cols = slice(at, at + 128)
        total = own_ref[:, cols]
        for message, (row_scale, column_scale) in zip(messages, scales):
            total = total + widen(message[0:rows, cols]) * (row_scale * column_scale[:, cols])
        tiles.append(total)
    return tiles, row_total, column_total


def second_sum_kernel(own_ref, rp_ref, cp_ref, m1, m2, m3, z_ref):
    tiles, rows, columns = add_messages(own_ref, rp_ref, cp_ref, (m1, m2, m3))
    row_gain, column_gain = column(gain(rows)), gain(columns)
    for t, tile in enumerate(tiles):
        cols = slice(t * 128, t * 128 + 128)
        z_ref[0:128, cols] = squeeze(tile * (row_gain * column_gain[:, cols]))
    z_ref[128:144, :] = pack(rows, columns)


def second_sum(kept, messages):
    return pl.pallas_call(
        second_sum_kernel,
        in_specs=[FULL] * 6,
        out_specs=FULL,
        out_shape=jax.ShapeDtypeStruct((144, kept[0].shape[1]), jnp.bfloat16),
        compiler_params=params(),
        cost_estimate=cost(5 << 20, 2 << 20),
        name="second_sum",
    )(*kept, *messages)


def last_sum_kernel(row_total, own_ref, rp_ref, cp_ref, m1, m2, m3, z, out_ref):
    tiles, rows, columns = add_messages(own_ref, rp_ref, cp_ref, (m1, m2, m3, z))

    def back(power):
        return jnp.where(power > 0, lax.rsqrt(power + np.float32(EPS * row_total)), 0.0)

    row_back, column_back = column(back(rows)), back(columns)
    for t, tile in enumerate(tiles):
        cols = slice(t * 128, t * 128 + 128)
        out_ref[:, cols] = tile * (row_back * column_back[:, cols])


def last_sum(row_total, kept, messages):
    return pl.pallas_call(
        functools.partial(last_sum_kernel, row_total),
        in_specs=[FULL] * 7,
        out_specs=FULL,
        out_shape=jax.ShapeDtypeStruct(kept[0].shape, jnp.float32),
        compiler_params=params(),
        cost_estimate=cost(5 << 20, 2 << 20),
        name="last_sum",
    )(*kept, *messages)


def shards(dino_acts, siglip_acts, dino_encoder, siglip_encoder, dino_threshold, siglip_threshold):
    z_hi = lax.axis_index("mp")
    patch = lax.axis_index("patch")
    latent = lax.axis_index("latent")
    x, y = patch // 4, patch % 4
    z_lo, core = latent // 2, latent % 2
    first = (x + 2 * y) % 4
    at = jnp.stack([
        first, core, jnp.where(core == 0, x, y), jnp.where(core == 0, y, x),
        (z_hi == z_lo).astype(jnp.int32)]).astype(jnp.int32)
    row_total = dino_acts.shape[0] * dino_acts.shape[1] * lax.axis_size(AXES)
    latents = dino_encoder.shape[1]

    thresholds = jnp.concatenate([
        jnp.broadcast_to(dino_threshold[None, :], (16, latents)),
        jnp.broadcast_to(siglip_threshold[None, :], (16, latents))])

    theta = (thresholds, to_sibling(thresholds))
    d_own = dino_acts.reshape(-1, dino_acts.shape[-1])
    dino_sibling = to_sibling(dino_encoder)
    siglip_sibling = to_sibling(siglip_encoder)

    piece = along_z(jnp.concatenate([
        lax.dynamic_slice_in_dim(siglip_encoder, first * PIECE, PIECE, 1),
        lax.dynamic_slice_in_dim(thresholds[16:], first * PIECE, PIECE, 1)]))
    s_own = resample_local(siglip_acts).reshape(-1, siglip_acts.shape[-1])
    s_ext = along_z(s_own)

    def dino_codes(xs):
        away = encode(xs, dino_sibling, theta[1], 0, "dino_codes")
        return encode(xs, dino_encoder, theta[0], 0, "dino_codes"), away

    piece, s_own, d_own, siglip_sibling, dino_sibling, theta_sibling = lax.optimization_barrier(
        (piece, s_own, d_own, siglip_sibling, dino_sibling, theta[1]))
    theta = (thresholds, theta_sibling)
    d_ext = along_z(d_own)
    pieces = [
        piece,
        send(piece, lambda c: (-1, 0, 0, 0)),
        send(piece, lambda c: (0, 1, 0, 0)),
        send(piece, lambda c: (1, 0, 0, 0)),
    ]

    d_near, d_near_away = encode_both([d_own], (dino_encoder, dino_sibling), theta, 0, "dino_codes")
    s_own, s_ext, d_near, d_near_away = lax.optimization_barrier((s_own, s_ext, d_near, d_near_away))
    xs = [s_own, s_ext]
    one = encode_both(xs, (siglip_encoder, siglip_sibling), theta, 16, "siglip_codes")
    *one, p0, p1, p2, p3 = lax.optimization_barrier((*one, *pieces))
    pieces = [p0, p1, p2, p3]
    pieces_sibling = [to_sibling(p) for p in pieces]
    two = [encode_pieces(at, xs, pieces, "siglip_codes")]
    d_ext, two[0] = lax.optimization_barrier((d_ext, two[0]))
    two.append(encode_pieces(at, xs, pieces_sibling, "siglip_codes"))
    d_far, d_far_away = dino_codes([d_ext])

    sets = [[*pair, to_sibling(pair[0]), to_sibling(pair[1])] for pair in (one, two)]
    ds = (d_near, d_far, to_sibling(d_near_away), to_sibling(d_far_away))

    ss = sets[0] + sets[1]
    d_power = None
    relays, arrived = [], []
    for turn in range(2):
        low, high, *powers = products([(2, turn)], at, ss, ds, d_power)
        d_power = powers[0] if powers else d_power
        relays.append((first_way(low, 1), first_way(high, 3)))
    for turn, pair in enumerate(relays):
        part_one, = products([(1, turn)], at, ss, ds, d_power, relays=pair[:1])
        part_three, = products([(3, turn)], at, ss, ds, d_power, relays=pair[1:])
        arrived.append((first_way(part_one, 1), first_way(part_three, 3)))
    own = products([(0, 0), (0, 1)], at, ss, ds, d_power, after=part_three)

    results = []
    for turn, pair in enumerate(arrived):
        sums = first_sum(at, *own[2 * turn:2 * turn + 2], d_power, pair)
        results.append((sums[3:], [second_way(sums[m - 1], m) for m in (1, 2, 3)]))
    message = send(second_sum(*results[0]), lambda c: (0, 0, 2, 0))
    kept, messages = results[1]
    return last_sum(row_total, kept, [*messages, message])


def solution(mesh):
    in_specs = (
        P(("mp", "patch", "latent"), None, None),
        P(("mp", "patch", "latent"), None, None),
        P(None, "latent"),
        P(None, "latent"),
        P("latent"),
        P("latent"),
    )
    out_specs = P(("mp", "patch"), "latent")
    return jax.shard_map(shards, mesh=mesh, in_specs=in_specs, out_specs=out_specs, check_vma=False)
```
